32 devices in a mesh: seq: 2 (over x), blk: 4 (over z), head: 4 (over y, core).
Axes of the slice: x: 2, y: 2, z: 4, core: 2. Of those that a mesh axis runs over, the one named last changes fastest.
Arguments:
- layer_input: bfloat16 [2, 8192, 1024], P('seq', ('blk', 'head')), may hold values from -6 to 6
- weight_query: bfloat16 [1024, 1024], P(('seq', 'blk', 'head')), may hold values from -0.1875 to 0.1875
- weight_key: bfloat16 [1024, 1024], P(('seq', 'blk', 'head')), may hold values from -0.1875 to 0.1875
- weight_value: bfloat16 [1024, 1024], P(('seq', 'blk', 'head')), may hold values from -0.1875 to 0.1875
- weight_output: bfloat16 [1024, 1024], P(('seq', 'blk', 'head')), may hold values from -1.5 to 1.5
- weight_expand: bfloat16 [1024, 4096], P(('seq', 'blk', 'head')), may hold values from -0.1875 to 0.1875
- weight_reduce: bfloat16 [4096, 1024], P(('seq', 'blk', 'head')), may hold values from -0.09375 to 0.09375
- bias_query: bfloat16 [1024], P(('seq', 'blk', 'head')), may hold values from -3 to 3
- bias_value: bfloat16 [1024], P(('seq', 'blk', 'head')), may hold values from -3 to 3
- bias_output: bfloat16 [1024], P(('seq', 'blk', 'head')), may hold values from -3 to 3
- bias_expand: bfloat16 [4096], P(('seq', 'blk', 'head')), may hold values from -3 to 3
- bias_reduce: bfloat16 [1024], P(('seq', 'blk', 'head')), may hold values from -3 to 3
- first_gain: bfloat16 [1024], P(('seq', 'blk', 'head')), may hold values from 0.5 to 1.5
- first_shift: bfloat16 [1024], P(('seq', 'blk', 'head')), may hold values from -3 to 3
- second_gain: bfloat16 [1024], P(('seq', 'blk', 'head')), may hold values from 0.5 to 1.5
- second_shift: bfloat16 [1024], P(('seq', 'blk', 'head')), may hold values from -3 to 3
- cotangent: bfloat16 [2, 8192, 1024], P('seq', ('blk', 'head')), may hold values from -6 to 6
- doc_lengths: int32 [2, 32], P('seq'), may hold values from 0 to 7168, as said below
Outputs:
- layer_output: bfloat16 [2, 8192, 1024], P('seq', ('blk', 'head'))
- grad_input: float32 [2, 8192, 1024], P('seq', ('blk', 'head'))
- grad_weight_query: float32 [1024, 1024], P(('seq', 'blk', 'head'))
- grad_weight_key: float32 [1024, 1024], P(('seq', 'blk', 'head'))
- grad_weight_value: float32 [1024, 1024], P(('seq', 'blk', 'head'))
- grad_weight_output: float32 [1024, 1024], P(('seq', 'blk', 'head'))
- grad_weight_expand: float32 [1024, 4096], P(('seq', 'blk', 'head'))
- grad_weight_reduce: float32 [4096, 1024], P(('seq', 'blk', 'head'))
- grad_bias_query: float32 [1024], P(('seq', 'blk', 'head'))
- grad_bias_value: float32 [1024], P(('seq', 'blk', 'head'))
- grad_bias_output: float32 [1024], P(('seq', 'blk', 'head'))
- grad_bias_expand: float32 [4096], P(('seq', 'blk', 'head'))
- grad_bias_reduce: float32 [1024], P(('seq', 'blk', 'head'))
- grad_first_gain: float32 [1024], P(('seq', 'blk', 'head'))
- grad_first_shift: float32 [1024], P(('seq', 'blk', 'head'))
- grad_second_gain: float32 [1024], P(('seq', 'blk', 'head'))
- grad_second_shift: float32 [1024], P(('seq', 'blk', 'head'))
The draws below stay inside these ranges and needn't reach their ends.
Inputs may be any that keep to these rules, and one draw needn't show every extreme that they name: `doc_lengths`: row s lists the lengths of the documents packed in order at the head of sequence s (zero for an unused slot); the tokens after them are padding. In each group of 1 sequence on one index of seq, one sequence, drawn from the seed, starts with a document of exactly 7168 tokens, leaves its last slot unused and ends with 1 to 512 tokens of padding; every other document is shorter, and every other sequence ends with more than 1024 tokens of padding.
All inputs are finite; a program needn't handle non-finite values.
Results may differ from the reference program's by a relative error of at most 0.022.
Values may be sent and summed in bfloat16 or wider, within the bound.
A program may use at most 256 MiB of HBM per device.

```python
import jax
import jax.numpy as jnp
from jax import lax

D = 1024
HEADS = 16
HEAD_DIM = 64
FF = 4096
SEQ_LEN = 8192
DOCS = 32
SEQ_DEV = 1
SEQS = 2
BLOCK_LEN = 2048


def draw_doc_lengths(key, part):
    key = jax.random.fold_in(key, 7)
    keys_all = jax.random.split(key, 5)
    exponent = jax.random.randint(keys_all[0], (SEQS, DOCS), 0, 9)
    factor = jax.random.randint(keys_all[1], (SEQS, DOCS), 1, 4)
    raw_weights = factor * jnp.power(2, exponent)
    half_block = max(BLOCK_LEN // 2, 1)
    quarter_block = max(half_block // 2, 1)
    padding = jax.random.randint(keys_all[2], (SEQS,), half_block + DOCS, BLOCK_LEN)
    groups = SEQS // SEQ_DEV
    chosen = jax.random.randint(keys_all[3], (groups,), 0, SEQ_DEV)
    member = jnp.arange(SEQS) % SEQ_DEV
    is_long = member == jnp.repeat(chosen, SEQ_DEV)
    long_padding = jax.random.randint(keys_all[4], (SEQS,), 1, quarter_block + 1)
    padding = jnp.where(is_long, long_padding, padding)
    available = SEQ_LEN - padding
    budget = jnp.where(is_long, half_block - long_padding, available)
    column = jnp.arange(DOCS)
    emptied = is_long[:, None] & ((column[None, :] == 0) | (column[None, :] == DOCS - 1))
    raw_weights = jnp.where(emptied, 0, raw_weights)
    shares = raw_weights * budget[:, None] // jnp.sum(raw_weights, axis=1, keepdims=True)
    shares = shares.at[:, 1].add(budget - jnp.sum(shares, axis=1))
    leading = jnp.where(is_long, SEQ_LEN - half_block, shares[:, 0])
    return shares.at[:, 0].set(leading).astype(jnp.int32)


def steps_of(key, shape, cuts, smallest, high):
    def one(axis_at, blocks):
        draws = jax.random.uniform(jax.random.fold_in(jax.random.fold_in(key, 6), axis_at), (blocks,), jnp.float32, smallest / len(cuts), high / len(cuts))
        return jnp.repeat(jnp.exp(draws), shape[axis_at] // blocks).reshape((-1,) + (1,) * (len(shape) - axis_at - 1))

    level = one(*cuts[0])
    for cut in cuts[1:]:
        level = level * one(*cut)
    return level


def normal_values(own_key, shape, scale, reach, pieces=(), kind=jnp.bfloat16):
    drawn = jax.random.normal(own_key, shape, jnp.float32) * scale
    if len(pieces) > 0:
        drawn = steps_of(own_key, shape, pieces, -0.22, 0.18) * drawn
    return jnp.clip(drawn, min=-reach, max=reach).astype(kind)


def setup_inputs(seed: int = 0) -> dict:
    splits = jax.random.split(jax.random.key(seed), 19)
    return {
        "layer_input": normal_values(splits[0], (SEQS, SEQ_LEN, D), 1.0, 6.0, ((0, 2), (1, 16))),
        "weight_query": normal_values(splits[1], (D, D), D ** -0.5, 0.1875, ((0, 32),)),
        "weight_key": normal_values(splits[2], (D, D), D ** -0.5, 0.1875, ((0, 32),)),
        "weight_value": normal_values(splits[3], (D, D), D ** -0.5, 0.1875, ((0, 32),)),
        "weight_output": normal_values(splits[4], (D, D), (D // 64) ** -0.5, 1.5, ((0, 32),)),
        "weight_expand": normal_values(splits[5], (D, FF), D ** -0.5, 0.1875, ((0, 32),)),
        "weight_reduce": normal_values(splits[6], (FF, D), FF ** -0.5, 0.09375, ((0, 32),)),
        "bias_query": normal_values(splits[7], (D,), 0.5, 3.0, ((0, 32),)),
        "bias_value": normal_values(splits[8], (D,), 0.3, 3.0, ((0, 32),)),
        "bias_output": normal_values(splits[9], (D,), 0.5, 3.0, ((0, 32),)),
        "bias_expand": normal_values(splits[10], (FF,), 0.5, 3.0, ((0, 32),)),
        "bias_reduce": normal_values(splits[11], (D,), 0.5, 3.0, ((0, 32),)),
        "first_gain": jnp.clip(1.0 + 0.1 * jax.random.normal(splits[12], (D,), jnp.float32), 0.5, 1.5).astype(jnp.bfloat16),
        "first_shift": normal_values(splits[13], (D,), 0.3, 3.0, ((0, 32),)),
        "second_gain": jnp.clip(1.0 + 0.1 * jax.random.normal(splits[14], (D,), jnp.float32), 0.5, 1.5).astype(jnp.bfloat16),
        "second_shift": normal_values(splits[15], (D,), 0.3, 3.0, ((0, 32),)),
        "cotangent": normal_values(splits[16], (SEQS, SEQ_LEN, D), 1.0, 6.0, ((0, 2), (1, 16))),
        "doc_lengths": draw_doc_lengths(jax.random.fold_in(splits[18], 71), 0),
    }


@jax.custom_vjp
def low(v):
    return lax.optimization_barrier(v.astype(jnp.bfloat16)).astype(jnp.float32)

@jax.custom_vjp
def low_back(v):
    return v

def low_keep(v):
    return (low(v), None)

def low_pass(kept, grad):
    return (grad,)

def back_keep(v):
    return (v, None)

def back_low(kept, grad):
    return (low(grad),)
low.defvjp(low_keep, low_pass)
low_back.defvjp(back_keep, back_low)
NORM_EPS = 1e-05
INV_ROOT2 = 0.7071067811865476

def round_both(value):
    return low(low_back(value))

def segment_ids(doc_lengths, positions):
    ends = jnp.cumsum(doc_lengths, axis=-1)
    counted = lax.optimization_barrier(jnp.sum((ends[:, None, :] <= positions[None, :, None]).astype(jnp.int32), axis=-1))
    return jnp.where(positions[None, :] < ends[:, -1:], counted + 1, 0).astype(jnp.int32)

def layer_norm(values, gain, shift):
    center = values - lax.optimization_barrier(jnp.mean(values, axis=-1, keepdims=True))
    spread = lax.optimization_barrier(jnp.mean(center * center, axis=-1, keepdims=True))
    return center * lax.rsqrt(spread + NORM_EPS) * gain + shift

def gelu_curve(values):
    return 0.5 * values * (1.0 + lax.erf(values * INV_ROOT2))

def high_dot(left, right):
    return jnp.dot(left, right, precision=lax.Precision.HIGHEST)

def attend_block(query_block, seg_query, key_seq, value_seq, seg_key):
    scores = jnp.einsum('qhd,khd->hqk', query_block, key_seq, precision=lax.Precision.HIGHEST) * HEAD_DIM ** (-0.5)
    scores = low_back(scores)
    allowed = seg_query[:, None] == seg_key[None, :]
    scores = jnp.where(allowed[None], scores, -1e+30)
    highest = lax.optimization_barrier(jnp.max(scores, axis=-1, keepdims=True))
    exponent = jnp.exp(scores - highest)
    attn_weights = exponent / lax.optimization_barrier(jnp.sum(exponent, axis=-1, keepdims=True))
    return jnp.einsum('hqk,khd->qhd', low(attn_weights), value_seq, precision=lax.Precision.HIGHEST)
block_checked = jax.checkpoint(attend_block)

def attend_sequence(inputs):
    query_seq, key_seq, value_seq, seg_seq = inputs
    block_rows = min(512, SEQ_LEN)
    query_blocks = query_seq.reshape(SEQ_LEN // block_rows, block_rows, HEADS, HEAD_DIM)
    seg_blocks = seg_seq.reshape(SEQ_LEN // block_rows, block_rows)
    result = lax.map(lambda block_pair: block_checked(block_pair[0], block_pair[1], key_seq, value_seq, seg_seq), (query_blocks, seg_blocks))
    return result.reshape(SEQ_LEN, D)

def reference(layer_input, weight_query, weight_key, weight_value, weight_output, weight_expand, weight_reduce, bias_query, bias_value, bias_output, bias_expand, bias_reduce, first_gain, first_shift, second_gain, second_shift, cotangent, doc_lengths):
    seg = segment_ids(doc_lengths, jnp.arange(SEQ_LEN, dtype=jnp.int32))
    live = (seg > 0).astype(jnp.float32)
    total_rows = SEQS * SEQ_LEN

    def forward(layer_in, w_query, w_key, w_value, w_output, w_expand, w_reduce, b_query, b_value, b_output, b_expand, b_reduce, gain_one, shift_one, gain_two, shift_two):
        rows_in = layer_in.reshape(total_rows, D)
        queries = round_both(high_dot(rows_in, w_query) + b_query)
        key_rows = round_both(high_dot(rows_in, w_key))
        value_rows = round_both(high_dot(rows_in, w_value) + b_value)
        shaped = (SEQS, SEQ_LEN, HEADS, HEAD_DIM)
        attn = lax.map(attend_sequence, (queries.reshape(shaped), key_rows.reshape(shaped), value_rows.reshape(shaped), seg))
        attn = round_both(attn.reshape(total_rows, D))
        branch = low_back(high_dot(attn, w_output) + b_output)
        normed_one = layer_norm(rows_in + branch, gain_one, shift_one)
        pre_act = low_back(high_dot(low(normed_one), w_expand) + b_expand)
        hidden = low(gelu_curve(pre_act))
        ffn_out = low_back(high_dot(hidden, w_reduce) + b_reduce)
        result = layer_norm(normed_one + ffn_out, gain_two, shift_two)
        return result.reshape(SEQS, SEQ_LEN, D)
    floats = (layer_input.astype(jnp.float32), weight_query.astype(jnp.float32), weight_key.astype(jnp.float32), weight_value.astype(jnp.float32), weight_output.astype(jnp.float32), weight_expand.astype(jnp.float32), weight_reduce.astype(jnp.float32), bias_query.astype(jnp.float32), bias_value.astype(jnp.float32), bias_output.astype(jnp.float32), bias_expand.astype(jnp.float32), bias_reduce.astype(jnp.float32), first_gain.astype(jnp.float32), first_shift.astype(jnp.float32), second_gain.astype(jnp.float32), second_shift.astype(jnp.float32))
    result, pull_back = jax.vjp(forward, *floats)
    grads = pull_back(cotangent.astype(jnp.float32) * live[..., None])
    return (result.astype(jnp.bfloat16), grads[0], grads[1], grads[2], grads[3], grads[4], grads[5], grads[6], grads[7], grads[8], grads[9], grads[10], grads[11], grads[12], grads[13], grads[14], grads[15])
```

```python
import functools
import math

import jax
import jax.numpy as jnp
from jax import lax
from jax.experimental import pallas as pl
from jax.experimental.pallas import tpu as pltpu
from jax.sharding import PartitionSpec as P

HEADS = 16
HEAD_DIM = 64


NORM_EPS = 1e-05
INV_ROOT2 = 0.7071067811865476


def segment_ids(doc_lengths, positions):
    ends = jnp.cumsum(doc_lengths, axis=-1)
    counted = jnp.sum((ends[:, None, :] <= positions[None, :, None]).astype(jnp.int32), axis=-1)
    return jnp.where(positions[None, :] < ends[:, -1:], counted + 1, 0)


def layer_norm(values, gain, shift):
    center = values - jnp.mean(values, axis=-1, keepdims=True)
    spread = jnp.mean(center * center, axis=-1, keepdims=True)
    return center * lax.rsqrt(spread + NORM_EPS) * gain + shift


def gelu_curve(values):
    return 0.5 * values * (1.0 + lax.erf(values * INV_ROOT2))


def plain_dot(left, right):
    return jnp.dot(left, right, preferred_element_type=jnp.float32)


def left_dot(left, right):
    return lax.dot_general(
        left, right, (((0,), (0,)), ((), ())), preferred_element_type=jnp.float32
    )


def right_dot(left, right):
    return lax.dot_general(
        left, right, (((1,), (1,)), ((), ())), preferred_element_type=jnp.float32
    )


def score_grads(scores, allowed, grad_part, value_part, lse_part, delta_part):
    probs = jnp.where(allowed, jnp.exp(scores - lse_part[..., None]), 0.0)
    grad_probs = jnp.einsum(
        "sqhd,skhd->shqk", grad_part, value_part, preferred_element_type=jnp.float32
    )
    grad_scores = (probs * (grad_probs - delta_part[..., None])).astype(jnp.bfloat16)
    return (probs, grad_scores)


def shards_general(
    layer_input,
    weight_query,
    weight_key,
    weight_value,
    weight_output,
    weight_expand,
    weight_reduce,
    bias_query,
    bias_value,
    bias_output,
    bias_expand,
    bias_reduce,
    first_gain,
    first_shift,
    second_gain,
    second_shift,
    cotangent,
    doc_lengths,
):
    seq_count, tok_rows, model_width = layer_input.shape
    head_count = lax.axis_size("head")
    blk_count = lax.axis_size("blk")
    heads_here = HEADS // head_count
    score_scale = HEAD_DIM ** (-0.5)
    gathered = (
        lax.all_gather(weight_query, ("seq", "blk", "head"), axis=0, tiled=True),
        lax.all_gather(weight_key, ("seq", "blk", "head"), axis=0, tiled=True),
        lax.all_gather(weight_value, ("seq", "blk", "head"), axis=0, tiled=True),
        lax.all_gather(weight_output, ("seq", "blk", "head"), axis=0, tiled=True),
        lax.all_gather(weight_expand, ("seq", "blk", "head"), axis=0, tiled=True),
        lax.all_gather(weight_reduce, ("seq", "blk", "head"), axis=0, tiled=True),
        lax.all_gather(bias_query, ("seq", "blk", "head"), axis=0, tiled=True),
        lax.all_gather(bias_value, ("seq", "blk", "head"), axis=0, tiled=True),
        lax.all_gather(bias_output, ("seq", "blk", "head"), axis=0, tiled=True),
        lax.all_gather(bias_expand, ("seq", "blk", "head"), axis=0, tiled=True),
        lax.all_gather(bias_reduce, ("seq", "blk", "head"), axis=0, tiled=True),
        lax.all_gather(first_gain, ("seq", "blk", "head"), axis=0, tiled=True),
        lax.all_gather(first_shift, ("seq", "blk", "head"), axis=0, tiled=True),
        lax.all_gather(second_gain, ("seq", "blk", "head"), axis=0, tiled=True),
        lax.all_gather(second_shift, ("seq", "blk", "head"), axis=0, tiled=True),
    )
    w_query, w_key, w_value, w_output, w_expand, w_reduce = gathered[:6]
    b_query, b_value, b_output, b_expand, b_reduce, gain_one, shift_one, gain_two, shift_two = [
        vector.astype(jnp.float32) for vector in gathered[6:]
    ]
    flat_rows = layer_input.reshape(-1, model_width)
    queries = (
        (plain_dot(flat_rows, w_query) + b_query).astype(jnp.bfloat16).reshape(layer_input.shape)
    )
    key_rows = plain_dot(flat_rows, w_key).astype(jnp.bfloat16).reshape(layer_input.shape)
    value_rows = (
        (plain_dot(flat_rows, w_value) + b_value).astype(jnp.bfloat16).reshape(layer_input.shape)
    )
    query_heads, key_heads, value_heads = (
        lax.all_to_all(queries, "head", split_axis=2, concat_axis=1, tiled=True),
        lax.all_to_all(key_rows, "head", split_axis=2, concat_axis=1, tiled=True),
        lax.all_to_all(value_rows, "head", split_axis=2, concat_axis=1, tiled=True),
    )
    block_rows = query_heads.shape[1]
    block_first = lax.axis_index("blk") * block_rows
    query_seg = segment_ids(doc_lengths, block_first + lax.iota(jnp.int32, block_rows))
    query_split = query_heads.reshape(seq_count, block_rows, heads_here, HEAD_DIM)

    def key_block(shard_piece, block_index, block_width):
        key_offset = block_index * block_width
        key_part = lax.dynamic_slice_in_dim(shard_piece[0], key_offset, block_width, 1).reshape(
            seq_count, block_width, heads_here, HEAD_DIM
        )
        value_part = lax.dynamic_slice_in_dim(shard_piece[1], key_offset, block_width, 1).reshape(
            seq_count, block_width, heads_here, HEAD_DIM
        )
        key_seg = segment_ids(doc_lengths, key_offset + lax.iota(jnp.int32, block_width))
        allowed = query_seg[:, None, :, None] == key_seg[:, None, None, :]
        scores = (
            jnp.einsum("sqhd,skhd->shqk", query_split, key_part, preferred_element_type=jnp.float32)
            * score_scale
        )
        return (key_offset, key_part, value_part, allowed, scores)

    stat_shape = (seq_count, heads_here, block_rows)
    start_state = (
        jnp.full(stat_shape, -1e30, jnp.float32),
        jnp.zeros(stat_shape, jnp.float32),
        jnp.zeros(stat_shape + (HEAD_DIM,), jnp.float32),
    )
    shard_piece = (
        lax.all_gather(key_heads, "blk", axis=1, tiled=True),
        lax.all_gather(value_heads, "blk", axis=1, tiled=True),
    )
    piece_rows = shard_piece[0].shape[1]
    block_width = math.gcd(piece_rows, 512)

    def advance(block_index, loop_state):
        running_max, row_total, accum = loop_state
        key_offset, key_part, value_part, allowed, scores = key_block(
            shard_piece, block_index, block_width
        )
        scores = jnp.where(allowed, scores, -1e30)
        new_max = jnp.maximum(running_max, jnp.max(scores, axis=-1))
        rescale = jnp.exp(running_max - new_max)
        weights = jnp.where(allowed, jnp.exp(scores - new_max[..., None]), 0.0)
        row_total = row_total * rescale + jnp.sum(weights, axis=-1)
        accum = accum * rescale[..., None] + jnp.einsum(
            "shqk,skhd->shqd",
            weights.astype(jnp.bfloat16),
            value_part,
            preferred_element_type=jnp.float32,
        )
        return (new_max, row_total, accum)

    running_max, row_total, accum = lax.fori_loop(
        0, piece_rows // block_width, advance, start_state
    )
    log_total = running_max + jnp.log(row_total)
    attn_heads = accum / row_total[..., None]
    attn_send = (
        attn_heads.transpose(0, 2, 1, 3)
        .reshape(seq_count, block_rows, heads_here * HEAD_DIM)
        .astype(jnp.bfloat16)
    )
    attn_tokens = lax.all_to_all(attn_send, "head", split_axis=1, concat_axis=2, tiled=True)
    attn_flat = attn_tokens.reshape(-1, model_width)
    resid_one = flat_rows.astype(jnp.float32) + plain_dot(attn_flat, w_output) + b_output
    normed_one, norm_one_pull = jax.vjp(layer_norm, resid_one, gain_one, shift_one)
    normed_low = normed_one.astype(jnp.bfloat16)
    pre_act = plain_dot(normed_low, w_expand) + b_expand
    hidden_f32, gelu_pull = jax.vjp(gelu_curve, pre_act)
    hidden = hidden_f32.astype(jnp.bfloat16)
    resid_two = normed_one + plain_dot(hidden, w_reduce) + b_reduce
    result, norm_two_pull = jax.vjp(layer_norm, resid_two, gain_two, shift_two)
    layer_output = result.astype(jnp.bfloat16).reshape(layer_input.shape)
    tok_first = (lax.axis_index("blk") * head_count + lax.axis_index("head")) * tok_rows
    tok_seg = segment_ids(doc_lengths, tok_first + lax.iota(jnp.int32, tok_rows))
    live = (tok_seg > 0).astype(jnp.float32)
    grad_out = (cotangent.astype(jnp.float32) * live[..., None]).reshape(-1, model_width)
    grad_resid_two, grad_gain_two, grad_shift_two = norm_two_pull(grad_out)
    grad_ffn = grad_resid_two.astype(jnp.bfloat16)
    grad_w_reduce = left_dot(hidden, grad_ffn)
    grad_b_reduce = jnp.sum(grad_ffn.astype(jnp.float32), axis=0)
    (grad_pre,) = gelu_pull(right_dot(grad_ffn, w_reduce))
    grad_pre = grad_pre.astype(jnp.bfloat16)
    grad_w_expand = left_dot(normed_low, grad_pre)
    grad_b_expand = jnp.sum(grad_pre.astype(jnp.float32), axis=0)
    grad_normed = grad_resid_two + right_dot(grad_pre, w_expand)
    grad_resid_one, grad_gain_one, grad_shift_one = norm_one_pull(grad_normed)
    grad_branch = grad_resid_one.astype(jnp.bfloat16)
    grad_w_output = left_dot(attn_flat, grad_branch)
    grad_b_output = jnp.sum(grad_branch.astype(jnp.float32), axis=0)
    grad_attn = right_dot(grad_branch, w_output).astype(jnp.bfloat16).reshape(layer_input.shape)
    grad_attn_heads = lax.all_to_all(grad_attn, "head", split_axis=2, concat_axis=1, tiled=True)
    grad_attn_split = grad_attn_heads.reshape(seq_count, block_rows, heads_here, HEAD_DIM)
    row_delta = jnp.einsum("sqhd,shqd->shq", grad_attn_split.astype(jnp.float32), attn_heads)
    full_rows = blk_count * block_rows
    query_zero = jnp.zeros((seq_count, block_rows, heads_here, HEAD_DIM), jnp.float32)
    back_state = (
        query_zero,
        jnp.zeros((seq_count, full_rows, heads_here * HEAD_DIM), jnp.float32),
        jnp.zeros((seq_count, full_rows, heads_here * HEAD_DIM), jnp.float32),
    )
    fold_shard_piece = (
        lax.all_gather(key_heads, "blk", axis=1, tiled=True),
        lax.all_gather(value_heads, "blk", axis=1, tiled=True),
    )
    piece_rows = fold_shard_piece[0].shape[1]
    fold_block_width = math.gcd(piece_rows, 512)

    def advance(block_index, loop_state):
        grad_query, grad_keys, grad_values = loop_state
        key_offset, key_part, value_part, allowed, scores = key_block(
            fold_shard_piece, block_index, fold_block_width
        )
        probs, grad_scores = score_grads(
            scores, allowed, grad_attn_split, value_part, log_total, row_delta
        )
        grad_query = (
            grad_query
            + jnp.einsum(
                "shqk,skhd->sqhd", grad_scores, key_part, preferred_element_type=jnp.float32
            )
            * score_scale
        )
        key_term = (
            jnp.einsum(
                "shqk,sqhd->skhd", grad_scores, query_split, preferred_element_type=jnp.float32
            )
            * score_scale
        )
        value_term = jnp.einsum(
            "shqk,sqhd->skhd",
            probs.astype(jnp.bfloat16),
            grad_attn_split,
            preferred_element_type=jnp.float32,
        )
        grad_keys = lax.dynamic_update_slice_in_dim(
            grad_keys,
            key_term.reshape(seq_count, fold_block_width, heads_here * HEAD_DIM),
            key_offset,
            1,
        )
        grad_values = lax.dynamic_update_slice_in_dim(
            grad_values,
            value_term.reshape(seq_count, fold_block_width, heads_here * HEAD_DIM),
            key_offset,
            1,
        )
        return (grad_query, grad_keys, grad_values)

    back_out = lax.fori_loop(0, piece_rows // fold_block_width, advance, back_state)
    grad_query = back_out[0]
    key_share, value_share = (
        lax.psum_scatter(
            back_out[1].astype(jnp.bfloat16), "blk", scatter_dimension=1, tiled=True
        ).astype(jnp.float32),
        lax.psum_scatter(
            back_out[2].astype(jnp.bfloat16), "blk", scatter_dimension=1, tiled=True
        ).astype(jnp.float32),
    )
    query_send = grad_query.reshape(seq_count, block_rows, heads_here * HEAD_DIM).astype(
        jnp.bfloat16
    )
    query_back, key_back, value_back = (
        lax.all_to_all(query_send, "head", split_axis=1, concat_axis=2, tiled=True),
        lax.all_to_all(
            key_share.astype(jnp.bfloat16), "head", split_axis=1, concat_axis=2, tiled=True
        ),
        lax.all_to_all(
            value_share.astype(jnp.bfloat16), "head", split_axis=1, concat_axis=2, tiled=True
        ),
    )
    query_back = query_back.reshape(-1, model_width)
    key_back = key_back.reshape(-1, model_width)
    value_back = value_back.reshape(-1, model_width)
    grad_w_query = left_dot(flat_rows, query_back)
    grad_w_key = left_dot(flat_rows, key_back)
    grad_w_value = left_dot(flat_rows, value_back)
    grad_b_query = jnp.sum(query_back.astype(jnp.float32), axis=0)
    grad_b_value = jnp.sum(value_back.astype(jnp.float32), axis=0)
    grad_input = (
        grad_resid_one
        + right_dot(query_back, w_query)
        + right_dot(key_back, w_key)
        + right_dot(value_back, w_value)
    )
    grad_input = grad_input.reshape(layer_input.shape)
    shares_all = (
        lax.psum_scatter(grad_w_query, ("seq", "blk", "head"), scatter_dimension=0, tiled=True),
        lax.psum_scatter(grad_w_key, ("seq", "blk", "head"), scatter_dimension=0, tiled=True),
        lax.psum_scatter(grad_w_value, ("seq", "blk", "head"), scatter_dimension=0, tiled=True),
        lax.psum_scatter(grad_w_output, ("seq", "blk", "head"), scatter_dimension=0, tiled=True),
        lax.psum_scatter(grad_w_expand, ("seq", "blk", "head"), scatter_dimension=0, tiled=True),
        lax.psum_scatter(grad_w_reduce, ("seq", "blk", "head"), scatter_dimension=0, tiled=True),
        lax.psum_scatter(grad_b_query, ("seq", "blk", "head"), scatter_dimension=0, tiled=True),
        lax.psum_scatter(grad_b_value, ("seq", "blk", "head"), scatter_dimension=0, tiled=True),
        lax.psum_scatter(grad_b_output, ("seq", "blk", "head"), scatter_dimension=0, tiled=True),
        lax.psum_scatter(grad_b_expand, ("seq", "blk", "head"), scatter_dimension=0, tiled=True),
        lax.psum_scatter(grad_b_reduce, ("seq", "blk", "head"), scatter_dimension=0, tiled=True),
        lax.psum_scatter(grad_gain_one, ("seq", "blk", "head"), scatter_dimension=0, tiled=True),
        lax.psum_scatter(grad_shift_one, ("seq", "blk", "head"), scatter_dimension=0, tiled=True),
        lax.psum_scatter(grad_gain_two, ("seq", "blk", "head"), scatter_dimension=0, tiled=True),
        lax.psum_scatter(grad_shift_two, ("seq", "blk", "head"), scatter_dimension=0, tiled=True),
    )
    return (
        layer_output,
        grad_input,
        shares_all[0],
        shares_all[1],
        shares_all[2],
        shares_all[3],
        shares_all[4],
        shares_all[5],
        shares_all[6],
        shares_all[7],
        shares_all[8],
        shares_all[9],
        shares_all[10],
        shares_all[11],
        shares_all[12],
        shares_all[13],
        shares_all[14],
    )


LOG2E = 1.4426950408889634
RR=(((1,),(1,)),((),()))
def fwd_kernel(bq,ck,q_ref,k_ref,v_ref,sc_ref,sr_ref,p_ref,pt_ref,o_ref,l_ref,kk,vv,s0,s1,m0,m1):
    g=pl.program_id(0); ng=pl.num_programs(0)
    L=q_ref.shape[1]; Lm=p_ref.shape[1]; T=L-Lm; nc=Lm//ck
    nb=Lm//bq
    c=LOG2E*HEAD_DIM**-0.5
    def qblk(start):
        q=q_ref[:,pl.ds(pl.multiple_of(start,bq),bq)].astype(jnp.float32)*c
        hi=q.astype(jnp.bfloat16).astype(jnp.float32)
        return jnp.concatenate([hi,q-hi],0).T.astype(jnp.bfloat16)
    def phase1(qb,s,j,mx):
        r=jnp.dot(qb,kk[:,j*ck:(j+1)*ck],preferred_element_type=jnp.float32)
        s[:,j*ck:(j+1)*ck]=r
        for t in range(ck//128):
            x=r[:,t*128:(t+1)*128]
            mx=x if mx is None else jnp.maximum(mx,x)
        return mx
    def setm(m,mx):
        m[...]=jnp.broadcast_to(jnp.max(mx,axis=1,keepdims=True),m.shape)
    def phase2(s,m,j,row,acc):
        p=jnp.exp2(s[:,j*ck:(j+1)*ck]-m[:,:1]).astype(jnp.bfloat16)
        p_ref[row:row+bq,j*ck:(j+1)*ck]=p
        r=lax.dot_general(vv[:,j*ck:(j+1)*ck],p,RR,preferred_element_type=jnp.float32)
        return r if acc is None else acc+r
    def finish(acc,start):
        il=1.0/acc[HEAD_DIM:HEAD_DIM+1]
        o_ref[:,pl.ds(pl.multiple_of(start,bq),bq)]=(acc[:HEAD_DIM]*il).astype(jnp.bfloat16)
        l_ref[:,pl.ds(pl.multiple_of(start,bq),bq)]=jnp.broadcast_to(il,(8,bq))
    @pl.when(g==0)
    def _():
        kk[0:HEAD_DIM,:]=k_ref[...]; kk[HEAD_DIM:,:]=k_ref[...]
        vv[0:HEAD_DIM,:]=v_ref[...]
        vv[HEAD_DIM:,:]=(lax.broadcasted_iota(jnp.int32,(16,L),0)==0).astype(jnp.float32).astype(jnp.bfloat16)
        qb=qblk(0); mx=None
        for j in range(nc): mx=phase1(qb,s0,j,mx)
        setm(m0,mx)
    for h,(sa,ma,sb,mb) in enumerate(((s0,m0,s1,m1),(s1,m1,s0,m0))):
        nxt=jnp.minimum(2*g+h+1,nb-1)*bq
        qb=qblk(nxt); acc=None; mx=None
        for j in range(nc):
            acc=phase2(sa,ma,j,h*bq,acc)
            mx=phase1(qb,sb,j,mx)
        setm(mb,mx)
        finish(acc,(2*g+h)*bq)
    @pl.when(g==ng-1)
    def _():
        for i in range(T//bq):
            qb=qblk(Lm+i*bq)
            s=jnp.dot(qb,kk[:,Lm:],preferred_element_type=jnp.float32)
            s=jnp.where(sc_ref[i*bq:(i+1)*bq,:1]==sr_ref[:1,:],s,-1e30)
            m=jnp.max(s,axis=1,keepdims=True)
            p=jnp.exp2(s-m).astype(jnp.bfloat16)
            pt_ref[i*bq:(i+1)*bq,:]=p
            finish(lax.dot_general(vv[:,Lm:],p,RR,preferred_element_type=jnp.float32),Lm+i*bq)

def attn_fwd(qT,kT,vT,seg,Lm,bq=256,ck=1024):
    L=qT.shape[1]; T=L-Lm
    sc=jnp.broadcast_to(seg[:,None],(T,128)); sr=jnp.broadcast_to(seg[None,:],(8,T))
    full=lambda s: pl.BlockSpec(s,lambda g:(0,)*len(s))
    ng=Lm//bq//2
    return pl.pallas_call(functools.partial(fwd_kernel,bq,ck),
        grid=(ng,),
        in_specs=[full((HEAD_DIM,L))]*3+[full((T,128)),full((8,T))],
        out_specs=[pl.BlockSpec((2*bq,Lm),lambda g:(g,0)),full((T,T)),full((HEAD_DIM,L)),full((8,L))],
        out_shape=[jax.ShapeDtypeStruct((Lm,Lm),jnp.bfloat16),jax.ShapeDtypeStruct((T,T),jnp.bfloat16),jax.ShapeDtypeStruct((HEAD_DIM,L),jnp.bfloat16),jax.ShapeDtypeStruct((8,L),jnp.float32)],
        scratch_shapes=[pltpu.VMEM((2*HEAD_DIM,L),jnp.bfloat16),pltpu.VMEM((HEAD_DIM+16,L),jnp.bfloat16),pltpu.VMEM((bq,Lm),jnp.float32),pltpu.VMEM((bq,Lm),jnp.float32),pltpu.VMEM((bq,128),jnp.float32),pltpu.VMEM((bq,128),jnp.float32)],
        compiler_params=pltpu.CompilerParams(vmem_limit_bytes=60*2**20),
        cost_estimate=pl.CostEstimate(flops=4*Lm*Lm*256,bytes_accessed=2*Lm*Lm,transcendentals=Lm*Lm),
        name="attn_fwd")(qT,kT,vT,sc,sr)

def bwd_kernel(bq,ck,p_ref,pt_ref,q_ref,k_ref,v_ref,o_ref,do_ref,l_ref,dq_ref,dk_ref,dv_ref,vv,dka,dva):
    g=pl.program_id(0); ng=pl.num_programs(0)
    L=q_ref.shape[1]; Lm=p_ref.shape[1]; T=L-Lm; nc=Lm//ck
    @pl.when(g==0)
    def _():
        vv[0:HEAD_DIM,:]=v_ref[...]
        vv[HEAD_DIM:,:]=(lax.broadcasted_iota(jnp.int32,(16,L),0)<2).astype(jnp.float32).astype(jnp.bfloat16)
        dka[...]=jnp.zeros_like(dka); dva[...]=jnp.zeros_like(dva)
    def prep(start,n):
        sl=pl.ds(pl.multiple_of(start,n),n)
        do=do_ref[:,sl].astype(jnp.float32); il=l_ref[:1,sl]
        dl=-jnp.sum(do*o_ref[:,sl].astype(jnp.float32),axis=0,keepdims=True)*il
        dh=dl.astype(jnp.bfloat16).astype(jnp.float32)
        row=lax.broadcasted_iota(jnp.int32,(16,n),0)
        extra=jnp.where(row==0,dh,jnp.where(row==1,dl-dh,0.0))
        d=do*il
        A=jnp.concatenate([d,extra],0).T.astype(jnp.bfloat16)
        return A,d.astype(jnp.bfloat16),q_ref[:,sl]
    def chunk(A,d,q,p,kc,vc,dq):
        dp=jnp.dot(A,vc,preferred_element_type=jnp.float32)
        ds=(p.astype(jnp.float32)*dp).astype(jnp.bfloat16)
        dv=jnp.dot(d,p,preferred_element_type=jnp.float32)
        dk=jnp.dot(q,ds,preferred_element_type=jnp.float32)
        r=lax.dot_general(kc,ds,RR,preferred_element_type=jnp.float32)
        return (r if dq is None else dq+r),dk,dv
    A,d,q=prep(g*bq,bq); dq=None
    for j in range(nc):
        sl=slice(j*ck,(j+1)*ck)
        dq,dk,dv=chunk(A,d,q,p_ref[:,sl],k_ref[:,sl],vv[:,sl],dq)
        dka[:,sl]+=dk; dva[:,sl]+=dv
    dq_ref[:,pl.ds(pl.multiple_of(g*bq,bq),bq)]=(dq*HEAD_DIM**-0.5).astype(jnp.bfloat16)
    @pl.when(g==ng-1)
    def _():
        for i in range(T//bq):
            A,d,q=prep(Lm+i*bq,bq)
            dq,dk,dv=chunk(A,d,q,pt_ref[i*bq:(i+1)*bq,:],k_ref[:,Lm:],vv[:,Lm:],None)
            dka[:,Lm:]+=dk; dva[:,Lm:]+=dv
            dq_ref[:,Lm+i*bq:Lm+(i+1)*bq]=(dq*HEAD_DIM**-0.5).astype(jnp.bfloat16)
        dk_ref[...]=(dka[...]*HEAD_DIM**-0.5).astype(jnp.bfloat16)
        dv_ref[...]=dva[...].astype(jnp.bfloat16)

def attn_bwd(P,Pt,qT,kT,vT,oT,doT,il,Lm,bq=512,ck=1024):
    L=qT.shape[1]; T=L-Lm
    full=lambda s: pl.BlockSpec(s,lambda g:(0,)*len(s))
    f=jax.ShapeDtypeStruct((HEAD_DIM,L),jnp.bfloat16)
    return pl.pallas_call(functools.partial(bwd_kernel,bq,ck),
        grid=(Lm//bq,),
        in_specs=[pl.BlockSpec((bq,Lm),lambda g:(g,0)),full((T,T))]+[full((HEAD_DIM,L))]*5+[full((8,L))],
        out_specs=[full((HEAD_DIM,L))]*3,
        out_shape=[f]*3,
        scratch_shapes=[pltpu.VMEM((HEAD_DIM+16,L),jnp.bfloat16),pltpu.VMEM((HEAD_DIM,L),jnp.float32),pltpu.VMEM((HEAD_DIM,L),jnp.float32)],
        compiler_params=pltpu.CompilerParams(vmem_limit_bytes=60*2**20),
        cost_estimate=pl.CostEstimate(flops=8*Lm*Lm*256,bytes_accessed=2*Lm*Lm,transcendentals=0),
        name="attn_bwd")(P,Pt,qT,kT,vT,oT,doT,il)


MESH = pl.DeviceIdType.MESH
GROUP = ("blk", "head")
EVERY = ("seq", "blk", "head")


def greet_group(me, count, heads):
    barrier = pltpu.get_barrier_semaphore()
    for step in range(1, count):
        peer = lax.rem(me + step, count)
        pl.semaphore_signal(
            barrier,
            inc=1,
            device_id={"blk": peer // heads, "head": lax.rem(peer, heads)},
            device_id_type=MESH,
        )
    pl.semaphore_wait(barrier, count - 1)


def swap_kernel(to_heads, blks, heads, in_ref, out_ref, send_sem, recv_sem, own_sem):
    count = blks * heads
    me = lax.axis_index("blk") * heads + lax.axis_index("head")
    greet_group(me, count, heads)
    if to_heads:
        rows = in_ref.shape[2]
        width = in_ref.shape[3]
        take = lambda owner: in_ref.at[:, owner]
        place = lambda source: out_ref.at[
            :, :, pl.ds(pl.multiple_of(source * width, width), width)
        ]
    else:
        rows = in_ref.shape[1]
        width = in_ref.shape[2] // count
        take = lambda owner: in_ref.at[:, :, pl.ds(pl.multiple_of(owner * width, width), width)]
        place = lambda source: out_ref.at[:, source]
    own = pltpu.make_async_copy(take(me), place(me), own_sem)
    own.start()
    copies = []
    for step in range(1, count):
        peer = lax.rem(me + step, count)
        copy = pltpu.make_async_remote_copy(
            src_ref=take(peer),
            dst_ref=place(me),
            send_sem=send_sem.at[step],
            recv_sem=recv_sem.at[step],
            device_id={"blk": peer // heads, "head": lax.rem(peer, heads)},
            device_id_type=MESH,
        )
        copy.start()
        copies.append(copy)
    own.wait()
    for copy in copies:
        copy.wait_send()
        copy.wait_recv()


def swap(values, to_heads, collective_id):
    blks, heads = lax.axis_size("blk"), lax.axis_size("head")
    count = blks * heads
    parts = values.shape[0]
    if to_heads:
        shape = (parts, values.shape[2], values.shape[3] * count)
    else:
        shape = (parts, count, values.shape[1], values.shape[2] // count)
    return pl.pallas_call(
        functools.partial(swap_kernel, to_heads, blks, heads),
        out_shape=jax.ShapeDtypeStruct(shape, values.dtype),
        in_specs=[pl.BlockSpec(memory_space=pl.ANY)],
        out_specs=pl.BlockSpec(memory_space=pl.ANY),
        scratch_shapes=[
            pltpu.SemaphoreType.DMA((count,)),
            pltpu.SemaphoreType.DMA((count,)),
            pltpu.SemaphoreType.DMA,
        ],
        compiler_params=pltpu.CompilerParams(collective_id=collective_id, has_side_effects=True),
        name="swap_to_heads" if to_heads else "swap_to_tokens",
    )(values)


def tail_segments(doc_lengths, first, rows):
    return segment_ids(doc_lengths, first + lax.iota(jnp.int32, rows))


def shards_heads(
    layer_input,
    weight_query,
    weight_key,
    weight_value,
    weight_output,
    weight_expand,
    weight_reduce,
    bias_query,
    bias_value,
    bias_output,
    bias_expand,
    bias_reduce,
    first_gain,
    first_shift,
    second_gain,
    second_shift,
    cotangent,
    doc_lengths,
):
    tok_rows, model_width = layer_input.shape[1:]
    head_count = lax.axis_size("head")
    blk_count = lax.axis_size("blk")
    count = head_count * blk_count
    seq_len = tok_rows * count
    long_rows = seq_len - seq_len // blk_count // 2
    flat_rows = layer_input.reshape(tok_rows, model_width)

    vectors = (
        bias_query,
        bias_value,
        bias_output,
        bias_reduce,
        first_gain,
        first_shift,
        second_gain,
        second_shift,
        bias_expand,
    )
    sizes = [vector.shape[0] for vector in vectors]
    packed = lax.all_gather(jnp.concatenate(vectors), EVERY, axis=0).astype(jnp.float32)
    whole, start = [], 0
    for size in sizes:
        whole.append(packed[:, start : start + size].reshape(-1))
        start += size
    b_query, b_value, b_output, b_reduce, gain_one, shift_one, gain_two, shift_two, b_expand = whole

    w_qkv = lax.all_gather(
        jnp.concatenate((weight_query, weight_key, weight_value), axis=1), EVERY, axis=0, tiled=True
    )
    w_output = lax.all_gather(weight_output, EVERY, axis=0, tiled=True)
    w_expand = lax.all_gather(weight_expand, EVERY, axis=0, tiled=True)
    w_reduce = lax.all_gather(weight_reduce, EVERY, axis=0, tiled=True)

    b_qkv = jnp.concatenate((b_query, jnp.zeros_like(b_query), b_value))
    qkv = lax.dot_general(
        w_qkv, flat_rows, (((0,), (1,)), ((), ())), preferred_element_type=jnp.float32
    )
    qkv = (qkv + b_qkv[:, None]).astype(jnp.bfloat16).reshape(3, HEADS, HEAD_DIM, tok_rows)
    qkv = swap(qkv, True, 0)
    query, key, value = qkv[0], qkv[1], qkv[2]
    seg = tail_segments(doc_lengths, long_rows, seq_len - long_rows)[0]
    probs, tail_probs, attn, inv_total = attn_fwd(query, key, value, seg, long_rows)
    attn_flat = swap(attn[None], False, 1).reshape(model_width, tok_rows)

    resid_one = flat_rows.astype(jnp.float32) + left_dot(attn_flat, w_output) + b_output
    normed_one, norm_one_pull = jax.vjp(layer_norm, resid_one, gain_one, shift_one)
    normed_low = normed_one.astype(jnp.bfloat16)
    pre_act = plain_dot(normed_low, w_expand) + b_expand
    hidden_f32, gelu_pull = jax.vjp(gelu_curve, pre_act)
    hidden = hidden_f32.astype(jnp.bfloat16)
    resid_two = normed_one + plain_dot(hidden, w_reduce) + b_reduce
    result, norm_two_pull = jax.vjp(layer_norm, resid_two, gain_two, shift_two)
    layer_output = result.astype(jnp.bfloat16).reshape(layer_input.shape)
    tok_first = (lax.axis_index("blk") * head_count + lax.axis_index("head")) * tok_rows
    tok_seg = segment_ids(doc_lengths, tok_first + lax.iota(jnp.int32, tok_rows))
    live = (tok_seg > 0).astype(jnp.float32)
    grad_out = (cotangent.astype(jnp.float32) * live[..., None]).reshape(-1, model_width)
    grad_resid_two, grad_gain_two, grad_shift_two = norm_two_pull(grad_out)
    grad_ffn = grad_resid_two.astype(jnp.bfloat16)
    grad_w_reduce = left_dot(hidden, grad_ffn)
    grad_b_reduce = jnp.sum(grad_ffn.astype(jnp.float32), axis=0)
    (grad_pre,) = gelu_pull(right_dot(grad_ffn, w_reduce))
    grad_pre = grad_pre.astype(jnp.bfloat16)
    grad_w_expand = left_dot(normed_low, grad_pre)
    grad_b_expand = jnp.sum(grad_pre.astype(jnp.float32), axis=0)
    grad_normed = grad_resid_two + right_dot(grad_pre, w_expand)
    grad_resid_one, grad_gain_one, grad_shift_one = norm_one_pull(grad_normed)
    grad_branch = grad_resid_one.astype(jnp.bfloat16)
    grad_w_output = plain_dot(attn_flat, grad_branch)
    grad_b_output = jnp.sum(grad_branch.astype(jnp.float32), axis=0)
    grad_attn = right_dot(w_output, grad_branch).astype(jnp.bfloat16)
    grad_attn = swap(grad_attn.reshape(1, HEADS, HEAD_DIM, tok_rows), True, 2)[0]

    def share(grad):
        return lax.psum_scatter(
            grad.astype(jnp.bfloat16), EVERY, scatter_dimension=0, tiled=True
        ).astype(jnp.float32)

    grad_w_output = share(grad_w_output)
    grad_w_expand = share(grad_w_expand)
    grad_w_reduce = share(grad_w_reduce)

    grad_qkv = attn_bwd(
        probs, tail_probs, query, key, value, attn, grad_attn, inv_total, long_rows
    )
    grad_qkv = swap(jnp.stack(grad_qkv), False, 3).reshape(3 * model_width, tok_rows)
    grad_w_qkv = lax.dot_general(
        flat_rows, grad_qkv, (((0,), (1,)), ((), ())), preferred_element_type=jnp.float32
    )
    grad_w_qkv = share(grad_w_qkv)
    grad_input = grad_resid_one + lax.dot_general(
        grad_qkv, w_qkv, (((0,), (1,)), ((), ())), preferred_element_type=jnp.float32
    )
    grad_b_qkv = jnp.sum(grad_qkv.astype(jnp.float32), axis=1)

    sums = (
        grad_b_qkv[:model_width],
        grad_b_qkv[2 * model_width :],
        grad_b_output,
        grad_b_reduce,
        grad_gain_one,
        grad_shift_one,
        grad_gain_two,
        grad_shift_two,
        grad_b_expand,
    )
    sums = jnp.concatenate([term.reshape(-1, size) for term, size in zip(sums, sizes)], axis=1)
    sums = lax.psum_scatter(sums, EVERY, scatter_dimension=0, tiled=True).reshape(-1)
    parts, start = [], 0
    for size in sizes:
        parts.append(sums[start : start + size])
        start += size
    g_query, g_value, g_output, g_reduce, g_gain_one, g_shift_one, g_gain_two, g_shift_two, g_expand = parts
    return (
        layer_output,
        grad_input.reshape(layer_input.shape),
        grad_w_qkv[:, :model_width],
        grad_w_qkv[:, model_width : 2 * model_width],
        grad_w_qkv[:, 2 * model_width :],
        grad_w_output,
        grad_w_expand,
        grad_w_reduce,
        g_query,
        g_value,
        g_output,
        g_expand,
        g_reduce,
        g_gain_one,
        g_shift_one,
        g_gain_two,
        g_shift_two,
    )


def solution(mesh):
    placed = (
        P("seq", ("blk", "head"), None),
        P(("seq", "blk", "head"), None),
        P(("seq", "blk", "head"), None),
        P(("seq", "blk", "head"), None),
        P(("seq", "blk", "head"), None),
        P(("seq", "blk", "head"), None),
        P(("seq", "blk", "head"), None),
        P(("seq", "blk", "head")),
        P(("seq", "blk", "head")),
        P(("seq", "blk", "head")),
        P(("seq", "blk", "head")),
        P(("seq", "blk", "head")),
        P(("seq", "blk", "head")),
        P(("seq", "blk", "head")),
        P(("seq", "blk", "head")),
        P(("seq", "blk", "head")),
        P("seq", ("blk", "head"), None),
        P("seq", None),
    )
    group = mesh.shape["blk"] * mesh.shape["head"]
    body = shards_heads if group == HEADS else shards_general
    return jax.shard_map(
        body,
        mesh=mesh,
        in_specs=placed,
        out_specs=(
            P("seq", ("blk", "head"), None),
            P("seq", ("blk", "head"), None),
            P(("seq", "blk", "head"), None),
            P(("seq", "blk", "head"), None),
            P(("seq", "blk", "head"), None),
            P(("seq", "blk", "head"), None),
            P(("seq", "blk", "head"), None),
            P(("seq", "blk", "head"), None),
            P(("seq", "blk", "head")),
            P(("seq", "blk", "head")),
            P(("seq", "blk", "head")),
            P(("seq", "blk", "head")),
            P(("seq", "blk", "head")),
            P(("seq", "blk", "head")),
            P(("seq", "blk", "head")),
            P(("seq", "blk", "head")),
            P(("seq", "blk", "head")),
        ),
        check_vma=False,
    )
```

```python
import functools
import math

import jax
import jax.numpy as jnp
from jax import lax
from jax.experimental import pallas as pl
from jax.experimental.pallas import tpu as pltpu
from jax.sharding import PartitionSpec as P

HEADS = 16
HEAD_DIM = 64


NORM_EPS = 1e-05
INV_ROOT2 = 0.7071067811865476


def segment_ids(doc_lengths, positions):
    ends = jnp.cumsum(doc_lengths, axis=-1)
    counted = jnp.sum((ends[:, None, :] <= positions[None, :, None]).astype(jnp.int32), axis=-1)
    return jnp.where(positions[None, :] < ends[:, -1:], counted + 1, 0)


def layer_norm(values, gain, shift):
    center = values - jnp.mean(values, axis=-1, keepdims=True)
    spread = jnp.mean(center * center, axis=-1, keepdims=True)
    return center * lax.rsqrt(spread + NORM_EPS) * gain + shift


def gelu_curve(values):
    return 0.5 * values * (1.0 + lax.erf(values * INV_ROOT2))


def plain_dot(left, right):
    return jnp.dot(left, right, preferred_element_type=jnp.float32)


def left_dot(left, right):
    return lax.dot_general(
        left, right, (((0,), (0,)), ((), ())), preferred_element_type=jnp.float32
    )


def right_dot(left, right):
    return lax.dot_general(
        left, right, (((1,), (1,)), ((), ())), preferred_element_type=jnp.float32
    )


def score_grads(scores, allowed, grad_part, value_part, lse_part, delta_part):
    probs = jnp.where(allowed, jnp.exp(scores - lse_part[..., None]), 0.0)
    grad_probs = jnp.einsum(
        "sqhd,skhd->shqk", grad_part, value_part, preferred_element_type=jnp.float32
    )
    grad_scores = (probs * (grad_probs - delta_part[..., None])).astype(jnp.bfloat16)
    return (probs, grad_scores)


def shards_general(
    layer_input,
    weight_query,
    weight_key,
    weight_value,
    weight_output,
    weight_expand,
    weight_reduce,
    bias_query,
    bias_value,
    bias_output,
    bias_expand,
    bias_reduce,
    first_gain,
    first_shift,
    second_gain,
    second_shift,
    cotangent,
    doc_lengths,
):
    seq_count, tok_rows, model_width = layer_input.shape
    head_count = lax.axis_size("head")
    blk_count = lax.axis_size("blk")
    heads_here = HEADS // head_count
    score_scale = HEAD_DIM ** (-0.5)
    gathered = (
        lax.all_gather(weight_query, ("seq", "blk", "head"), axis=0, tiled=True),
        lax.all_gather(weight_key, ("seq", "blk", "head"), axis=0, tiled=True),
        lax.all_gather(weight_value, ("seq", "blk", "head"), axis=0, tiled=True),
        lax.all_gather(weight_output, ("seq", "blk", "head"), axis=0, tiled=True),
        lax.all_gather(weight_expand, ("seq", "blk", "head"), axis=0, tiled=True),
        lax.all_gather(weight_reduce, ("seq", "blk", "head"), axis=0, tiled=True),
        lax.all_gather(bias_query, ("seq", "blk", "head"), axis=0, tiled=True),
        lax.all_gather(bias_value, ("seq", "blk", "head"), axis=0, tiled=True),
        lax.all_gather(bias_output, ("seq", "blk", "head"), axis=0, tiled=True),
        lax.all_gather(bias_expand, ("seq", "blk", "head"), axis=0, tiled=True),
        lax.all_gather(bias_reduce, ("seq", "blk", "head"), axis=0, tiled=True),
        lax.all_gather(first_gain, ("seq", "blk", "head"), axis=0, tiled=True),
        lax.all_gather(first_shift, ("seq", "blk", "head"), axis=0, tiled=True),
        lax.all_gather(second_gain, ("seq", "blk", "head"), axis=0, tiled=True),
        lax.all_gather(second_shift, ("seq", "blk", "head"), axis=0, tiled=True),
    )
    w_query, w_key, w_value, w_output, w_expand, w_reduce = gathered[:6]
    b_query, b_value, b_output, b_expand, b_reduce, gain_one, shift_one, gain_two, shift_two = [
        vector.astype(jnp.float32) for vector in gathered[6:]
    ]
    flat_rows = layer_input.reshape(-1, model_width)
    queries = (
        (plain_dot(flat_rows, w_query) + b_query).astype(jnp.bfloat16).reshape(layer_input.shape)
    )
    key_rows = plain_dot(flat_rows, w_key).astype(jnp.bfloat16).reshape(layer_input.shape)
    value_rows = (
        (plain_dot(flat_rows, w_value) + b_value).astype(jnp.bfloat16).reshape(layer_input.shape)
    )
    query_heads, key_heads, value_heads = (
        lax.all_to_all(queries, "head", split_axis=2, concat_axis=1, tiled=True),
        lax.all_to_all(key_rows, "head", split_axis=2, concat_axis=1, tiled=True),
        lax.all_to_all(value_rows, "head", split_axis=2, concat_axis=1, tiled=True),
    )
    block_rows = query_heads.shape[1]
    block_first = lax.axis_index("blk") * block_rows
    query_seg = segment_ids(doc_lengths, block_first + lax.iota(jnp.int32, block_rows))
    query_split = query_heads.reshape(seq_count, block_rows, heads_here, HEAD_DIM)

    def key_block(shard_piece, block_index, block_width):
        key_offset = block_index * block_width
        key_part = lax.dynamic_slice_in_dim(shard_piece[0], key_offset, block_width, 1).reshape(
            seq_count, block_width, heads_here, HEAD_DIM
        )
        value_part = lax.dynamic_slice_in_dim(shard_piece[1], key_offset, block_width, 1).reshape(
            seq_count, block_width, heads_here, HEAD_DIM
        )
        key_seg = segment_ids(doc_lengths, key_offset + lax.iota(jnp.int32, block_width))
        allowed = query_seg[:, None, :, None] == key_seg[:, None, None, :]
        scores = (
            jnp.einsum("sqhd,skhd->shqk", query_split, key_part, preferred_element_type=jnp.float32)
            * score_scale
        )
        return (key_offset, key_part, value_part, allowed, scores)

    stat_shape = (seq_count, heads_here, block_rows)
    start_state = (
        jnp.full(stat_shape, -1e30, jnp.float32),
        jnp.zeros(stat_shape, jnp.float32),
        jnp.zeros(stat_shape + (HEAD_DIM,), jnp.float32),
    )
    shard_piece = (
        lax.all_gather(key_heads, "blk", axis=1, tiled=True),
        lax.all_gather(value_heads, "blk", axis=1, tiled=True),
    )
    piece_rows = shard_piece[0].shape[1]
    block_width = math.gcd(piece_rows, 512)

    def advance(block_index, loop_state):
        running_max, row_total, accum = loop_state
        key_offset, key_part, value_part, allowed, scores = key_block(
            shard_piece, block_index, block_width
        )
        scores = jnp.where(allowed, scores, -1e30)
        new_max = jnp.maximum(running_max, jnp.max(scores, axis=-1))
        rescale = jnp.exp(running_max - new_max)
        weights = jnp.where(allowed, jnp.exp(scores - new_max[..., None]), 0.0)
        row_total = row_total * rescale + jnp.sum(weights, axis=-1)
        accum = accum * rescale[..., None] + jnp.einsum(
            "shqk,skhd->shqd",
            weights.astype(jnp.bfloat16),
            value_part,
            preferred_element_type=jnp.float32,
        )
        return (new_max, row_total, accum)

    running_max, row_total, accum = lax.fori_loop(
        0, piece_rows // block_width, advance, start_state
    )
    log_total = running_max + jnp.log(row_total)
    attn_heads = accum / row_total[..., None]
    attn_send = (
        attn_heads.transpose(0, 2, 1, 3)
        .reshape(seq_count, block_rows, heads_here * HEAD_DIM)
        .astype(jnp.bfloat16)
    )
    attn_tokens = lax.all_to_all(attn_send, "head", split_axis=1, concat_axis=2, tiled=True)
    attn_flat = attn_tokens.reshape(-1, model_width)
    resid_one = flat_rows.astype(jnp.float32) + plain_dot(attn_flat, w_output) + b_output
    normed_one, norm_one_pull = jax.vjp(layer_norm, resid_one, gain_one, shift_one)
    normed_low = normed_one.astype(jnp.bfloat16)
    pre_act = plain_dot(normed_low, w_expand) + b_expand
    hidden_f32, gelu_pull = jax.vjp(gelu_curve, pre_act)
    hidden = hidden_f32.astype(jnp.bfloat16)
    resid_two = normed_one + plain_dot(hidden, w_reduce) + b_reduce
    result, norm_two_pull = jax.vjp(layer_norm, resid_two, gain_two, shift_two)
    layer_output = result.astype(jnp.bfloat16).reshape(layer_input.shape)
    tok_first = (lax.axis_index("blk") * head_count + lax.axis_index("head")) * tok_rows
    tok_seg = segment_ids(doc_lengths, tok_first + lax.iota(jnp.int32, tok_rows))
    live = (tok_seg > 0).astype(jnp.float32)
    grad_out = (cotangent.astype(jnp.float32) * live[..., None]).reshape(-1, model_width)
    grad_resid_two, grad_gain_two, grad_shift_two = norm_two_pull(grad_out)
    grad_ffn = grad_resid_two.astype(jnp.bfloat16)
    grad_w_reduce = left_dot(hidden, grad_ffn)
    grad_b_reduce = jnp.sum(grad_ffn.astype(jnp.float32), axis=0)
    (grad_pre,) = gelu_pull(right_dot(grad_ffn, w_reduce))
    grad_pre = grad_pre.astype(jnp.bfloat16)
    grad_w_expand = left_dot(normed_low, grad_pre)
    grad_b_expand = jnp.sum(grad_pre.astype(jnp.float32), axis=0)
    grad_normed = grad_resid_two + right_dot(grad_pre, w_expand)
    grad_resid_one, grad_gain_one, grad_shift_one = norm_one_pull(grad_normed)
    grad_branch = grad_resid_one.astype(jnp.bfloat16)
    grad_w_output = left_dot(attn_flat, grad_branch)
    grad_b_output = jnp.sum(grad_branch.astype(jnp.float32), axis=0)
    grad_attn = right_dot(grad_branch, w_output).astype(jnp.bfloat16).reshape(layer_input.shape)
    grad_attn_heads = lax.all_to_all(grad_attn, "head", split_axis=2, concat_axis=1, tiled=True)
    grad_attn_split = grad_attn_heads.reshape(seq_count, block_rows, heads_here, HEAD_DIM)
    row_delta = jnp.einsum("sqhd,shqd->shq", grad_attn_split.astype(jnp.float32), attn_heads)
    full_rows = blk_count * block_rows
    query_zero = jnp.zeros((seq_count, block_rows, heads_here, HEAD_DIM), jnp.float32)
    back_state = (
        query_zero,
        jnp.zeros((seq_count, full_rows, heads_here * HEAD_DIM), jnp.float32),
        jnp.zeros((seq_count, full_rows, heads_here * HEAD_DIM), jnp.float32),
    )
    fold_shard_piece = (
        lax.all_gather(key_heads, "blk", axis=1, tiled=True),
        lax.all_gather(value_heads, "blk", axis=1, tiled=True),
    )
    piece_rows = fold_shard_piece[0].shape[1]
    fold_block_width = math.gcd(piece_rows, 512)

    def advance(block_index, loop_state):
        grad_query, grad_keys, grad_values = loop_state
        key_offset, key_part, value_part, allowed, scores = key_block(
            fold_shard_piece, block_index, fold_block_width
        )
        probs, grad_scores = score_grads(
            scores, allowed, grad_attn_split, value_part, log_total, row_delta
        )
        grad_query = (
            grad_query
            + jnp.einsum(
                "shqk,skhd->sqhd", grad_scores, key_part, preferred_element_type=jnp.float32
            )
            * score_scale
        )
        key_term = (
            jnp.einsum(
                "shqk,sqhd->skhd", grad_scores, query_split, preferred_element_type=jnp.float32
            )
            * score_scale
        )
        value_term = jnp.einsum(
            "shqk,sqhd->skhd",
            probs.astype(jnp.bfloat16),
            grad_attn_split,
            preferred_element_type=jnp.float32,
        )
        grad_keys = lax.dynamic_update_slice_in_dim(
            grad_keys,
            key_term.reshape(seq_count, fold_block_width, heads_here * HEAD_DIM),
            key_offset,
            1,
        )
        grad_values = lax.dynamic_update_slice_in_dim(
            grad_values,
            value_term.reshape(seq_count, fold_block_width, heads_here * HEAD_DIM),
            key_offset,
            1,
        )
        return (grad_query, grad_keys, grad_values)

    back_out = lax.fori_loop(0, piece_rows // fold_block_width, advance, back_state)
    grad_query = back_out[0]
    key_share, value_share = (
        lax.psum_scatter(
            back_out[1].astype(jnp.bfloat16), "blk", scatter_dimension=1, tiled=True
        ).astype(jnp.float32),
        lax.psum_scatter(
            back_out[2].astype(jnp.bfloat16), "blk", scatter_dimension=1, tiled=True
        ).astype(jnp.float32),
    )
    query_send = grad_query.reshape(seq_count, block_rows, heads_here * HEAD_DIM).astype(
        jnp.bfloat16
    )
    query_back, key_back, value_back = (
        lax.all_to_all(query_send, "head", split_axis=1, concat_axis=2, tiled=True),
        lax.all_to_all(
            key_share.astype(jnp.bfloat16), "head", split_axis=1, concat_axis=2, tiled=True
        ),
        lax.all_to_all(
            value_share.astype(jnp.bfloat16), "head", split_axis=1, concat_axis=2, tiled=True
        ),
    )
    query_back = query_back.reshape(-1, model_width)
    key_back = key_back.reshape(-1, model_width)
    value_back = value_back.reshape(-1, model_width)
    grad_w_query = left_dot(flat_rows, query_back)
    grad_w_key = left_dot(flat_rows, key_back)
    grad_w_value = left_dot(flat_rows, value_back)
    grad_b_query = jnp.sum(query_back.astype(jnp.float32), axis=0)
    grad_b_value = jnp.sum(value_back.astype(jnp.float32), axis=0)
    grad_input = (
        grad_resid_one
        + right_dot(query_back, w_query)
        + right_dot(key_back, w_key)
        + right_dot(value_back, w_value)
    )
    grad_input = grad_input.reshape(layer_input.shape)
    shares_all = (
        lax.psum_scatter(grad_w_query, ("seq", "blk", "head"), scatter_dimension=0, tiled=True),
        lax.psum_scatter(grad_w_key, ("seq", "blk", "head"), scatter_dimension=0, tiled=True),
        lax.psum_scatter(grad_w_value, ("seq", "blk", "head"), scatter_dimension=0, tiled=True),
        lax.psum_scatter(grad_w_output, ("seq", "blk", "head"), scatter_dimension=0, tiled=True),
        lax.psum_scatter(grad_w_expand, ("seq", "blk", "head"), scatter_dimension=0, tiled=True),
        lax.psum_scatter(grad_w_reduce, ("seq", "blk", "head"), scatter_dimension=0, tiled=True),
        lax.psum_scatter(grad_b_query, ("seq", "blk", "head"), scatter_dimension=0, tiled=True),
        lax.psum_scatter(grad_b_value, ("seq", "blk", "head"), scatter_dimension=0, tiled=True),
        lax.psum_scatter(grad_b_output, ("seq", "blk", "head"), scatter_dimension=0, tiled=True),
        lax.psum_scatter(grad_b_expand, ("seq", "blk", "head"), scatter_dimension=0, tiled=True),
        lax.psum_scatter(grad_b_reduce, ("seq", "blk", "head"), scatter_dimension=0, tiled=True),
        lax.psum_scatter(grad_gain_one, ("seq", "blk", "head"), scatter_dimension=0, tiled=True),
        lax.psum_scatter(grad_shift_one, ("seq", "blk", "head"), scatter_dimension=0, tiled=True),
        lax.psum_scatter(grad_gain_two, ("seq", "blk", "head"), scatter_dimension=0, tiled=True),
        lax.psum_scatter(grad_shift_two, ("seq", "blk", "head"), scatter_dimension=0, tiled=True),
    )
    return (
        layer_output,
        grad_input,
        shares_all[0],
        shares_all[1],
        shares_all[2],
        shares_all[3],
        shares_all[4],
        shares_all[5],
        shares_all[6],
        shares_all[7],
        shares_all[8],
        shares_all[9],
        shares_all[10],
        shares_all[11],
        shares_all[12],
        shares_all[13],
        shares_all[14],
    )


MESH = pl.DeviceIdType.MESH
EVERY = ("seq", "blk", "head")
EDGE = 32
UNIT = 1024


class Place:
    def __init__(self, blks):
        self.blks = blks
        self.x = lax.axis_index("seq")
        self.z = lax.axis_index("blk")
        lane = lax.axis_index("head")
        self.y = lane // 2
        self.c = lax.rem(lane, 2)

    def at(self, x=None, z=None, y=None, c=None):
        x = self.x if x is None else x
        z = self.z if z is None else z
        y = self.y if y is None else y
        c = self.c if c is None else c
        return {"seq": x, "blk": z, "head": y * 2 + c}

    def column(self):
        return [lax.rem(self.z + step, self.blks) for step in range(1, self.blks)]

    def near(self):
        return [self.at(z=z) for z in self.column()] + [
            self.at(x=1 - self.x),
            self.at(y=1 - self.y),
            self.at(c=1 - self.c),
        ]

    def others(self, devices):
        own = (self.x * self.blks + self.z) * 4 + self.y * 2 + self.c
        found = []
        for step in range(1, devices):
            index = lax.rem(own + step, devices)
            found.append(
                {
                    "seq": index // (self.blks * 4),
                    "blk": lax.rem(index // 4, self.blks),
                    "head": lax.rem(index, 4),
                }
            )
        return own, found


def greet(devices):
    barrier = pltpu.get_barrier_semaphore()
    for device in devices:
        pl.semaphore_signal(barrier, inc=1, device_id=device, device_id_type=MESH)
    pl.semaphore_wait(barrier, len(devices))


class Wires:
    def __init__(self, send, recv):
        self.send, self.recv, self.used = send, recv, 0

    def copy(self, source, target, device):
        slot = self.used
        self.used += 1
        return pltpu.make_async_remote_copy(
            src_ref=source,
            dst_ref=target,
            send_sem=self.send.at[slot],
            recv_sem=self.recv.at[slot],
            device_id=device,
            device_id_type=MESH,
        )


def view(ref, index, piece):
    rows, cols = piece
    return ref.at[tuple(index) + (pl.ds(*rows), pl.ds(*cols))]


ALL = slice(None)


class Gather:
    WIRES = 7

    def __init__(self, me, wires, ref, piece, turned):
        x, z, y, c = me.x, me.z, me.y, me.c
        own = view(ref, (x, z, y, c), piece)
        self.first = [wires.copy(own, own, me.at(z=peer)) for peer in me.column()]
        line = view(ref, (x, ALL, y, c), piece)
        if turned:
            half, rest = view(ref, (ALL, ALL, y, c), piece), view(ref, (ALL, ALL, 1 - y, c), piece)
            self.second = wires.copy(line, line, me.at(x=1 - x))
            self.third = wires.copy(half, half, me.at(y=1 - y))
        else:
            half, rest = view(ref, (x, ALL, ALL, c), piece), view(ref, (1 - x, ALL, ALL, c), piece)
            self.second = wires.copy(line, line, me.at(y=1 - y))
            self.third = wires.copy(half, half, me.at(x=1 - x))
        self.near = wires.copy(half, half, me.at(c=1 - c))
        self.far = wires.copy(rest, rest, me.at(c=1 - c))

    def stage(self, index):
        if index == 0:
            for copy in self.first:
                copy.start()
        elif index == 1:
            for copy in self.first:
                copy.wait_recv()
            self.second.start()
        elif index == 2:
            self.second.wait_recv()
            self.third.start()
            self.near.start()
        elif index == 3:
            self.third.wait_recv()
            self.far.start()
        else:
            self.near.wait_recv()
            self.far.wait_recv()
            for copy in (*self.first, self.second, self.third, self.near, self.far):
                copy.wait_send()


class Reduce:
    WIRES = 6

    def __init__(self, me, wires, ref, piece, turned, own, own_sem, r0, r1, r2, r3, out, out_piece):
        x, z, y, c = me.x, me.z, me.y, me.c
        self.place, self.turned, self.out, self.out_piece = me, turned, out, out_piece
        self.own, self.r0, self.r1, self.r2, self.r3 = own, r0, r1, r2, r3
        self.load = pltpu.make_async_copy(view(ref, (ALL, ALL, ALL, c), piece), own, own_sem)
        self.zero = wires.copy(view(ref, (ALL, ALL, ALL, 1 - c), piece), r0, me.at(c=1 - c))
        if turned:
            self.one = wires.copy(r0.at[:, :, 1 - y], r1, me.at(y=1 - y))
            self.two = wires.copy(r0.at[1 - x, :, y], r2, me.at(x=1 - x))
        else:
            self.one = wires.copy(r0.at[1 - x], r1, me.at(x=1 - x))
            self.two = wires.copy(r0.at[x, :, 1 - y], r2, me.at(y=1 - y))
        self.three = [
            wires.copy(r0.at[x, peer, y], r3.at[slot], me.at(z=peer))
            for slot, peer in enumerate(me.column())
        ]

    def stage(self, index):
        x, z, y = self.place.x, self.place.z, self.place.y
        blks = self.place.blks
        r0 = self.r0

        def add(target, term):
            total = r0[target].astype(jnp.float32) + term.astype(jnp.float32)
            r0[target] = total.astype(r0.dtype)

        if index == 0:
            self.zero.start()
        elif index == 1:
            self.load.start()
        elif index == 2:
            self.load.wait()
            self.zero.wait_recv()

            @pl.loop(0, 4 * blks)
            def _(i):
                at = (i // (2 * blks), lax.rem(i // 2, blks), lax.rem(i, 2))
                add(at, self.own[at])

            self.one.start()
        elif index == 3:
            self.one.wait_recv()

            @pl.loop(0, 2 * blks)
            def _(i):
                if self.turned:
                    a, b = i // blks, lax.rem(i, blks)
                    add((a, b, y), self.r1[a, b])
                else:
                    a, b = i // 2, lax.rem(i, 2)
                    add((x, a, b), self.r1[a, b])

            self.two.start()
        elif index == 4:
            self.two.wait_recv()

            @pl.loop(0, blks)
            def _(i):
                add((x, i, y), self.r2[i])

            for copy in self.three:
                copy.start()
        else:
            for copy in self.three:
                copy.wait_recv()
            total = r0[x, z, y].astype(jnp.float32)
            for slot in range(blks - 1):
                total = total + self.r3[slot].astype(jnp.float32)
            rows, cols = self.out_piece
            self.out[rows[0] : rows[0] + rows[1], cols[0] : cols[0] + cols[1]] = total
            for copy in (self.zero, self.one, self.two, *self.three):
                copy.wait_send()


def reduce_scratch(units, blks, dtype=jnp.bfloat16):
    return [
        pltpu.VMEM((2, 2, blks, 2, EDGE, UNIT), dtype),
        pltpu.VMEM((units, 2, blks, 2, EDGE, UNIT), dtype),
        pltpu.VMEM((units // 2 + units % 2, blks, 2, EDGE, UNIT), dtype),
        pltpu.VMEM((max(units // 2, 1), 2, blks, EDGE, UNIT), dtype),
        pltpu.VMEM((units, blks, EDGE, UNIT), dtype),
        pltpu.VMEM((units, blks - 1, EDGE, UNIT), dtype),
        pltpu.SemaphoreType.DMA((2,)),
        pltpu.SemaphoreType.DMA((Reduce.WIRES * units,)),
        pltpu.SemaphoreType.DMA((Reduce.WIRES * units,)),
    ]


def final_kernel(blks, devices, grad, sums, out, sums_out, own, r0, r1a, r1b, r2, r3, own_sem, send, recv, landed, sums_send, sums_recv, sums_sem):
    me = Place(blks)
    index, others = me.others(devices)
    greet(others)
    wires = Wires(send, recv)
    units = r0.shape[0]
    plan = [
        Reduce(
            me,
            wires,
            grad,
            ((0, EDGE), (unit * UNIT, UNIT)),
            unit % 2 == 1,
            own.at[unit % 2],
            own_sem.at[unit % 2],
            r0.at[unit],
            (r1b if unit % 2 else r1a).at[unit // 2],
            r2.at[unit],
            r3.at[unit],
            out,
            ((0, EDGE), (unit * UNIT, UNIT)),
        )
        for unit in range(units)
    ]
    small = []
    for slot, device in enumerate(others):
        peer = (device["seq"] * blks + device["blk"]) * 4 + device["head"]
        small.append(
            pltpu.make_async_remote_copy(
                src_ref=sums.at[peer],
                dst_ref=landed.at[slot],
                send_sem=sums_send.at[slot],
                recv_sem=sums_recv.at[slot],
                device_id=device,
                device_id_type=MESH,
            )
        )
    for unit in plan:
        unit.stage(0)
    plan[0].stage(1)
    plan[1].stage(1)
    for copy in small:
        copy.start()
    mine = pltpu.make_async_copy(sums.at[index], landed.at[devices - 1], sums_sem)
    mine.start()
    for number, unit in enumerate(plan):
        unit.stage(2)
        if number + 2 < units:
            plan[number + 2].stage(1)
    for index in (3, 4):
        for unit in plan:
            unit.stage(index)
    mine.wait()
    for copy in small:
        copy.wait()
    sums_out[...] = jnp.sum(landed[...], axis=0)
    for unit in plan:
        unit.stage(5)


def final_reduce(grad, sums, collective_id):
    seqs, blks, heads = (lax.axis_size(name) for name in EVERY)
    devices = seqs * blks * heads
    units = grad.shape[1] // UNIT
    shares = grad.reshape(seqs, blks, heads // 2, 2, EDGE, grad.shape[1])
    return pl.pallas_call(
        functools.partial(final_kernel, blks, devices),
        out_shape=[
            jax.ShapeDtypeStruct((EDGE, grad.shape[1]), jnp.float32),
            jax.ShapeDtypeStruct(sums.shape[1:], jnp.float32),
        ],
        in_specs=[pl.BlockSpec(memory_space=pl.ANY)] * 2,
        out_specs=[pl.BlockSpec(memory_space=pltpu.VMEM)] * 2,
        scratch_shapes=[
            *reduce_scratch(units, blks),
            pltpu.VMEM((devices,) + sums.shape[1:], jnp.float32),
            pltpu.SemaphoreType.DMA((devices,)),
            pltpu.SemaphoreType.DMA((devices,)),
            pltpu.SemaphoreType.DMA,
        ],
        compiler_params=pltpu.CompilerParams(
            collective_id=collective_id, has_side_effects=True, vmem_limit_bytes=40 * 2**20
        ),
        name="final_reduce",
    )(shares, sums)


def first_kernel(blks, devices, wq, wk, wv, vec, out, vec_out, own_sem, send, recv, vec_send, vec_recv):
    me = Place(blks)
    index, others = me.others(devices)
    local = [
        pltpu.make_async_copy(
            ref, out.at[me.x, me.z, me.y, me.c, :, pl.ds(unit * UNIT, UNIT)], own_sem.at[unit]
        )
        for unit, ref in enumerate((wq, wk, wv))
    ]
    local.append(pltpu.make_async_copy(vec, vec_out.at[index], own_sem.at[3]))
    for copy in local:
        copy.start()
    greet(others)
    for copy in local:
        copy.wait()
    wires = Wires(send, recv)
    plan = [
        Gather(me, wires, out, ((0, EDGE), (half * UNIT // 2, UNIT // 2)), half % 2 == 1)
        for half in range(6)
    ]
    small = []
    for slot, device in enumerate(others):
        small.append(
            pltpu.make_async_remote_copy(
                src_ref=vec,
                dst_ref=vec_out.at[index],
                send_sem=vec_send.at[slot],
                recv_sem=vec_recv.at[slot],
                device_id=device,
                device_id_type=MESH,
            )
        )
    for unit in plan:
        unit.stage(0)
    for copy in small:
        copy.start()
    for wave in range(3 + 4):
        for pair in range(3):
            index = wave - pair + 1
            if 1 <= index <= 4:
                for unit in plan[2 * pair : 2 * pair + 2]:
                    unit.stage(index)
    for copy in small:
        copy.wait()


def first_gather(wq, wk, wv, vec, collective_id):
    seqs, blks, heads = (lax.axis_size(name) for name in EVERY)
    devices = seqs * blks * heads
    return pl.pallas_call(
        functools.partial(first_kernel, blks, devices),
        out_shape=[
            jax.ShapeDtypeStruct((seqs, blks, heads // 2, 2, EDGE, 3 * UNIT), wq.dtype),
            jax.ShapeDtypeStruct((devices,) + vec.shape, vec.dtype),
        ],
        in_specs=[pl.BlockSpec(memory_space=pl.ANY)] * 4,
        out_specs=[pl.BlockSpec(memory_space=pl.ANY)] * 2,
        scratch_shapes=[
            pltpu.SemaphoreType.DMA((4,)),
            pltpu.SemaphoreType.DMA((6 * Gather.WIRES,)),
            pltpu.SemaphoreType.DMA((6 * Gather.WIRES,)),
            pltpu.SemaphoreType.DMA((devices,)),
            pltpu.SemaphoreType.DMA((devices,)),
        ],
        compiler_params=pltpu.CompilerParams(collective_id=collective_id, has_side_effects=True),
        name="first_gather",
    )(wq, wk, wv, vec)


LOG2E = 1.4426950408889634
BY_LAST = (((1,), (1,)), ((), ()))


def weight_units(edges):
    out_rows, expand_cols, reduce_rows = edges
    units = [(0, ((0, out_rows), (0, UNIT)))]
    expand = [(1, ((0, EDGE), (first, UNIT))) for first in range(0, expand_cols, UNIT)]
    reduce = [(2, ((first, EDGE), (0, UNIT))) for first in range(0, reduce_rows, EDGE)]
    for pair in zip(expand, reduce):
        units.extend(pair)
    return units


def attn_fwd_kernel(
    blks, rows, cols, q_ref, k_ref, v_ref, down_ref, across_ref, wo, we, wr,
    p_ref, tail_ref, o_ref, inv_ref, go, ge, gr,
    keys, values, s0, s1, m0, m1, own_sem, send, recv,
):
    step, steps = pl.program_id(0), pl.num_programs(0)
    length, long = q_ref.shape[1], p_ref.shape[1]
    tail, chunks, blocks = length - long, long // cols, long // rows
    scale = LOG2E * HEAD_DIM**-0.5

    me = Place(blks)
    wires = Wires(send, recv)
    shares, wholes = (wo, we, wr), (go, ge, gr)
    units = weight_units((wo.shape[0], we.shape[1], wr.shape[0]))
    plan = [
        Gather(me, wires, wholes[which], piece, number % 2 == 1)
        for number, (which, piece) in enumerate(units)
    ]
    moves = {0: []}
    for number, unit in enumerate(plan):
        begin = number if number < 2 else number - 1
        for stage, at in enumerate((begin, begin + 1, begin + 2, begin + 4, blocks)):
            moves.setdefault(min(at, blocks // 2 - 1), []).append((stage, number, unit))

    def take_queries(start):
        part = q_ref[:, pl.ds(pl.multiple_of(start, rows), rows)].astype(jnp.float32) * scale
        high = part.astype(jnp.bfloat16).astype(jnp.float32)
        return jnp.concatenate([high, part - high], 0).T.astype(jnp.bfloat16)

    def score(queries, store, j, peak):
        found = jnp.dot(
            queries, keys[:, j * cols : (j + 1) * cols], preferred_element_type=jnp.float32
        )
        store[:, j * cols : (j + 1) * cols] = found
        for first in range(0, cols, 128):
            piece = found[:, first : first + 128]
            peak = piece if peak is None else jnp.maximum(peak, piece)
        return peak

    def keep_peak(store, peak):
        store[...] = jnp.broadcast_to(jnp.max(peak, axis=1, keepdims=True), store.shape)

    def weigh(store, peak, j, row, total):
        weights = jnp.exp2(store[:, j * cols : (j + 1) * cols] - peak[:, :1]).astype(jnp.bfloat16)
        p_ref[row : row + rows, j * cols : (j + 1) * cols] = weights
        term = lax.dot_general(
            values[:, j * cols : (j + 1) * cols],
            weights,
            BY_LAST,
            preferred_element_type=jnp.float32,
        )
        return term if total is None else total + term

    def finish(total, start):
        place = pl.ds(pl.multiple_of(start, rows), rows)
        inverse = 1.0 / total[HEAD_DIM : HEAD_DIM + 1]
        o_ref[:, place] = (total[:HEAD_DIM] * inverse).astype(jnp.bfloat16)
        inv_ref[:, place] = jnp.broadcast_to(inverse, (8, rows))

    @pl.when(step == 0)
    def _():
        local = [
            pltpu.make_async_copy(share, whole.at[me.x, me.z, me.y, me.c], own_sem.at[number])
            for number, (share, whole) in enumerate(zip(shares, wholes))
        ]
        for copy in local:
            copy.start()
        keys[0:HEAD_DIM, :] = k_ref[...]
        keys[HEAD_DIM:, :] = k_ref[...]
        values[0:HEAD_DIM, :] = v_ref[...]
        values[HEAD_DIM:, :] = (
            (lax.broadcasted_iota(jnp.int32, (16, length), 0) == 0)
            .astype(jnp.float32)
            .astype(jnp.bfloat16)
        )
        greet(me.near())
        for copy in local:
            copy.wait()

    for at, todo in sorted(moves.items()):

        @pl.when(step == at)
        def _():
            for stage, number, unit in sorted(todo, key=lambda entry: (-entry[0], entry[1])):
                if stage < 4:
                    unit.stage(stage)

    @pl.when(step == 0)
    def _():
        queries, peak = take_queries(0), None
        for j in range(chunks):
            peak = score(queries, s0, j, peak)
        keep_peak(m0, peak)

    for half, (old, old_peak, new, new_peak) in enumerate(((s0, m0, s1, m1), (s1, m1, s0, m0))):
        queries = take_queries(jnp.minimum(2 * step + half + 1, blocks - 1) * rows)
        total, peak = None, None
        for j in range(chunks):
            total = weigh(old, old_peak, j, half * rows, total)
            peak = score(queries, new, j, peak)
        keep_peak(new_peak, peak)
        finish(total, (2 * step + half) * rows)

    @pl.when(step == steps - 1)
    def _():
        for first in range(0, tail, rows):
            queries = take_queries(long + first)
            found = jnp.dot(queries, keys[:, long:], preferred_element_type=jnp.float32)
            allowed = down_ref[first : first + rows, :1] == across_ref[:1, :]
            found = jnp.where(allowed, found, -1e30)
            peak = jnp.max(found, axis=1, keepdims=True)
            weights = jnp.exp2(found - peak).astype(jnp.bfloat16)
            tail_ref[first : first + rows, :] = weights
            total = lax.dot_general(
                values[:, long:], weights, BY_LAST, preferred_element_type=jnp.float32
            )
            finish(total, long + first)
        for unit in plan:
            unit.stage(4)


def once(shape):
    return pl.BlockSpec(shape, lambda step: (0,) * len(shape), pipeline_mode=pl.Buffered(1))


def attn_fwd(query, key, value, seg, long, shares, collective_id, rows=256, cols=1024):
    blks = lax.axis_size("blk")
    lead = (lax.axis_size("seq"), blks, lax.axis_size("head") // 2, 2)
    length = query.shape[1]
    tail = length - long
    down = jnp.broadcast_to(seg[:, None], (tail, 128))
    across = jnp.broadcast_to(seg[None, :], (8, tail))
    anywhere = pl.BlockSpec(memory_space=pl.ANY)
    wires = Gather.WIRES * len(
        weight_units((shares[0].shape[0], shares[1].shape[1], shares[2].shape[0]))
    )
    return pl.pallas_call(
        functools.partial(attn_fwd_kernel, blks, rows, cols),
        grid=(long // rows // 2,),
        in_specs=[once((HEAD_DIM, length))] * 3
        + [once((tail, 128)), once((8, tail))]
        + [anywhere] * 3,
        out_specs=[
            pl.BlockSpec((2 * rows, long), lambda step: (step, 0)),
            once((tail, tail)),
            once((HEAD_DIM, length)),
            once((8, length)),
        ]
        + [anywhere] * 3,
        out_shape=[
            jax.ShapeDtypeStruct((long, long), jnp.bfloat16),
            jax.ShapeDtypeStruct((tail, tail), jnp.bfloat16),
            jax.ShapeDtypeStruct((HEAD_DIM, length), jnp.bfloat16),
            jax.ShapeDtypeStruct((8, length), jnp.float32),
        ]
        + [jax.ShapeDtypeStruct(lead + share.shape, share.dtype) for share in shares],
        scratch_shapes=[
            pltpu.VMEM((2 * HEAD_DIM, length), jnp.bfloat16),
            pltpu.VMEM((HEAD_DIM + 16, length), jnp.bfloat16),
            pltpu.VMEM((rows, long), jnp.float32),
            pltpu.VMEM((rows, long), jnp.float32),
            pltpu.VMEM((rows, 128), jnp.float32),
            pltpu.VMEM((rows, 128), jnp.float32),
            pltpu.SemaphoreType.DMA((3,)),
            pltpu.SemaphoreType.DMA((wires,)),
            pltpu.SemaphoreType.DMA((wires,)),
        ],
        compiler_params=pltpu.CompilerParams(
            collective_id=collective_id, has_side_effects=True, vmem_limit_bytes=56 * 2**20
        ),
        cost_estimate=pl.CostEstimate(
            flops=4 * long * long * HEAD_DIM,
            bytes_accessed=2 * long * long,
            transcendentals=long * long,
        ),
        name="attn_fwd",
    )(query, key, value, down, across, *shares)


def attn_bwd_kernel(
    blks, rows, cols, p_ref, tail_ref, q_ref, k_ref, v_ref, o_ref, do_ref, inv_ref, wo, we, wr,
    dq_ref, dk_ref, dv_ref, go, ge, gr,
    values, dk_sum, dv_sum, own, r0, r1a, r1b, r2, r3, own_sem, send, recv,
):
    step, steps = pl.program_id(0), pl.num_programs(0)
    length, long = q_ref.shape[1], p_ref.shape[1]
    tail, chunks = length - long, long // cols
    scale = HEAD_DIM**-0.5

    me = Place(blks)
    wires = Wires(send, recv)
    partials, totals = (wo, we, wr), (go, ge, gr)
    units = weight_units((wo.shape[4], we.shape[5], wr.shape[4]))
    last = long // rows - 1
    plan, moves = [], {}
    for number, (which, piece) in enumerate(units):
        turned = number % 2 == 1
        unit = Reduce(
            me,
            wires,
            partials[which],
            piece,
            turned,
            own.at[number % 2],
            own_sem.at[number % 2],
            r0.at[number],
            (r1b if turned else r1a).at[number // 2],
            r2.at[number],
            r3.at[number],
            totals[which],
            piece,
        )
        plan.append(unit)
        for stage, at in enumerate((0, number, number + 1, number + 3, number + 4)):
            moves.setdefault(min(at, last), []).append((stage, number, unit))

    def prepare(start, width):
        place = pl.ds(pl.multiple_of(start, width), width)
        grads, inverse = do_ref[:, place].astype(jnp.float32), inv_ref[:1, place]
        delta = -jnp.sum(grads * o_ref[:, place].astype(jnp.float32), axis=0, keepdims=True)
        delta = delta * inverse
        high = delta.astype(jnp.bfloat16).astype(jnp.float32)
        row = lax.broadcasted_iota(jnp.int32, (16, width), 0)
        extra = jnp.where(row == 0, high, jnp.where(row == 1, delta - high, 0.0))
        grads = grads * inverse
        wide = jnp.concatenate([grads, extra], 0).T.astype(jnp.bfloat16)
        return wide, grads.astype(jnp.bfloat16), q_ref[:, place]

    def part(wide, grads, queries, weights, keys_here, values_here, dq):
        dp = jnp.dot(wide, values_here, preferred_element_type=jnp.float32)
        ds = (weights.astype(jnp.float32) * dp).astype(jnp.bfloat16)
        dv = jnp.dot(grads, weights, preferred_element_type=jnp.float32)
        dk = jnp.dot(queries, ds, preferred_element_type=jnp.float32)
        term = lax.dot_general(keys_here, ds, BY_LAST, preferred_element_type=jnp.float32)
        return (term if dq is None else dq + term), dk, dv

    @pl.when(step == 0)
    def _():
        greet(me.near())

    for at, todo in sorted(moves.items()):

        @pl.when(step == at)
        def _():
            for stage, number, unit in sorted(todo, key=lambda entry: (-entry[0], entry[1])):
                unit.stage(stage)

    @pl.when(step == 0)
    def _():
        values[0:HEAD_DIM, :] = v_ref[...]
        values[HEAD_DIM:, :] = (
            (lax.broadcasted_iota(jnp.int32, (16, length), 0) < 2)
            .astype(jnp.float32)
            .astype(jnp.bfloat16)
        )
        dk_sum[...] = jnp.zeros_like(dk_sum)
        dv_sum[...] = jnp.zeros_like(dv_sum)

    wide, grads, queries = prepare(step * rows, rows)
    dq = None
    for j in range(chunks):
        here = slice(j * cols, (j + 1) * cols)
        dq, dk, dv = part(
            wide, grads, queries, p_ref[:, here], k_ref[:, here], values[:, here], dq
        )
        dk_sum[:, here] += dk
        dv_sum[:, here] += dv
    dq_ref[:, pl.ds(pl.multiple_of(step * rows, rows), rows)] = (dq * scale).astype(jnp.bfloat16)

    @pl.when(step == steps - 1)
    def _():
        for first in range(0, tail, rows):
            wide, grads, queries = prepare(long + first, rows)
            dq, dk, dv = part(
                wide,
                grads,
                queries,
                tail_ref[first : first + rows, :],
                k_ref[:, long:],
                values[:, long:],
                None,
            )
            dk_sum[:, long:] += dk
            dv_sum[:, long:] += dv
            dq_ref[:, long + first : long + first + rows] = (dq * scale).astype(jnp.bfloat16)
        dk_ref[...] = (dk_sum[...] * scale).astype(jnp.bfloat16)
        dv_ref[...] = dv_sum[...].astype(jnp.bfloat16)
        for unit in plan:
            unit.stage(5)


def attn_bwd(
    probs, tail_probs, query, key, value, attn, grad_attn, inv_total, long, partials,
    collective_id, rows=512, cols=1024,
):
    blks = lax.axis_size("blk")
    lead = (lax.axis_size("seq"), blks, lax.axis_size("head") // 2, 2)
    devices = math.prod(lead)
    length = query.shape[1]
    tail = length - long
    anywhere = pl.BlockSpec(memory_space=pl.ANY)
    edges = [(partial.shape[0] // devices, partial.shape[1]) for partial in partials]
    units = len(weight_units((edges[0][0], edges[1][1], edges[2][0])))
    narrow = jax.ShapeDtypeStruct((HEAD_DIM, length), jnp.bfloat16)
    return pl.pallas_call(
        functools.partial(attn_bwd_kernel, blks, rows, cols),
        grid=(long // rows,),
        in_specs=[pl.BlockSpec((rows, long), lambda step: (step, 0)), once((tail, tail))]
        + [once((HEAD_DIM, length))] * 5
        + [once((8, length))]
        + [anywhere] * 3,
        out_specs=[once((HEAD_DIM, length))] * 3 + [once(edge) for edge in edges],
        out_shape=[narrow] * 3 + [jax.ShapeDtypeStruct(edge, jnp.float32) for edge in edges],
        scratch_shapes=[
            pltpu.VMEM((HEAD_DIM + 16, length), jnp.bfloat16),
            pltpu.VMEM((HEAD_DIM, length), jnp.float32),
            pltpu.VMEM((HEAD_DIM, length), jnp.float32),
            *reduce_scratch(units, blks),
        ],
        compiler_params=pltpu.CompilerParams(
            collective_id=collective_id, has_side_effects=True, vmem_limit_bytes=62 * 2**20
        ),
        cost_estimate=pl.CostEstimate(
            flops=8 * long * long * HEAD_DIM, bytes_accessed=2 * long * long, transcendentals=0
        ),
        name="attn_bwd",
    )(
        probs, tail_probs, query, key, value, attn, grad_attn, inv_total,
        *[partial.reshape(lead + edge) for partial, edge in zip(partials, edges)],
    )


GROUP = ("blk", "head")


def greet_group(me, count, heads):
    barrier = pltpu.get_barrier_semaphore()
    for step in range(1, count):
        peer = lax.rem(me + step, count)
        pl.semaphore_signal(
            barrier,
            inc=1,
            device_id={"blk": peer // heads, "head": lax.rem(peer, heads)},
            device_id_type=MESH,
        )
    pl.semaphore_wait(barrier, count - 1)


def swap_kernel(to_heads, blks, heads, in_ref, out_ref, send_sem, recv_sem, own_sem):
    count = blks * heads
    me = lax.axis_index("blk") * heads + lax.axis_index("head")
    greet_group(me, count, heads)
    if to_heads:
        rows = in_ref.shape[2]
        width = in_ref.shape[3]
        take = lambda owner: in_ref.at[:, owner]
        place = lambda source: out_ref.at[
            :, :, pl.ds(pl.multiple_of(source * width, width), width)
        ]
    else:
        rows = in_ref.shape[1]
        width = in_ref.shape[2] // count
        take = lambda owner: in_ref.at[:, :, pl.ds(pl.multiple_of(owner * width, width), width)]
        place = lambda source: out_ref.at[:, source]
    own = pltpu.make_async_copy(take(me), place(me), own_sem)
    own.start()
    copies = []
    for step in range(1, count):
        peer = lax.rem(me + step, count)
        copy = pltpu.make_async_remote_copy(
            src_ref=take(peer),
            dst_ref=place(me),
            send_sem=send_sem.at[step],
            recv_sem=recv_sem.at[step],
            device_id={"blk": peer // heads, "head": lax.rem(peer, heads)},
            device_id_type=MESH,
        )
        copy.start()
        copies.append(copy)
    own.wait()
    for copy in copies:
        copy.wait_send()
        copy.wait_recv()


def swap(values, to_heads, collective_id):
    blks, heads = lax.axis_size("blk"), lax.axis_size("head")
    count = blks * heads
    parts = values.shape[0]
    if to_heads:
        shape = (parts, values.shape[2], values.shape[3] * count)
    else:
        shape = (parts, count, values.shape[1], values.shape[2] // count)
    return pl.pallas_call(
        functools.partial(swap_kernel, to_heads, blks, heads),
        out_shape=jax.ShapeDtypeStruct(shape, values.dtype),
        in_specs=[pl.BlockSpec(memory_space=pl.ANY)],
        out_specs=pl.BlockSpec(memory_space=pl.ANY),
        scratch_shapes=[
            pltpu.SemaphoreType.DMA((count,)),
            pltpu.SemaphoreType.DMA((count,)),
            pltpu.SemaphoreType.DMA,
        ],
        compiler_params=pltpu.CompilerParams(collective_id=collective_id, has_side_effects=True),
        name="swap_to_heads" if to_heads else "swap_to_tokens",
    )(values)


def tail_segments(doc_lengths, first, rows):
    return segment_ids(doc_lengths, first + lax.iota(jnp.int32, rows))


def shards_heads(
    layer_input,
    weight_query,
    weight_key,
    weight_value,
    weight_output,
    weight_expand,
    weight_reduce,
    bias_query,
    bias_value,
    bias_output,
    bias_expand,
    bias_reduce,
    first_gain,
    first_shift,
    second_gain,
    second_shift,
    cotangent,
    doc_lengths,
):
    tok_rows, model_width = layer_input.shape[1:]
    head_count = lax.axis_size("head")
    blk_count = lax.axis_size("blk")
    count = head_count * blk_count
    seq_len = tok_rows * count
    long_rows = seq_len - seq_len // blk_count // 2
    flat_rows = layer_input.reshape(tok_rows, model_width)

    vectors = (
        bias_query,
        bias_value,
        bias_output,
        bias_reduce,
        first_gain,
        first_shift,
        second_gain,
        second_shift,
        bias_expand,
    )
    sizes = [vector.shape[0] for vector in vectors]
    lanes = 128
    spare = 16 * lanes - sum(sizes)
    packed = jnp.concatenate(vectors + (jnp.zeros((spare,), layer_input.dtype),))
    w_qkv, packed = first_gather(
        weight_query, weight_key, weight_value, packed.reshape(16, lanes), 4
    )
    w_qkv = w_qkv.reshape(model_width, 3 * model_width)
    packed = packed.reshape(-1, 16 * lanes).astype(jnp.float32)
    whole, start = [], 0
    for size in sizes:
        whole.append(packed[:, start : start + size].reshape(-1))
        start += size
    b_query, b_value, b_output, b_reduce, gain_one, shift_one, gain_two, shift_two, b_expand = whole

    b_qkv = jnp.concatenate((b_query, jnp.zeros_like(b_query), b_value))
    qkv = lax.dot_general(
        w_qkv, flat_rows, (((0,), (1,)), ((), ())), preferred_element_type=jnp.float32
    )
    qkv = (qkv + b_qkv[:, None]).astype(jnp.bfloat16).reshape(3, HEADS, HEAD_DIM, tok_rows)
    qkv = swap(qkv, True, 0)
    query, key, value = qkv[0], qkv[1], qkv[2]
    seg = tail_segments(doc_lengths, long_rows, seq_len - long_rows)[0]
    probs, tail_probs, attn, inv_total, w_output, w_expand, w_reduce = attn_fwd(
        query,
        key,
        value,
        seg,
        long_rows,
        (weight_output, weight_expand, weight_reduce),
        5,
    )
    w_output = w_output.reshape(-1, weight_output.shape[1])
    w_expand = w_expand.reshape(-1, weight_expand.shape[1])
    w_reduce = w_reduce.reshape(-1, weight_reduce.shape[1])
    attn_flat = swap(attn[None], False, 1).reshape(model_width, tok_rows)

    resid_one = flat_rows.astype(jnp.float32) + left_dot(attn_flat, w_output) + b_output
    normed_one, norm_one_pull = jax.vjp(layer_norm, resid_one, gain_one, shift_one)
    normed_low = normed_one.astype(jnp.bfloat16)
    pre_act = plain_dot(normed_low, w_expand) + b_expand
    hidden_f32, gelu_pull = jax.vjp(gelu_curve, pre_act)
    hidden = hidden_f32.astype(jnp.bfloat16)
    resid_two = normed_one + plain_dot(hidden, w_reduce) + b_reduce
    result, norm_two_pull = jax.vjp(layer_norm, resid_two, gain_two, shift_two)
    layer_output = result.astype(jnp.bfloat16).reshape(layer_input.shape)
    tok_first = (lax.axis_index("blk") * head_count + lax.axis_index("head")) * tok_rows
    tok_seg = segment_ids(doc_lengths, tok_first + lax.iota(jnp.int32, tok_rows))
    live = (tok_seg > 0).astype(jnp.float32)
    grad_out = (cotangent.astype(jnp.float32) * live[..., None]).reshape(-1, model_width)
    grad_resid_two, grad_gain_two, grad_shift_two = norm_two_pull(grad_out)
    grad_ffn = grad_resid_two.astype(jnp.bfloat16)
    grad_w_reduce = left_dot(hidden, grad_ffn)
    grad_b_reduce = jnp.sum(grad_ffn.astype(jnp.float32), axis=0)
    (grad_pre,) = gelu_pull(right_dot(grad_ffn, w_reduce))
    grad_pre = grad_pre.astype(jnp.bfloat16)
    grad_w_expand = left_dot(normed_low, grad_pre)
    grad_b_expand = jnp.sum(grad_pre.astype(jnp.float32), axis=0)
    grad_normed = grad_resid_two + right_dot(grad_pre, w_expand)
    grad_resid_one, grad_gain_one, grad_shift_one = norm_one_pull(grad_normed)
    grad_branch = grad_resid_one.astype(jnp.bfloat16)
    grad_w_output = plain_dot(attn_flat, grad_branch)
    grad_b_output = jnp.sum(grad_branch.astype(jnp.float32), axis=0)
    grad_attn = right_dot(w_output, grad_branch).astype(jnp.bfloat16)
    grad_attn = swap(grad_attn.reshape(1, HEADS, HEAD_DIM, tok_rows), True, 2)[0]

    *grad_qkv, grad_w_output, grad_w_expand, grad_w_reduce = attn_bwd(
        probs,
        tail_probs,
        query,
        key,
        value,
        attn,
        grad_attn,
        inv_total,
        long_rows,
        [grad.astype(jnp.bfloat16) for grad in (grad_w_output, grad_w_expand, grad_w_reduce)],
        6,
    )
    grad_qkv = swap(jnp.stack(grad_qkv), False, 3).reshape(3 * model_width, tok_rows)
    grad_w_qkv = lax.dot_general(
        flat_rows, grad_qkv, (((0,), (1,)), ((), ())), preferred_element_type=jnp.float32
    )
    grad_input = grad_resid_one + lax.dot_general(
        grad_qkv, w_qkv, (((0,), (1,)), ((), ())), preferred_element_type=jnp.float32
    )
    grad_b_qkv = jnp.sum(grad_qkv.astype(jnp.float32), axis=1)

    sums = (
        grad_b_qkv[:model_width],
        grad_b_qkv[2 * model_width :],
        grad_b_output,
        grad_b_reduce,
        grad_gain_one,
        grad_shift_one,
        grad_gain_two,
        grad_shift_two,
        grad_b_expand,
    )
    sums = jnp.concatenate([term.reshape(-1, size) for term, size in zip(sums, sizes)], axis=1)
    sums = jnp.pad(sums, ((0, 0), (0, 8 * lanes - sums.shape[1]))).reshape(-1, 8, lanes)
    grad_w_qkv, sums = final_reduce(grad_w_qkv.astype(jnp.bfloat16), sums, 7)
    sums = sums.reshape(-1)
    parts, start = [], 0
    for size in sizes:
        parts.append(sums[start : start + size])
        start += size
    g_query, g_value, g_output, g_reduce, g_gain_one, g_shift_one, g_gain_two, g_shift_two, g_expand = parts
    return (
        layer_output,
        grad_input.reshape(layer_input.shape),
        grad_w_qkv[:, :model_width],
        grad_w_qkv[:, model_width : 2 * model_width],
        grad_w_qkv[:, 2 * model_width :],
        grad_w_output,
        grad_w_expand,
        grad_w_reduce,
        g_query,
        g_value,
        g_output,
        g_expand,
        g_reduce,
        g_gain_one,
        g_shift_one,
        g_gain_two,
        g_shift_two,
    )


def solution(mesh):
    placed = (
        P("seq", ("blk", "head"), None),
        P(("seq", "blk", "head"), None),
        P(("seq", "blk", "head"), None),
        P(("seq", "blk", "head"), None),
        P(("seq", "blk", "head"), None),
        P(("seq", "blk", "head"), None),
        P(("seq", "blk", "head"), None),
        P(("seq", "blk", "head")),
        P(("seq", "blk", "head")),
        P(("seq", "blk", "head")),
        P(("seq", "blk", "head")),
        P(("seq", "blk", "head")),
        P(("seq", "blk", "head")),
        P(("seq", "blk", "head")),
        P(("seq", "blk", "head")),
        P(("seq", "blk", "head")),
        P("seq", ("blk", "head"), None),
        P("seq", None),
    )
    group = mesh.shape["blk"] * mesh.shape["head"]
    body = shards_heads if group == HEADS else shards_general
    return jax.shard_map(
        body,
        mesh=mesh,
        in_specs=placed,
        out_specs=(
            P("seq", ("blk", "head"), None),
            P("seq", ("blk", "head"), None),
            P(("seq", "blk", "head"), None),
            P(("seq", "blk", "head"), None),
            P(("seq", "blk", "head"), None),
            P(("seq", "blk", "head"), None),
            P(("seq", "blk", "head"), None),
            P(("seq", "blk", "head"), None),
            P(("seq", "blk", "head")),
            P(("seq", "blk", "head")),
            P(("seq", "blk", "head")),
            P(("seq", "blk", "head")),
            P(("seq", "blk", "head")),
            P(("seq", "blk", "head")),
            P(("seq", "blk", "head")),
            P(("seq", "blk", "head")),
            P(("seq", "blk", "head")),
        ),
        check_vma=False,
    )
```

```python
import functools
import math

import jax
import jax.numpy as jnp
from jax import lax
from jax.experimental import pallas as pl
from jax.experimental.pallas import tpu as pltpu
from jax.sharding import PartitionSpec as P

HEADS = 16
HEAD_DIM = 64


NORM_EPS = 1e-05
INV_ROOT2 = 0.7071067811865476


def segment_ids(doc_lengths, positions):
    ends = jnp.cumsum(doc_lengths, axis=-1)
    counted = jnp.sum((ends[:, None, :] <= positions[None, :, None]).astype(jnp.int32), axis=-1)
    return jnp.where(positions[None, :] < ends[:, -1:], counted + 1, 0)


def layer_norm(values, gain, shift):
    center = values - jnp.mean(values, axis=-1, keepdims=True)
    spread = jnp.mean(center * center, axis=-1, keepdims=True)
    return center * lax.rsqrt(spread + NORM_EPS) * gain + shift


def gelu_curve(values):
    return 0.5 * values * (1.0 + lax.erf(values * INV_ROOT2))


def plain_dot(left, right):
    return jnp.dot(left, right, preferred_element_type=jnp.float32)


def left_dot(left, right):
    return lax.dot_general(
        left, right, (((0,), (0,)), ((), ())), preferred_element_type=jnp.float32
    )


def right_dot(left, right):
    return lax.dot_general(
        left, right, (((1,), (1,)), ((), ())), preferred_element_type=jnp.float32
    )


def score_grads(scores, allowed, grad_part, value_part, lse_part, delta_part):
    probs = jnp.where(allowed, jnp.exp(scores - lse_part[..., None]), 0.0)
    grad_probs = jnp.einsum(
        "sqhd,skhd->shqk", grad_part, value_part, preferred_element_type=jnp.float32
    )
    grad_scores = (probs * (grad_probs - delta_part[..., None])).astype(jnp.bfloat16)
    return (probs, grad_scores)


def shards_general(
    layer_input,
    weight_query,
    weight_key,
    weight_value,
    weight_output,
    weight_expand,
    weight_reduce,
    bias_query,
    bias_value,
    bias_output,
    bias_expand,
    bias_reduce,
    first_gain,
    first_shift,
    second_gain,
    second_shift,
    cotangent,
    doc_lengths,
):
    seq_count, tok_rows, model_width = layer_input.shape
    head_count = lax.axis_size("head")
    blk_count = lax.axis_size("blk")
    heads_here = HEADS // head_count
    score_scale = HEAD_DIM ** (-0.5)
    gathered = (
        lax.all_gather(weight_query, ("seq", "blk", "head"), axis=0, tiled=True),
        lax.all_gather(weight_key, ("seq", "blk", "head"), axis=0, tiled=True),
        lax.all_gather(weight_value, ("seq", "blk", "head"), axis=0, tiled=True),
        lax.all_gather(weight_output, ("seq", "blk", "head"), axis=0, tiled=True),
        lax.all_gather(weight_expand, ("seq", "blk", "head"), axis=0, tiled=True),
        lax.all_gather(weight_reduce, ("seq", "blk", "head"), axis=0, tiled=True),
        lax.all_gather(bias_query, ("seq", "blk", "head"), axis=0, tiled=True),
        lax.all_gather(bias_value, ("seq", "blk", "head"), axis=0, tiled=True),
        lax.all_gather(bias_output, ("seq", "blk", "head"), axis=0, tiled=True),
        lax.all_gather(bias_expand, ("seq", "blk", "head"), axis=0, tiled=True),
        lax.all_gather(bias_reduce, ("seq", "blk", "head"), axis=0, tiled=True),
        lax.all_gather(first_gain, ("seq", "blk", "head"), axis=0, tiled=True),
        lax.all_gather(first_shift, ("seq", "blk", "head"), axis=0, tiled=True),
        lax.all_gather(second_gain, ("seq", "blk", "head"), axis=0, tiled=True),
        lax.all_gather(second_shift, ("seq", "blk", "head"), axis=0, tiled=True),
    )
    w_query, w_key, w_value, w_output, w_expand, w_reduce = gathered[:6]
    b_query, b_value, b_output, b_expand, b_reduce, gain_one, shift_one, gain_two, shift_two = [
        vector.astype(jnp.float32) for vector in gathered[6:]
    ]
    flat_rows = layer_input.reshape(-1, model_width)
    queries = (
        (plain_dot(flat_rows, w_query) + b_query).astype(jnp.bfloat16).reshape(layer_input.shape)
    )
    key_rows = plain_dot(flat_rows, w_key).astype(jnp.bfloat16).reshape(layer_input.shape)
    value_rows = (
        (plain_dot(flat_rows, w_value) + b_value).astype(jnp.bfloat16).reshape(layer_input.shape)
    )
    query_heads, key_heads, value_heads = (
        lax.all_to_all(queries, "head", split_axis=2, concat_axis=1, tiled=True),
        lax.all_to_all(key_rows, "head", split_axis=2, concat_axis=1, tiled=True),
        lax.all_to_all(value_rows, "head", split_axis=2, concat_axis=1, tiled=True),
    )
    block_rows = query_heads.shape[1]
    block_first = lax.axis_index("blk") * block_rows
    query_seg = segment_ids(doc_lengths, block_first + lax.iota(jnp.int32, block_rows))
    query_split = query_heads.reshape(seq_count, block_rows, heads_here, HEAD_DIM)

    def key_block(shard_piece, block_index, block_width):
        key_offset = block_index * block_width
        key_part = lax.dynamic_slice_in_dim(shard_piece[0], key_offset, block_width, 1).reshape(
            seq_count, block_width, heads_here, HEAD_DIM
        )
        value_part = lax.dynamic_slice_in_dim(shard_piece[1], key_offset, block_width, 1).reshape(
            seq_count, block_width, heads_here, HEAD_DIM
        )
        key_seg = segment_ids(doc_lengths, key_offset + lax.iota(jnp.int32, block_width))
        allowed = query_seg[:, None, :, None] == key_seg[:, None, None, :]
        scores = (
            jnp.einsum("sqhd,skhd->shqk", query_split, key_part, preferred_element_type=jnp.float32)
            * score_scale
        )
        return (key_offset, key_part, value_part, allowed, scores)

    stat_shape = (seq_count, heads_here, block_rows)
    start_state = (
        jnp.full(stat_shape, -1e30, jnp.float32),
        jnp.zeros(stat_shape, jnp.float32),
        jnp.zeros(stat_shape + (HEAD_DIM,), jnp.float32),
    )
    shard_piece = (
        lax.all_gather(key_heads, "blk", axis=1, tiled=True),
        lax.all_gather(value_heads, "blk", axis=1, tiled=True),
    )
    piece_rows = shard_piece[0].shape[1]
    block_width = math.gcd(piece_rows, 512)

    def advance(block_index, loop_state):
        running_max, row_total, accum = loop_state
        key_offset, key_part, value_part, allowed, scores = key_block(
            shard_piece, block_index, block_width
        )
        scores = jnp.where(allowed, scores, -1e30)
        new_max = jnp.maximum(running_max, jnp.max(scores, axis=-1))
        rescale = jnp.exp(running_max - new_max)
        weights = jnp.where(allowed, jnp.exp(scores - new_max[..., None]), 0.0)
        row_total = row_total * rescale + jnp.sum(weights, axis=-1)
        accum = accum * rescale[..., None] + jnp.einsum(
            "shqk,skhd->shqd",
            weights.astype(jnp.bfloat16),
            value_part,
            preferred_element_type=jnp.float32,
        )
        return (new_max, row_total, accum)

    running_max, row_total, accum = lax.fori_loop(
        0, piece_rows // block_width, advance, start_state
    )
    log_total = running_max + jnp.log(row_total)
    attn_heads = accum / row_total[..., None]
    attn_send = (
        attn_heads.transpose(0, 2, 1, 3)
        .reshape(seq_count, block_rows, heads_here * HEAD_DIM)
        .astype(jnp.bfloat16)
    )
    attn_tokens = lax.all_to_all(attn_send, "head", split_axis=1, concat_axis=2, tiled=True)
    attn_flat = attn_tokens.reshape(-1, model_width)
    resid_one = flat_rows.astype(jnp.float32) + plain_dot(attn_flat, w_output) + b_output
    normed_one, norm_one_pull = jax.vjp(layer_norm, resid_one, gain_one, shift_one)
    normed_low = normed_one.astype(jnp.bfloat16)
    pre_act = plain_dot(normed_low, w_expand) + b_expand
    hidden_f32, gelu_pull = jax.vjp(gelu_curve, pre_act)
    hidden = hidden_f32.astype(jnp.bfloat16)
    resid_two = normed_one + plain_dot(hidden, w_reduce) + b_reduce
    result, norm_two_pull = jax.vjp(layer_norm, resid_two, gain_two, shift_two)
    layer_output = result.astype(jnp.bfloat16).reshape(layer_input.shape)
    tok_first = (lax.axis_index("blk") * head_count + lax.axis_index("head")) * tok_rows
    tok_seg = segment_ids(doc_lengths, tok_first + lax.iota(jnp.int32, tok_rows))
    live = (tok_seg > 0).astype(jnp.float32)
    grad_out = (cotangent.astype(jnp.float32) * live[..., None]).reshape(-1, model_width)
    grad_resid_two, grad_gain_two, grad_shift_two = norm_two_pull(grad_out)
    grad_ffn = grad_resid_two.astype(jnp.bfloat16)
    grad_w_reduce = left_dot(hidden, grad_ffn)
    grad_b_reduce = jnp.sum(grad_ffn.astype(jnp.float32), axis=0)
    (grad_pre,) = gelu_pull(right_dot(grad_ffn, w_reduce))
    grad_pre = grad_pre.astype(jnp.bfloat16)
    grad_w_expand = left_dot(normed_low, grad_pre)
    grad_b_expand = jnp.sum(grad_pre.astype(jnp.float32), axis=0)
    grad_normed = grad_resid_two + right_dot(grad_pre, w_expand)
    grad_resid_one, grad_gain_one, grad_shift_one = norm_one_pull(grad_normed)
    grad_branch = grad_resid_one.astype(jnp.bfloat16)
    grad_w_output = left_dot(attn_flat, grad_branch)
    grad_b_output = jnp.sum(grad_branch.astype(jnp.float32), axis=0)
    grad_attn = right_dot(grad_branch, w_output).astype(jnp.bfloat16).reshape(layer_input.shape)
    grad_attn_heads = lax.all_to_all(grad_attn, "head", split_axis=2, concat_axis=1, tiled=True)
    grad_attn_split = grad_attn_heads.reshape(seq_count, block_rows, heads_here, HEAD_DIM)
    row_delta = jnp.einsum("sqhd,shqd->shq", grad_attn_split.astype(jnp.float32), attn_heads)
    full_rows = blk_count * block_rows
    query_zero = jnp.zeros((seq_count, block_rows, heads_here, HEAD_DIM), jnp.float32)
    back_state = (
        query_zero,
        jnp.zeros((seq_count, full_rows, heads_here * HEAD_DIM), jnp.float32),
        jnp.zeros((seq_count, full_rows, heads_here * HEAD_DIM), jnp.float32),
    )
    fold_shard_piece = (
        lax.all_gather(key_heads, "blk", axis=1, tiled=True),
        lax.all_gather(value_heads, "blk", axis=1, tiled=True),
    )
    piece_rows = fold_shard_piece[0].shape[1]
    fold_block_width = math.gcd(piece_rows, 512)

    def advance(block_index, loop_state):
        grad_query, grad_keys, grad_values = loop_state
        key_offset, key_part, value_part, allowed, scores = key_block(
            fold_shard_piece, block_index, fold_block_width
        )
        probs, grad_scores = score_grads(
            scores, allowed, grad_attn_split, value_part, log_total, row_delta
        )
        grad_query = (
            grad_query
            + jnp.einsum(
                "shqk,skhd->sqhd", grad_scores, key_part, preferred_element_type=jnp.float32
            )
            * score_scale
        )
        key_term = (
            jnp.einsum(
                "shqk,sqhd->skhd", grad_scores, query_split, preferred_element_type=jnp.float32
            )
            * score_scale
        )
        value_term = jnp.einsum(
            "shqk,sqhd->skhd",
            probs.astype(jnp.bfloat16),
            grad_attn_split,
            preferred_element_type=jnp.float32,
        )
        grad_keys = lax.dynamic_update_slice_in_dim(
            grad_keys,
            key_term.reshape(seq_count, fold_block_width, heads_here * HEAD_DIM),
            key_offset,
            1,
        )
        grad_values = lax.dynamic_update_slice_in_dim(
            grad_values,
            value_term.reshape(seq_count, fold_block_width, heads_here * HEAD_DIM),
            key_offset,
            1,
        )
        return (grad_query, grad_keys, grad_values)

    back_out = lax.fori_loop(0, piece_rows // fold_block_width, advance, back_state)
    grad_query = back_out[0]
    key_share, value_share = (
        lax.psum_scatter(
            back_out[1].astype(jnp.bfloat16), "blk", scatter_dimension=1, tiled=True
        ).astype(jnp.float32),
        lax.psum_scatter(
            back_out[2].astype(jnp.bfloat16), "blk", scatter_dimension=1, tiled=True
        ).astype(jnp.float32),
    )
    query_send = grad_query.reshape(seq_count, block_rows, heads_here * HEAD_DIM).astype(
        jnp.bfloat16
    )
    query_back, key_back, value_back = (
        lax.all_to_all(query_send, "head", split_axis=1, concat_axis=2, tiled=True),
        lax.all_to_all(
            key_share.astype(jnp.bfloat16), "head", split_axis=1, concat_axis=2, tiled=True
        ),
        lax.all_to_all(
            value_share.astype(jnp.bfloat16), "head", split_axis=1, concat_axis=2, tiled=True
        ),
    )
    query_back = query_back.reshape(-1, model_width)
    key_back = key_back.reshape(-1, model_width)
    value_back = value_back.reshape(-1, model_width)
    grad_w_query = left_dot(flat_rows, query_back)
    grad_w_key = left_dot(flat_rows, key_back)
    grad_w_value = left_dot(flat_rows, value_back)
    grad_b_query = jnp.sum(query_back.astype(jnp.float32), axis=0)
    grad_b_value = jnp.sum(value_back.astype(jnp.float32), axis=0)
    grad_input = (
        grad_resid_one
        + right_dot(query_back, w_query)
        + right_dot(key_back, w_key)
        + right_dot(value_back, w_value)
    )
    grad_input = grad_input.reshape(layer_input.shape)
    shares_all = (
        lax.psum_scatter(grad_w_query, ("seq", "blk", "head"), scatter_dimension=0, tiled=True),
        lax.psum_scatter(grad_w_key, ("seq", "blk", "head"), scatter_dimension=0, tiled=True),
        lax.psum_scatter(grad_w_value, ("seq", "blk", "head"), scatter_dimension=0, tiled=True),
        lax.psum_scatter(grad_w_output, ("seq", "blk", "head"), scatter_dimension=0, tiled=True),
        lax.psum_scatter(grad_w_expand, ("seq", "blk", "head"), scatter_dimension=0, tiled=True),
        lax.psum_scatter(grad_w_reduce, ("seq", "blk", "head"), scatter_dimension=0, tiled=True),
        lax.psum_scatter(grad_b_query, ("seq", "blk", "head"), scatter_dimension=0, tiled=True),
        lax.psum_scatter(grad_b_value, ("seq", "blk", "head"), scatter_dimension=0, tiled=True),
        lax.psum_scatter(grad_b_output, ("seq", "blk", "head"), scatter_dimension=0, tiled=True),
        lax.psum_scatter(grad_b_expand, ("seq", "blk", "head"), scatter_dimension=0, tiled=True),
        lax.psum_scatter(grad_b_reduce, ("seq", "blk", "head"), scatter_dimension=0, tiled=True),
        lax.psum_scatter(grad_gain_one, ("seq", "blk", "head"), scatter_dimension=0, tiled=True),
        lax.psum_scatter(grad_shift_one, ("seq", "blk", "head"), scatter_dimension=0, tiled=True),
        lax.psum_scatter(grad_gain_two, ("seq", "blk", "head"), scatter_dimension=0, tiled=True),
        lax.psum_scatter(grad_shift_two, ("seq", "blk", "head"), scatter_dimension=0, tiled=True),
    )
    return (
        layer_output,
        grad_input,
        shares_all[0],
        shares_all[1],
        shares_all[2],
        shares_all[3],
        shares_all[4],
        shares_all[5],
        shares_all[6],
        shares_all[7],
        shares_all[8],
        shares_all[9],
        shares_all[10],
        shares_all[11],
        shares_all[12],
        shares_all[13],
        shares_all[14],
    )


MESH = pl.DeviceIdType.MESH
EVERY = ("seq", "blk", "head")
EDGE = 32
UNIT = 1024


class Place:
    def __init__(self, blks):
        self.blks = blks
        self.x = lax.axis_index("seq")
        self.z = lax.axis_index("blk")
        lane = lax.axis_index("head")
        self.y = lane // 2
        self.c = lax.rem(lane, 2)
        self.index = self.z * 4 + lane
        self.group = blks * 4

    def peer(self, step):
        index = lax.rem(self.index + step, self.group)
        return index, self.member(index)

    def member(self, index):
        return {"seq": self.x, "blk": index // 4, "head": lax.rem(index, 4)}

    def at(self, x=None, z=None, y=None, c=None):
        x = self.x if x is None else x
        z = self.z if z is None else z
        y = self.y if y is None else y
        c = self.c if c is None else c
        return {"seq": x, "blk": z, "head": y * 2 + c}

    def column(self):
        return [lax.rem(self.z + step, self.blks) for step in range(1, self.blks)]

    def near(self):
        return [self.at(z=z) for z in self.column()] + [
            self.at(x=1 - self.x),
            self.at(y=1 - self.y),
            self.at(c=1 - self.c),
        ]

    def others(self, devices):
        own = (self.x * self.blks + self.z) * 4 + self.y * 2 + self.c
        found = []
        for step in range(1, devices):
            index = lax.rem(own + step, devices)
            found.append(
                {
                    "seq": index // (self.blks * 4),
                    "blk": lax.rem(index // 4, self.blks),
                    "head": lax.rem(index, 4),
                }
            )
        return own, found


def greet(devices):
    barrier = pltpu.get_barrier_semaphore()
    for device in devices:
        pl.semaphore_signal(barrier, inc=1, device_id=device, device_id_type=MESH)
    pl.semaphore_wait(barrier, len(devices))


class Wires:
    def __init__(self, send, recv):
        self.send, self.recv, self.used = send, recv, 0

    def copy(self, source, target, device):
        slot = self.used
        self.used += 1
        return pltpu.make_async_remote_copy(
            src_ref=source,
            dst_ref=target,
            send_sem=self.send.at[slot],
            recv_sem=self.recv.at[slot],
            device_id=device,
            device_id_type=MESH,
        )


def view(ref, index, piece):
    rows, cols = piece
    return ref.at[tuple(index) + (pl.ds(*rows), pl.ds(*cols))]


ALL = slice(None)


def share_line(me, wires, ref, piece):
    own = view(ref, (me.x, me.z, me.y, me.c), piece)
    return [wires.copy(own, own, me.at(z=peer)) for peer in me.column()]


class Gather:
    WIRES = 7

    def __init__(self, me, wires, ref, piece, turned, ready=False):
        x, z, y, c = me.x, me.z, me.y, me.c
        self.first = [] if ready else share_line(me, wires, ref, piece)
        line = view(ref, (x, ALL, y, c), piece)
        if turned:
            half, rest = view(ref, (ALL, ALL, y, c), piece), view(ref, (ALL, ALL, 1 - y, c), piece)
            self.second = wires.copy(line, line, me.at(x=1 - x))
            self.third = wires.copy(half, half, me.at(y=1 - y))
        else:
            half, rest = view(ref, (x, ALL, ALL, c), piece), view(ref, (1 - x, ALL, ALL, c), piece)
            self.second = wires.copy(line, line, me.at(y=1 - y))
            self.third = wires.copy(half, half, me.at(x=1 - x))
        self.near = wires.copy(half, half, me.at(c=1 - c))
        self.far = wires.copy(rest, rest, me.at(c=1 - c))

    def stage(self, index):
        if index == 0:
            for copy in self.first:
                copy.start()
        elif index == 1:
            for copy in self.first:
                copy.wait_recv()
            self.second.start()
        elif index == 2:
            self.second.wait_recv()
            self.third.start()
            self.near.start()
        elif index == 3:
            self.third.wait_recv()
            self.far.start()
        else:
            self.near.wait_recv()
            self.far.wait_recv()
            for copy in (*self.first, self.second, self.third, self.near, self.far):
                copy.wait_send()


class Reduce:
    WIRES = 6

    def __init__(self, me, wires, ref, piece, turned, own, own_sem, r0, r1, r2, r3, out, out_piece):
        x, z, y, c = me.x, me.z, me.y, me.c
        self.place, self.turned, self.out, self.out_piece = me, turned, out, out_piece
        self.r0, self.r1, self.r2, self.r3 = r0, r1, r2, r3
        if own is None:
            self.load = None
            self.own = lambda at: ref[at + (c, pl.ds(*piece[0]), pl.ds(*piece[1]))]
        else:
            self.load = pltpu.make_async_copy(view(ref, (ALL, ALL, ALL, c), piece), own, own_sem)
            self.own = lambda at: own[at]
        self.zero = wires.copy(view(ref, (ALL, ALL, ALL, 1 - c), piece), r0, me.at(c=1 - c))
        if turned:
            self.one = wires.copy(r0.at[:, :, 1 - y], r1, me.at(y=1 - y))
            self.two = wires.copy(r0.at[1 - x, :, y], r2, me.at(x=1 - x))
        else:
            self.one = wires.copy(r0.at[1 - x], r1, me.at(x=1 - x))
            self.two = wires.copy(r0.at[x, :, 1 - y], r2, me.at(y=1 - y))
        self.three = [
            wires.copy(r0.at[x, peer, y], r3.at[slot], me.at(z=peer))
            for slot, peer in enumerate(me.column())
        ]

    def stage(self, index):
        x, z, y = self.place.x, self.place.z, self.place.y
        blks = self.place.blks
        r0 = self.r0

        def add(target, term):
            total = r0[target].astype(jnp.float32) + term.astype(jnp.float32)
            r0[target] = total.astype(r0.dtype)

        if index == 0:
            self.zero.start()
        elif index == 1:
            self.load.start()
        elif index == 2:
            if self.load is not None:
                self.load.wait()
            self.zero.wait_recv()

            @pl.loop(0, 4 * blks)
            def _(i):
                at = (i // (2 * blks), lax.rem(i // 2, blks), lax.rem(i, 2))
                add(at, self.own(at))

            self.one.start()
        elif index == 3:
            self.one.wait_recv()

            @pl.loop(0, 2 * blks)
            def _(i):
                if self.turned:
                    a, b = i // blks, lax.rem(i, blks)
                    add((a, b, y), self.r1[a, b])
                else:
                    a, b = i // 2, lax.rem(i, 2)
                    add((x, a, b), self.r1[a, b])

            self.two.start()
        elif index == 4:
            self.two.wait_recv()

            @pl.loop(0, blks)
            def _(i):
                add((x, i, y), self.r2[i])

            for copy in self.three:
                copy.start()
        else:
            for copy in self.three:
                copy.wait_recv()
            total = r0[x, z, y].astype(jnp.float32)
            for slot in range(blks - 1):
                total = total + self.r3[slot].astype(jnp.float32)
            rows, cols = self.out_piece
            self.out[rows[0] : rows[0] + rows[1], cols[0] : cols[0] + cols[1]] = total
            for copy in (self.zero, self.one, self.two, *self.three):
                copy.wait_send()


def reduce_scratch(units, blks, cols=UNIT, dtype=jnp.bfloat16):
    turned = units // 2
    return [
        pltpu.VMEM((units, 2, blks, 2, EDGE, cols), dtype),
        pltpu.VMEM((units - turned, blks, 2, EDGE, cols), dtype),
        pltpu.VMEM((turned, 2, blks, EDGE, cols), dtype),
        pltpu.VMEM((units, blks, EDGE, cols), dtype),
        pltpu.VMEM((units, blks - 1, EDGE, cols), dtype),
        pltpu.SemaphoreType.DMA((Reduce.WIRES * units,)),
        pltpu.SemaphoreType.DMA((Reduce.WIRES * units,)),
    ]


def weight_units(edges):
    out_rows, expand_cols, reduce_rows = edges
    units = [(0, ((0, out_rows), (0, UNIT)))]
    expand = [(1, ((0, EDGE), (first, UNIT))) for first in range(0, expand_cols, UNIT)]
    reduce = [(2, ((first, EDGE), (0, UNIT))) for first in range(0, reduce_rows, EDGE)]
    for pair in zip(expand, reduce):
        units.extend(pair)
    return units


EARLY = 5


def first_kernel(
    blks, devices, wq, wk, wv, wo, we, wr, vec, out, go, ge, gr, vec_out,
    own_sem, send, recv, vec_send, vec_recv,
):
    me = Place(blks)
    index, others = me.others(devices)
    here = (me.x, me.z, me.y, me.c)
    pairs = [
        (ref, out.at[here + (ALL, pl.ds(unit * UNIT, UNIT))])
        for unit, ref in enumerate((wq, wk, wv))
    ]
    pairs += [(ref, whole.at[here]) for ref, whole in zip((wo, we, wr), (go, ge, gr))]
    pairs.append((vec, vec_out.at[index]))
    local = [
        pltpu.make_async_copy(source, target, own_sem.at[number])
        for number, (source, target) in enumerate(pairs)
    ]
    for copy in local:
        copy.start()
    greet(others)
    for copy in local:
        copy.wait()
    wires = Wires(send, recv)
    plan = [
        Gather(me, wires, out, ((0, EDGE), (half * UNIT // 2, UNIT // 2)), half % 2 == 1)
        for half in range(6)
    ]
    wholes = (go, ge, gr)
    units = weight_units((wo.shape[0], we.shape[1], wr.shape[0]))
    lines = []
    for which, piece in units[:EARLY]:
        lines += share_line(me, wires, wholes[which], piece)
    small = []
    for slot, device in enumerate(others):
        small.append(
            pltpu.make_async_remote_copy(
                src_ref=vec,
                dst_ref=vec_out.at[index],
                send_sem=vec_send.at[slot],
                recv_sem=vec_recv.at[slot],
                device_id=device,
                device_id_type=MESH,
            )
        )
    for unit in plan:
        unit.stage(0)
    for copy in small:
        copy.start()
    for wave in range(3 + 4):
        for pair in range(3):
            index = wave - pair + 1
            if 1 <= index <= 4:
                for unit in plan[2 * pair : 2 * pair + 2]:
                    unit.stage(index)
        if wave == 0:
            for copy in lines:
                copy.start()
    for copy in lines + small:
        copy.wait()


def first_gather(wq, wk, wv, shares, vec, collective_id):
    seqs, blks, heads = (lax.axis_size(name) for name in EVERY)
    devices = seqs * blks * heads
    lead = (seqs, blks, heads // 2, 2)
    wires = 6 * Gather.WIRES + EARLY * (blks - 1)
    return pl.pallas_call(
        functools.partial(first_kernel, blks, devices),
        out_shape=[jax.ShapeDtypeStruct(lead + (EDGE, 3 * UNIT), wq.dtype)]
        + [jax.ShapeDtypeStruct(lead + share.shape, share.dtype) for share in shares]
        + [jax.ShapeDtypeStruct((devices,) + vec.shape, vec.dtype)],
        in_specs=[pl.BlockSpec(memory_space=pl.ANY)] * 7,
        out_specs=[pl.BlockSpec(memory_space=pl.ANY)] * 5,
        scratch_shapes=[
            pltpu.SemaphoreType.DMA((7,)),
            pltpu.SemaphoreType.DMA((wires,)),
            pltpu.SemaphoreType.DMA((wires,)),
            pltpu.SemaphoreType.DMA((devices,)),
            pltpu.SemaphoreType.DMA((devices,)),
        ],
        compiler_params=pltpu.CompilerParams(collective_id=collective_id, has_side_effects=True),
        name="first_gather",
    )(wq, wk, wv, *shares, vec)


LOG2E = 1.4426950408889634
BY_LAST = (((1,), (1,)), ((), ()))


def lanes(ref, lead, first, width):
    return ref.at[tuple(lead) + (pl.ds(pl.multiple_of(first, width), width),)]


def wire(source, target, send_sem, recv_sem, device):
    return pltpu.make_async_remote_copy(
        src_ref=source,
        dst_ref=target,
        send_sem=send_sem,
        recv_sem=recv_sem,
        device_id=device,
        device_id_type=MESH,
    )


def attn_fwd_kernel(
    blks, rows, cols, qkv_ref, down_ref, across_ref, go_in, ge_in, gr_in,
    p_ref, tail_ref, o_ref, inv_ref, kept_ref, tokens_ref, go, ge, gr,
    land, keys, values, s0, s1, m0, m1,
    own_sem, kv_send, kv_recv, q_send, q_recv, o_send, o_recv, send, recv,
):
    step, steps = pl.program_id(0), pl.num_programs(0)
    length, long = land.shape[2], p_ref.shape[1]
    width = 2 * rows
    tail, chunks = length - long, long // cols
    main = long // width
    scale = LOG2E * HEAD_DIM**-0.5

    me = Place(blks)
    group = me.group

    def block_at(turn):
        return lax.rem(lax.rem(me.index, main) + turn, main)

    def ahead(block):
        return lax.rem(block + group - me.index, group)

    kv_copies, q_copies = [], []
    for ahead_by in range(1, group):
        peer, device = me.peer(group - ahead_by)
        kv_copies.append(
            wire(
                qkv_ref.at[1:3, peer],
                lanes(land, (pl.ds(1, 2), ALL), me.index * width, width),
                kv_send.at[ahead_by],
                kv_recv.at[ahead_by],
                device,
            )
        )
        q_copies.append(
            wire(
                qkv_ref.at[0, peer],
                lanes(land, (0, ALL), me.index * width, width),
                q_send.at[ahead_by],
                q_recv.at[ahead_by],
                device,
            )
        )
    own_in = pltpu.make_async_copy(
        qkv_ref.at[:, me.index],
        lanes(land, (ALL, ALL), me.index * width, width),
        own_sem.at[0],
    )
    keep = pltpu.make_async_copy(land, kept_ref, own_sem.at[1])

    def await_queries(block):
        @pl.when(block != me.index)
        def _():
            wire(
                qkv_ref.at[0, block],
                lanes(land, (0, ALL), block * width, width),
                q_send.at[0],
                q_recv.at[ahead(block)],
                me.member(block),
            ).wait_recv()

    def send_block(block, slot, start):
        source = lanes(o_ref, (ALL,), block * width, width)
        remote = wire(
            source,
            tokens_ref.at[me.index],
            o_send.at[slot],
            o_recv.at[lax.rem(me.index + group - block, group)],
            me.member(block),
        )
        local = pltpu.make_async_copy(source, tokens_ref.at[me.index], own_sem.at[2])

        @pl.when(block != me.index)
        def _():
            if start:
                remote.start()
            else:
                remote.wait_send()

        @pl.when(block == me.index)
        def _():
            if start:
                local.start()
            else:
                local.wait()

    wires = Wires(send, recv)
    wholes = (go, ge, gr)
    units = weight_units((go.shape[4], ge.shape[5], gr.shape[4]))
    plan = [
        Gather(me, wires, wholes[which], piece, number % 2 == 1, number < EARLY)
        for number, (which, piece) in enumerate(units)
    ]
    late = len(units) - EARLY
    moves = {}
    for number in range(late):
        for stage, at in enumerate((2, 6 + number // 2, 8 + number // 2)):
            moves.setdefault(at, []).append((plan[EARLY + number], stage))
        moves.setdefault(12, []).append((plan[EARLY + number], 3))
    for number in range(EARLY):
        moves.setdefault(1 + number // 2, []).append((plan[number], 3))

    def take_queries(start):
        part = land[0, :, pl.ds(pl.multiple_of(start, rows), rows)].astype(jnp.float32) * scale
        high = part.astype(jnp.bfloat16).astype(jnp.float32)
        return jnp.concatenate([high, part - high], 0).T.astype(jnp.bfloat16)

    def score(queries, store, j, peak):
        found = jnp.dot(
            queries, keys[:, j * cols : (j + 1) * cols], preferred_element_type=jnp.float32
        )
        store[:, j * cols : (j + 1) * cols] = found
        for first in range(0, cols, 128):
            piece = found[:, first : first + 128]
            peak = piece if peak is None else jnp.maximum(peak, piece)
        return peak

    def keep_peak(store, peak):
        store[...] = jnp.broadcast_to(jnp.max(peak, axis=1, keepdims=True), store.shape)

    def weigh(store, peak, j, row, total):
        weights = jnp.exp2(store[:, j * cols : (j + 1) * cols] - peak[:, :1]).astype(jnp.bfloat16)
        p_ref[row : row + rows, j * cols : (j + 1) * cols] = weights
        term = lax.dot_general(
            values[:, j * cols : (j + 1) * cols],
            weights,
            BY_LAST,
            preferred_element_type=jnp.float32,
        )
        return term if total is None else total + term

    def finish(total, start):
        place = pl.ds(pl.multiple_of(start, rows), rows)
        inverse = 1.0 / total[HEAD_DIM : HEAD_DIM + 1]
        o_ref[:, place] = (total[:HEAD_DIM] * inverse).astype(jnp.bfloat16)
        inv_ref[:, place] = jnp.broadcast_to(inverse, (8, rows))

    @pl.when(step == 0)
    def _():
        own_in.start()
        greet([me.peer(by)[1] for by in range(1, group)] + [me.at(x=1 - me.x)])
        for copy in kv_copies:
            copy.start()
        for unit in plan[:EARLY]:
            unit.stage(1)
        for copy in q_copies:
            copy.start()
        for unit in plan[:EARLY]:
            unit.stage(2)
        own_in.wait()
        for copy in kv_copies:
            copy.wait_recv()
        keys[0:HEAD_DIM, :] = land[1]
        keys[HEAD_DIM:, :] = land[1]
        values[0:HEAD_DIM, :] = land[2]
        values[HEAD_DIM:, :] = (
            (lax.broadcasted_iota(jnp.int32, (16, length), 0) == 0)
            .astype(jnp.float32)
            .astype(jnp.bfloat16)
        )
        await_queries(block_at(0))
        queries, peak = take_queries(block_at(0) * width), None
        for j in range(chunks):
            peak = score(queries, s0, j, peak)
        keep_peak(m0, peak)

    for at, todo in sorted(moves.items()):

        @pl.when(step == at)
        def _():
            for unit, stage in todo:
                unit.stage(stage)

    block = block_at(step)
    later = block_at(jnp.minimum(step + 1, steps - 1))

    @pl.when(step < steps - 1)
    def _():
        await_queries(later)

    for half, (old, old_peak, new, new_peak) in enumerate(((s0, m0, s1, m1), (s1, m1, s0, m0))):
        queries = take_queries(block * width + rows if half == 0 else later * width)
        total, peak = None, None
        for j in range(chunks):
            total = weigh(old, old_peak, j, half * rows, total)
            peak = score(queries, new, j, peak)
        keep_peak(new_peak, peak)
        finish(total, block * width + half * rows)
    send_block(block, step, True)

    @pl.when(step == steps - 1)
    def _():
        for number in range(tail // width):
            await_queries(main + number)
        keep.start()
        for first in range(0, tail, rows):
            queries = take_queries(long + first)
            found = jnp.dot(queries, keys[:, long:], preferred_element_type=jnp.float32)
            allowed = down_ref[first : first + rows, :1] == across_ref[:1, :]
            found = jnp.where(allowed, found, -1e30)
            peak = jnp.max(found, axis=1, keepdims=True)
            weights = jnp.exp2(found - peak).astype(jnp.bfloat16)
            tail_ref[first : first + rows, :] = weights
            total = lax.dot_general(
                values[:, long:], weights, BY_LAST, preferred_element_type=jnp.float32
            )
            finish(total, long + first)
            if (first + rows) % width == 0:
                number = main + first // width
                send_block(number, number, True)
        for unit in plan:
            unit.stage(4)
        for copy in kv_copies + q_copies:
            copy.wait_send()
        for turn in range(main):
            send_block(block_at(turn), turn, False)
        for number in range(main, group):
            send_block(number, number, False)
        for ahead_by in range(1, group):
            source, device = me.peer(ahead_by)
            wire(
                lanes(o_ref, (ALL,), source * width, width),
                tokens_ref.at[source],
                o_send.at[0],
                o_recv.at[ahead_by],
                device,
            ).wait_recv()
        keep.wait()


def once(shape):
    return pl.BlockSpec(shape, lambda step: (0,) * len(shape), pipeline_mode=pl.Buffered(1))


def attn_fwd(qkv, seg, long, wholes, collective_id, cols=1024):
    blks = lax.axis_size("blk")
    group, width = qkv.shape[1], qkv.shape[3]
    rows = width // 2
    length = group * width
    tail = length - long
    down = jnp.broadcast_to(seg[:, None], (tail, 128))
    across = jnp.broadcast_to(seg[None, :], (8, tail))
    anywhere = pl.BlockSpec(memory_space=pl.ANY)
    wires = Gather.WIRES * len(
        weight_units((wholes[0].shape[4], wholes[1].shape[5], wholes[2].shape[4]))
    )
    kept = jax.ShapeDtypeStruct((3, HEAD_DIM, length), jnp.bfloat16)
    pair = [pltpu.SemaphoreType.DMA((group,))] * 2
    return pl.pallas_call(
        functools.partial(attn_fwd_kernel, blks, rows, cols),
        grid=(long // width,),
        in_specs=[anywhere, once((tail, 128)), once((8, tail))] + [anywhere] * 3,
        out_specs=[
            pl.BlockSpec((width, long), lambda step: (step, 0)),
            once((tail, tail)),
            once((HEAD_DIM, length)),
            once((8, length)),
        ]
        + [anywhere] * 5,
        out_shape=[
            jax.ShapeDtypeStruct((long, long), jnp.bfloat16),
            jax.ShapeDtypeStruct((tail, tail), jnp.bfloat16),
            jax.ShapeDtypeStruct((HEAD_DIM, length), jnp.bfloat16),
            jax.ShapeDtypeStruct((8, length), jnp.float32),
            kept,
            jax.ShapeDtypeStruct((group, HEAD_DIM, width), jnp.bfloat16),
        ]
        + [jax.ShapeDtypeStruct(whole.shape, whole.dtype) for whole in wholes],
        input_output_aliases={3: 6, 4: 7, 5: 8},
        scratch_shapes=[
            pltpu.VMEM(kept.shape, kept.dtype),
            pltpu.VMEM((2 * HEAD_DIM, length), jnp.bfloat16),
            pltpu.VMEM((HEAD_DIM + 16, length), jnp.bfloat16),
            pltpu.VMEM((rows, long), jnp.float32),
            pltpu.VMEM((rows, long), jnp.float32),
            pltpu.VMEM((rows, 128), jnp.float32),
            pltpu.VMEM((rows, 128), jnp.float32),
            pltpu.SemaphoreType.DMA((3,)),
            *pair,
            *pair,
            *pair,
            pltpu.SemaphoreType.DMA((wires,)),
            pltpu.SemaphoreType.DMA((wires,)),
        ],
        compiler_params=pltpu.CompilerParams(
            collective_id=collective_id, has_side_effects=True, vmem_limit_bytes=56 * 2**20
        ),
        cost_estimate=pl.CostEstimate(
            flops=4 * long * long * HEAD_DIM,
            bytes_accessed=2 * long * long,
            transcendentals=long * long,
        ),
        name="attn_fwd",
    )(qkv, down, across, *wholes)


def attn_bwd_kernel(
    blks, rows, cols, p_ref, tail_ref, qkv_ref, o_ref, inv_ref, grads_ref, wo, we, wr,
    dkv_ref, tokens_ref, go, ge, gr,
    land, dq_out, values, dk_sum, dv_sum, own, r0, r1a, r1b, r2, r3, send, recv,
    own_sem, do_send, do_recv, dq_send, dq_recv,
):
    step, steps = pl.program_id(0), pl.num_programs(0)
    length, long = land.shape[1], p_ref.shape[1]
    tail, chunks = length - long, long // cols
    main = long // rows
    scale = HEAD_DIM**-0.5

    me = Place(blks)
    group = me.group

    def block_at(turn):
        return lax.rem(lax.rem(me.index, main) + turn, main)

    do_copies = []
    for ahead_by in range(1, group):
        peer, device = me.peer(group - ahead_by)
        do_copies.append(
            wire(
                grads_ref.at[peer],
                lanes(land, (ALL,), me.index * rows, rows),
                do_send.at[ahead_by],
                do_recv.at[ahead_by],
                device,
            )
        )
    own_in = pltpu.make_async_copy(
        grads_ref.at[me.index], lanes(land, (ALL,), me.index * rows, rows), own_sem.at[2]
    )

    def await_grads(block):
        @pl.when(block != me.index)
        def _():
            wire(
                grads_ref.at[block],
                lanes(land, (ALL,), block * rows, rows),
                do_send.at[0],
                do_recv.at[lax.rem(block + group - me.index, group)],
                me.member(block),
            ).wait_recv()

    def send_block(block, slot, start):
        source = lanes(dq_out, (ALL,), block * rows, rows)
        remote = wire(
            source,
            tokens_ref.at[me.index],
            dq_send.at[slot],
            dq_recv.at[lax.rem(me.index + group - block, group)],
            me.member(block),
        )
        local = pltpu.make_async_copy(source, tokens_ref.at[me.index], own_sem.at[3])

        @pl.when(block != me.index)
        def _():
            if start:
                remote.start()
            else:
                remote.wait_send()

        @pl.when(block == me.index)
        def _():
            if start:
                local.start()
            else:
                local.wait()

    wires = Wires(send, recv)
    partials, totals = (wo, we, wr), (go, ge, gr)
    units = weight_units((wo.shape[4], we.shape[5], wr.shape[4]))
    plan, moves = [], {}
    for number, (which, piece) in enumerate(units):
        turned = number % 2 == 1
        unit = Reduce(
            me,
            wires,
            partials[which],
            piece,
            turned,
            own.at[number % 2],
            own_sem.at[number % 2],
            r0.at[number],
            (r1b if turned else r1a).at[number // 2],
            r2.at[number],
            r3.at[number],
            totals[which],
            piece,
        )
        plan.append(unit)
        pair = number // 2
        for stage, at in enumerate((0, pair, pair + 1, 2 * pair + 3, 2 * pair + 5)):
            moves.setdefault(min(at, main - 1), []).append((stage, number, unit))

    def prepare(start, width):
        place = pl.ds(pl.multiple_of(start, width), width)
        grads, inverse = land[:, place].astype(jnp.float32), inv_ref[:1, place]
        delta = -jnp.sum(grads * o_ref[:, place].astype(jnp.float32), axis=0, keepdims=True)
        delta = delta * inverse
        high = delta.astype(jnp.bfloat16).astype(jnp.float32)
        row = lax.broadcasted_iota(jnp.int32, (16, width), 0)
        extra = jnp.where(row == 0, high, jnp.where(row == 1, delta - high, 0.0))
        grads = grads * inverse
        wide = jnp.concatenate([grads, extra], 0).T.astype(jnp.bfloat16)
        return wide, grads.astype(jnp.bfloat16), qkv_ref[0, :, place]

    def part(wide, grads, queries, weights, keys_here, values_here, dq):
        dp = jnp.dot(wide, values_here, preferred_element_type=jnp.float32)
        ds = (weights.astype(jnp.float32) * dp).astype(jnp.bfloat16)
        dv = jnp.dot(grads, weights, preferred_element_type=jnp.float32)
        dk = jnp.dot(queries, ds, preferred_element_type=jnp.float32)
        term = lax.dot_general(keys_here, ds, BY_LAST, preferred_element_type=jnp.float32)
        return (term if dq is None else dq + term), dk, dv

    @pl.when(step == 0)
    def _():
        own_in.start()
        greet([me.peer(by)[1] for by in range(1, group)] + [me.at(x=1 - me.x)])
        for copy in do_copies:
            copy.start()

    for at, todo in sorted(moves.items()):

        @pl.when(step == at)
        def _():
            for stage, number, unit in sorted(todo, key=lambda entry: (-entry[0], entry[1])):
                unit.stage(stage)

    @pl.when(step == 0)
    def _():
        values[0:HEAD_DIM, :] = qkv_ref[2]
        values[HEAD_DIM:, :] = (
            (lax.broadcasted_iota(jnp.int32, (16, length), 0) < 2)
            .astype(jnp.float32)
            .astype(jnp.bfloat16)
        )
        dk_sum[...] = jnp.zeros_like(dk_sum)
        dv_sum[...] = jnp.zeros_like(dv_sum)
        own_in.wait()

    block = block_at(step)
    await_grads(block)
    wide, grads, queries = prepare(block * rows, rows)
    dq = None
    for j in range(chunks):
        here = slice(j * cols, (j + 1) * cols)
        dq, dk, dv = part(
            wide, grads, queries, p_ref[:, here], qkv_ref[1, :, here], values[:, here], dq
        )
        dk_sum[:, here] += dk
        dv_sum[:, here] += dv
    dq_out[:, pl.ds(pl.multiple_of(block * rows, rows), rows)] = (dq * scale).astype(jnp.bfloat16)
    send_block(block, step, True)

    @pl.when(step == steps - 1)
    def _():
        for number in range(main, group):
            await_grads(number)
            first = (number - main) * rows
            wide, grads, queries = prepare(long + first, rows)
            dq, dk, dv = part(
                wide,
                grads,
                queries,
                tail_ref[first : first + rows, :],
                qkv_ref[1, :, long:],
                values[:, long:],
                None,
            )
            dk_sum[:, long:] += dk
            dv_sum[:, long:] += dv
            dq_out[:, long + first : long + first + rows] = (dq * scale).astype(jnp.bfloat16)
            send_block(number, number, True)
        dkv_ref[0] = (dk_sum[...] * scale).astype(jnp.bfloat16)
        dkv_ref[1] = dv_sum[...].astype(jnp.bfloat16)
        for unit in plan:
            unit.stage(5)
        for copy in do_copies:
            copy.wait_send()
        for turn in range(main):
            send_block(block_at(turn), turn, False)
        for number in range(main, group):
            send_block(number, number, False)
        for ahead_by in range(1, group):
            source, device = me.peer(ahead_by)
            wire(
                lanes(dq_out, (ALL,), source * rows, rows),
                tokens_ref.at[source],
                dq_send.at[0],
                dq_recv.at[ahead_by],
                device,
            ).wait_recv()


def attn_bwd(
    probs, tail_probs, kept, attn, inv_total, grad_attn, long, partials, collective_id, cols=1024
):
    blks = lax.axis_size("blk")
    lead = (lax.axis_size("seq"), blks, lax.axis_size("head") // 2, 2)
    devices = math.prod(lead)
    length = kept.shape[2]
    tail = length - long
    group, _, rows = grad_attn.shape
    anywhere = pl.BlockSpec(memory_space=pl.ANY)
    edges = [(partial.shape[0] // devices, partial.shape[1]) for partial in partials]
    units = len(weight_units((edges[0][0], edges[1][1], edges[2][0])))
    pair = [pltpu.SemaphoreType.DMA((group,))] * 2
    return pl.pallas_call(
        functools.partial(attn_bwd_kernel, blks, rows, cols),
        grid=(long // rows,),
        in_specs=[
            pl.BlockSpec((rows, long), lambda step: (step, 0)),
            once((tail, tail)),
            once(kept.shape),
            once((HEAD_DIM, length)),
            once((8, length)),
        ]
        + [anywhere] * 4,
        out_specs=[once((2, HEAD_DIM, length)), anywhere] + [once(edge) for edge in edges],
        out_shape=[
            jax.ShapeDtypeStruct((2, HEAD_DIM, length), jnp.bfloat16),
            jax.ShapeDtypeStruct((group, HEAD_DIM, rows), jnp.bfloat16),
        ]
        + [jax.ShapeDtypeStruct(edge, jnp.float32) for edge in edges],
        scratch_shapes=[
            pltpu.VMEM((HEAD_DIM, length), jnp.bfloat16),
            pltpu.VMEM((HEAD_DIM, length), jnp.bfloat16),
            pltpu.VMEM((HEAD_DIM + 16, length), jnp.bfloat16),
            pltpu.VMEM((HEAD_DIM, length), jnp.float32),
            pltpu.VMEM((HEAD_DIM, length), jnp.float32),
            pltpu.VMEM((2, 2, blks, 2, EDGE, UNIT), jnp.bfloat16),
            *reduce_scratch(units, blks),
            pltpu.SemaphoreType.DMA((4,)),
            *pair,
            *pair,
        ],
        compiler_params=pltpu.CompilerParams(
            collective_id=collective_id, has_side_effects=True, vmem_limit_bytes=62 * 2**20
        ),
        cost_estimate=pl.CostEstimate(
            flops=8 * long * long * HEAD_DIM, bytes_accessed=2 * long * long, transcendentals=0
        ),
        name="attn_bwd",
    )(
        probs, tail_probs, kept, attn, inv_total, grad_attn,
        *[partial.reshape(lead + edge) for partial, edge in zip(partials, edges)],
    )


def last_kernel(
    blks, devices, dkv_ref, dq_ref, x_ref, w_ref, base_ref, sums_ref,
    dw_out, dx_out, sums_out,
    grads, x, xt, weights, base, turned_dx, partial, bias, landed,
    r0, r1a, r1b, r2, r3, send, recv,
    own_sem, kv_send, kv_recv, sums_send, sums_recv,
):
    me = Place(blks)
    group = me.group
    width = x.shape[0]
    depth = x.shape[1]
    index, others = me.others(devices)
    loads = [
        pltpu.make_async_copy(source, target, own_sem.at[number])
        for number, (source, target) in enumerate(
            (
                (x_ref, x),
                (dq_ref, grads.at[0]),
                (w_ref, weights),
                (base_ref, base),
                (sums_ref, bias),
                (dkv_ref.at[0, :, pl.ds(pl.multiple_of(me.index * width, width), width)], grads.at[1, me.index]),
                (dkv_ref.at[1, :, pl.ds(pl.multiple_of(me.index * width, width), width)], grads.at[2, me.index]),
            )
        )
    ]
    for copy in loads:
        copy.start()
    greet(others)
    kv_copies = [[], []]
    for which in range(2):
        for ahead_by in range(1, group):
            peer, device = me.peer(group - ahead_by)
            slot = which * group + ahead_by
            copy = wire(
                lanes(dkv_ref, (which, ALL), peer * width, width),
                grads.at[which + 1, me.index],
                kv_send.at[slot],
                kv_recv.at[slot],
                device,
            )
            copy.start()
            kv_copies[which].append(copy)

    wires = Wires(send, recv)
    plan = []
    for number in range(6):
        tensor, half = number // 2, number % 2
        plan.append(
            Reduce(
                me,
                wires,
                partial.at[tensor],
                ((0, EDGE), (half * UNIT // 2, UNIT // 2)),
                half == 1,
                None,
                None,
                r0.at[number],
                (r1b if half else r1a).at[tensor],
                r2.at[number],
                r3.at[number],
                dw_out,
                ((0, EDGE), (tensor * UNIT + half * UNIT // 2, UNIT // 2)),
            )
        )

    def work(tensor):
        taken = grads[tensor].reshape(depth, width)
        for first in range(0, depth, 256):
            term = lax.dot_general(
                xt[first : first + 256, :], taken, BY_LAST, preferred_element_type=jnp.float32
            ).astype(jnp.bfloat16)
            for share in range(first // EDGE, (first + 256) // EDGE):
                at = (share // (blks * 4), share // 4 % blks, share // 2 % 2, share % 2)
                partial[(tensor,) + at] = term[share * EDGE - first : (share + 1) * EDGE - first]
        for unit in plan[2 * tensor : 2 * tensor + 2]:
            unit.stage(0)

    def work_input(tensor):
        taken = grads[tensor].reshape(depth, width)
        for first in range(0, depth, 256):
            term = jnp.dot(
                weights[first : first + 256, tensor * depth : (tensor + 1) * depth],
                taken,
                preferred_element_type=jnp.float32,
            )
            if tensor == 0:
                turned_dx[first : first + 256, :] = term
            elif tensor == 1:
                turned_dx[first : first + 256, :] += term
            else:
                total = turned_dx[first : first + 256, :] + term
                dx_out[:, first : first + 256] = base[:, first : first + 256] + total.T

    def stages(tensor, *which):
        for stage in which:
            for unit in plan[2 * tensor : 2 * tensor + 2]:
                unit.stage(stage)

    def note_bias(tensor, row):
        ones = jnp.ones((8, width), jnp.bfloat16)
        found = lax.dot_general(
            ones, grads[tensor].reshape(depth, width), BY_LAST, preferred_element_type=jnp.float32
        )
        per = 128 * devices // depth
        for owner in range(devices):
            first = owner // per * 128
            bias[owner, row : row + 1, :] = found[:1, first : first + 128]

    loads[0].wait()
    xt[...] = x[...].astype(jnp.float32).T.astype(jnp.bfloat16)
    loads[1].wait()
    work(0)
    stages(0, 2)
    loads[4].wait()
    note_bias(0, 3)
    loads[2].wait()
    work_input(0)
    stages(0, 3)
    loads[5].wait()
    for copy in kv_copies[0]:
        copy.wait_recv()
    work(1)
    stages(0, 4)
    stages(1, 2)
    work_input(1)
    stages(1, 3)
    loads[6].wait()
    for copy in kv_copies[1]:
        copy.wait_recv()
    work(2)
    note_bias(2, 4)
    small = []
    for slot, device in enumerate(others):
        peer = (device["seq"] * blks + device["blk"]) * 4 + device["head"]
        copy = wire(
            bias.at[peer], landed.at[slot], sums_send.at[slot], sums_recv.at[slot], device
        )
        small.append(copy)
    stages(2, 2)
    for copy in small:
        copy.start()
    stages(1, 4)
    loads[3].wait()
    work_input(2)
    stages(2, 3)
    stages(0, 5)
    stages(2, 4)
    for copy in small:
        copy.wait()
    sums_out[...] = jnp.sum(landed[...], axis=0) + bias[index]
    stages(1, 5)
    stages(2, 5)
    for copy in kv_copies[0] + kv_copies[1]:
        copy.wait_send()


def last_reduce(dkv, dq, x, w_qkv, base, sums, collective_id):
    seqs, blks, heads = (lax.axis_size(name) for name in EVERY)
    devices = seqs * blks * heads
    group = blks * heads
    width, depth = x.shape
    half = UNIT // 2
    return pl.pallas_call(
        functools.partial(last_kernel, blks, devices),
        out_shape=[
            jax.ShapeDtypeStruct((EDGE, 3 * depth), jnp.float32),
            jax.ShapeDtypeStruct((width, depth), jnp.float32),
            jax.ShapeDtypeStruct(sums.shape[1:], jnp.float32),
        ],
        in_specs=[pl.BlockSpec(memory_space=pl.ANY)] * 6,
        out_specs=[pl.BlockSpec(memory_space=pltpu.VMEM)] * 3,
        scratch_shapes=[
            pltpu.VMEM((3, group, HEAD_DIM, width), jnp.bfloat16),
            pltpu.VMEM((width, depth), jnp.bfloat16),
            pltpu.VMEM((depth, width), jnp.bfloat16),
            pltpu.VMEM((depth, 3 * depth), jnp.bfloat16),
            pltpu.VMEM((width, depth), jnp.float32),
            pltpu.VMEM((depth, width), jnp.float32),
            pltpu.VMEM((3, seqs, blks, heads // 2, 2, EDGE, UNIT), jnp.bfloat16),
            pltpu.VMEM(sums.shape, jnp.float32),
            pltpu.VMEM((devices - 1,) + sums.shape[1:], jnp.float32),
            *reduce_scratch(6, blks, half),
            pltpu.SemaphoreType.DMA((7,)),
            pltpu.SemaphoreType.DMA((2 * group,)),
            pltpu.SemaphoreType.DMA((2 * group,)),
            pltpu.SemaphoreType.DMA((devices,)),
            pltpu.SemaphoreType.DMA((devices,)),
        ],
        compiler_params=pltpu.CompilerParams(
            collective_id=collective_id, has_side_effects=True, vmem_limit_bytes=56 * 2**20
        ),
        name="last_reduce",
    )(dkv, dq, x, w_qkv, base, sums)


def tail_segments(doc_lengths, first, rows):
    return segment_ids(doc_lengths, first + lax.iota(jnp.int32, rows))


def shards_heads(
    layer_input,
    weight_query,
    weight_key,
    weight_value,
    weight_output,
    weight_expand,
    weight_reduce,
    bias_query,
    bias_value,
    bias_output,
    bias_expand,
    bias_reduce,
    first_gain,
    first_shift,
    second_gain,
    second_shift,
    cotangent,
    doc_lengths,
):
    tok_rows, model_width = layer_input.shape[1:]
    head_count = lax.axis_size("head")
    blk_count = lax.axis_size("blk")
    count = head_count * blk_count
    seq_len = tok_rows * count
    long_rows = seq_len - seq_len // blk_count // 2
    flat_rows = layer_input.reshape(tok_rows, model_width)

    vectors = (
        bias_query,
        bias_value,
        bias_output,
        bias_reduce,
        first_gain,
        first_shift,
        second_gain,
        second_shift,
        bias_expand,
    )
    sizes = [vector.shape[0] for vector in vectors]
    lane = 128
    spare = 16 * lane - sum(sizes)
    packed = jnp.concatenate(vectors + (jnp.zeros((spare,), layer_input.dtype),))
    w_qkv, *wholes, packed = first_gather(
        weight_query,
        weight_key,
        weight_value,
        (weight_output, weight_expand, weight_reduce),
        packed.reshape(16, lane),
        4,
    )
    w_qkv = w_qkv.reshape(model_width, 3 * model_width)
    packed = packed.reshape(-1, 16 * lane).astype(jnp.float32)
    whole, start = [], 0
    for size in sizes:
        whole.append(packed[:, start : start + size].reshape(-1))
        start += size
    b_query, b_value, b_output, b_reduce, gain_one, shift_one, gain_two, shift_two, b_expand = whole

    b_qkv = jnp.concatenate((b_query, jnp.zeros_like(b_query), b_value))
    qkv = lax.dot_general(
        w_qkv, flat_rows, (((0,), (1,)), ((), ())), preferred_element_type=jnp.float32
    )
    qkv = (qkv + b_qkv[:, None]).astype(jnp.bfloat16).reshape(3, HEADS, HEAD_DIM, tok_rows)
    seg = tail_segments(doc_lengths, long_rows, seq_len - long_rows)[0]
    probs, tail_probs, attn, inv_total, kept, attn_flat, w_output, w_expand, w_reduce = attn_fwd(
        qkv, seg, long_rows, wholes, 5
    )
    attn_flat = attn_flat.reshape(model_width, tok_rows)
    w_output = w_output.reshape(-1, weight_output.shape[1])
    w_expand = w_expand.reshape(-1, weight_expand.shape[1])
    w_reduce = w_reduce.reshape(-1, weight_reduce.shape[1])

    resid_one = flat_rows.astype(jnp.float32) + left_dot(attn_flat, w_output) + b_output
    normed_one, norm_one_pull = jax.vjp(layer_norm, resid_one, gain_one, shift_one)
    normed_low = normed_one.astype(jnp.bfloat16)
    pre_act = plain_dot(normed_low, w_expand) + b_expand
    hidden_f32, gelu_pull = jax.vjp(gelu_curve, pre_act)
    hidden = hidden_f32.astype(jnp.bfloat16)
    resid_two = normed_one + plain_dot(hidden, w_reduce) + b_reduce
    result, norm_two_pull = jax.vjp(layer_norm, resid_two, gain_two, shift_two)
    layer_output = result.astype(jnp.bfloat16).reshape(layer_input.shape)
    tok_first = (lax.axis_index("blk") * head_count + lax.axis_index("head")) * tok_rows
    tok_seg = segment_ids(doc_lengths, tok_first + lax.iota(jnp.int32, tok_rows))
    live = (tok_seg > 0).astype(jnp.float32)
    grad_out = (cotangent.astype(jnp.float32) * live[..., None]).reshape(-1, model_width)
    grad_resid_two, grad_gain_two, grad_shift_two = norm_two_pull(grad_out)
    grad_ffn = grad_resid_two.astype(jnp.bfloat16)
    grad_w_reduce = left_dot(hidden, grad_ffn)
    grad_b_reduce = jnp.sum(grad_ffn.astype(jnp.float32), axis=0)
    (grad_pre,) = gelu_pull(right_dot(grad_ffn, w_reduce))
    grad_pre = grad_pre.astype(jnp.bfloat16)
    grad_w_expand = left_dot(normed_low, grad_pre)
    grad_b_expand = jnp.sum(grad_pre.astype(jnp.float32), axis=0)
    grad_normed = grad_resid_two + right_dot(grad_pre, w_expand)
    grad_resid_one, grad_gain_one, grad_shift_one = norm_one_pull(grad_normed)
    grad_branch = grad_resid_one.astype(jnp.bfloat16)
    grad_w_output = plain_dot(attn_flat, grad_branch)
    grad_b_output = jnp.sum(grad_branch.astype(jnp.float32), axis=0)
    grad_attn = right_dot(w_output, grad_branch).astype(jnp.bfloat16)
    grad_attn = grad_attn.reshape(HEADS, HEAD_DIM, tok_rows)

    grad_kv, grad_query, grad_w_output, grad_w_expand, grad_w_reduce = attn_bwd(
        probs,
        tail_probs,
        kept,
        attn,
        inv_total,
        grad_attn,
        long_rows,
        [grad.astype(jnp.bfloat16) for grad in (grad_w_output, grad_w_expand, grad_w_reduce)],
        6,
    )

    sums = (
        jnp.zeros_like(b_query),
        jnp.zeros_like(b_value),
        grad_b_output,
        grad_b_reduce,
        grad_gain_one,
        grad_shift_one,
        grad_gain_two,
        grad_shift_two,
        grad_b_expand,
    )
    sums = jnp.concatenate([term.reshape(-1, size) for term, size in zip(sums, sizes)], axis=1)
    sums = jnp.pad(sums, ((0, 0), (0, 8 * lane - sums.shape[1]))).reshape(-1, 8, lane)
    grad_w_qkv, grad_input, sums = last_reduce(
        grad_kv, grad_query, flat_rows, w_qkv, grad_resid_one, sums, 7
    )
    owner = (lax.axis_index("seq") * blk_count + lax.axis_index("blk")) * head_count
    owner = owner + lax.axis_index("head")
    within = lax.rem(owner, lane // sizes[0]) * sizes[0]
    g_query = lax.dynamic_slice_in_dim(sums[3], within, sizes[0])
    g_value = lax.dynamic_slice_in_dim(sums[4], within, sizes[1])
    sums = sums.reshape(-1)
    parts, start = [], 0
    for size in sizes:
        parts.append(sums[start : start + size])
        start += size
    g_output, g_reduce, g_gain_one, g_shift_one, g_gain_two, g_shift_two, g_expand = parts[2:]
    return (
        layer_output,
        grad_input.reshape(layer_input.shape),
        grad_w_qkv[:, :model_width],
        grad_w_qkv[:, model_width : 2 * model_width],
        grad_w_qkv[:, 2 * model_width :],
        grad_w_output,
        grad_w_expand,
        grad_w_reduce,
        g_query,
        g_value,
        g_output,
        g_expand,
        g_reduce,
        g_gain_one,
        g_shift_one,
        g_gain_two,
        g_shift_two,
    )


def solution(mesh):
    placed = (
        P("seq", ("blk", "head"), None),
        P(("seq", "blk", "head"), None),
        P(("seq", "blk", "head"), None),
        P(("seq", "blk", "head"), None),
        P(("seq", "blk", "head"), None),
        P(("seq", "blk", "head"), None),
        P(("seq", "blk", "head"), None),
        P(("seq", "blk", "head")),
        P(("seq", "blk", "head")),
        P(("seq", "blk", "head")),
        P(("seq", "blk", "head")),
        P(("seq", "blk", "head")),
        P(("seq", "blk", "head")),
        P(("seq", "blk", "head")),
        P(("seq", "blk", "head")),
        P(("seq", "blk", "head")),
        P("seq", ("blk", "head"), None),
        P("seq", None),
    )
    group = mesh.shape["blk"] * mesh.shape["head"]
    body = shards_heads if group == HEADS else shards_general
    return jax.shard_map(
        body,
        mesh=mesh,
        in_specs=placed,
        out_specs=(
            P("seq", ("blk", "head"), None),
            P("seq", ("blk", "head"), None),
            P(("seq", "blk", "head"), None),
            P(("seq", "blk", "head"), None),
            P(("seq", "blk", "head"), None),
            P(("seq", "blk", "head"), None),
            P(("seq", "blk", "head"), None),
            P(("seq", "blk", "head"), None),
            P(("seq", "blk", "head")),
            P(("seq", "blk", "head")),
            P(("seq", "blk", "head")),
            P(("seq", "blk", "head")),
            P(("seq", "blk", "head")),
            P(("seq", "blk", "head")),
            P(("seq", "blk", "head")),
            P(("seq", "blk", "head")),
            P(("seq", "blk", "head")),
        ),
        check_vma=False,
    )
```

```python
import functools
import math

import jax
import jax.numpy as jnp
from jax import lax
from jax.experimental import pallas as pl
from jax.experimental.pallas import tpu as pltpu
from jax.sharding import PartitionSpec as P

HEADS = 16
HEAD_DIM = 64


NORM_EPS = 1e-05
INV_ROOT2 = 0.7071067811865476


def segment_ids(doc_lengths, positions):
    ends = jnp.cumsum(doc_lengths, axis=-1)
    counted = jnp.sum((ends[:, None, :] <= positions[None, :, None]).astype(jnp.int32), axis=-1)
    return jnp.where(positions[None, :] < ends[:, -1:], counted + 1, 0)


def layer_norm(values, gain, shift):
    center = values - jnp.mean(values, axis=-1, keepdims=True)
    spread = jnp.mean(center * center, axis=-1, keepdims=True)
    return center * lax.rsqrt(spread + NORM_EPS) * gain + shift


def gelu_curve(values):
    return 0.5 * values * (1.0 + lax.erf(values * INV_ROOT2))


def plain_dot(left, right):
    return jnp.dot(left, right, preferred_element_type=jnp.float32)


def left_dot(left, right):
    return lax.dot_general(
        left, right, (((0,), (0,)), ((), ())), preferred_element_type=jnp.float32
    )


def right_dot(left, right):
    return lax.dot_general(
        left, right, (((1,), (1,)), ((), ())), preferred_element_type=jnp.float32
    )


def score_grads(scores, allowed, grad_part, value_part, lse_part, delta_part):
    probs = jnp.where(allowed, jnp.exp(scores - lse_part[..., None]), 0.0)
    grad_probs = jnp.einsum(
        "sqhd,skhd->shqk", grad_part, value_part, preferred_element_type=jnp.float32
    )
    grad_scores = (probs * (grad_probs - delta_part[..., None])).astype(jnp.bfloat16)
    return (probs, grad_scores)


def shards_general(
    layer_input,
    weight_query,
    weight_key,
    weight_value,
    weight_output,
    weight_expand,
    weight_reduce,
    bias_query,
    bias_value,
    bias_output,
    bias_expand,
    bias_reduce,
    first_gain,
    first_shift,
    second_gain,
    second_shift,
    cotangent,
    doc_lengths,
):
    seq_count, tok_rows, model_width = layer_input.shape
    head_count = lax.axis_size("head")
    blk_count = lax.axis_size("blk")
    heads_here = HEADS // head_count
    score_scale = HEAD_DIM ** (-0.5)
    gathered = (
        lax.all_gather(weight_query, ("seq", "blk", "head"), axis=0, tiled=True),
        lax.all_gather(weight_key, ("seq", "blk", "head"), axis=0, tiled=True),
        lax.all_gather(weight_value, ("seq", "blk", "head"), axis=0, tiled=True),
        lax.all_gather(weight_output, ("seq", "blk", "head"), axis=0, tiled=True),
        lax.all_gather(weight_expand, ("seq", "blk", "head"), axis=0, tiled=True),
        lax.all_gather(weight_reduce, ("seq", "blk", "head"), axis=0, tiled=True),
        lax.all_gather(bias_query, ("seq", "blk", "head"), axis=0, tiled=True),
        lax.all_gather(bias_value, ("seq", "blk", "head"), axis=0, tiled=True),
        lax.all_gather(bias_output, ("seq", "blk", "head"), axis=0, tiled=True),
        lax.all_gather(bias_expand, ("seq", "blk", "head"), axis=0, tiled=True),
        lax.all_gather(bias_reduce, ("seq", "blk", "head"), axis=0, tiled=True),
        lax.all_gather(first_gain, ("seq", "blk", "head"), axis=0, tiled=True),
        lax.all_gather(first_shift, ("seq", "blk", "head"), axis=0, tiled=True),
        lax.all_gather(second_gain, ("seq", "blk", "head"), axis=0, tiled=True),
        lax.all_gather(second_shift, ("seq", "blk", "head"), axis=0, tiled=True),
    )
    w_query, w_key, w_value, w_output, w_expand, w_reduce = gathered[:6]
    b_query, b_value, b_output, b_expand, b_reduce, gain_one, shift_one, gain_two, shift_two = [
        vector.astype(jnp.float32) for vector in gathered[6:]
    ]
    flat_rows = layer_input.reshape(-1, model_width)
    queries = (
        (plain_dot(flat_rows, w_query) + b_query).astype(jnp.bfloat16).reshape(layer_input.shape)
    )
    key_rows = plain_dot(flat_rows, w_key).astype(jnp.bfloat16).reshape(layer_input.shape)
    value_rows = (
        (plain_dot(flat_rows, w_value) + b_value).astype(jnp.bfloat16).reshape(layer_input.shape)
    )
    query_heads, key_heads, value_heads = (
        lax.all_to_all(queries, "head", split_axis=2, concat_axis=1, tiled=True),
        lax.all_to_all(key_rows, "head", split_axis=2, concat_axis=1, tiled=True),
        lax.all_to_all(value_rows, "head", split_axis=2, concat_axis=1, tiled=True),
    )
    block_rows = query_heads.shape[1]
    block_first = lax.axis_index("blk") * block_rows
    query_seg = segment_ids(doc_lengths, block_first + lax.iota(jnp.int32, block_rows))
    query_split = query_heads.reshape(seq_count, block_rows, heads_here, HEAD_DIM)

    def key_block(shard_piece, block_index, block_width):
        key_offset = block_index * block_width
        key_part = lax.dynamic_slice_in_dim(shard_piece[0], key_offset, block_width, 1).reshape(
            seq_count, block_width, heads_here, HEAD_DIM
        )
        value_part = lax.dynamic_slice_in_dim(shard_piece[1], key_offset, block_width, 1).reshape(
            seq_count, block_width, heads_here, HEAD_DIM
        )
        key_seg = segment_ids(doc_lengths, key_offset + lax.iota(jnp.int32, block_width))
        allowed = query_seg[:, None, :, None] == key_seg[:, None, None, :]
        scores = (
            jnp.einsum("sqhd,skhd->shqk", query_split, key_part, preferred_element_type=jnp.float32)
            * score_scale
        )
        return (key_offset, key_part, value_part, allowed, scores)

    stat_shape = (seq_count, heads_here, block_rows)
    start_state = (
        jnp.full(stat_shape, -1e30, jnp.float32),
        jnp.zeros(stat_shape, jnp.float32),
        jnp.zeros(stat_shape + (HEAD_DIM,), jnp.float32),
    )
    shard_piece = (
        lax.all_gather(key_heads, "blk", axis=1, tiled=True),
        lax.all_gather(value_heads, "blk", axis=1, tiled=True),
    )
    piece_rows = shard_piece[0].shape[1]
    block_width = math.gcd(piece_rows, 512)

    def advance(block_index, loop_state):
        running_max, row_total, accum = loop_state
        key_offset, key_part, value_part, allowed, scores = key_block(
            shard_piece, block_index, block_width
        )
        scores = jnp.where(allowed, scores, -1e30)
        new_max = jnp.maximum(running_max, jnp.max(scores, axis=-1))
        rescale = jnp.exp(running_max - new_max)
        weights = jnp.where(allowed, jnp.exp(scores - new_max[..., None]), 0.0)
        row_total = row_total * rescale + jnp.sum(weights, axis=-1)
        accum = accum * rescale[..., None] + jnp.einsum(
            "shqk,skhd->shqd",
            weights.astype(jnp.bfloat16),
            value_part,
            preferred_element_type=jnp.float32,
        )
        return (new_max, row_total, accum)

    running_max, row_total, accum = lax.fori_loop(
        0, piece_rows // block_width, advance, start_state
    )
    log_total = running_max + jnp.log(row_total)
    attn_heads = accum / row_total[..., None]
    attn_send = (
        attn_heads.transpose(0, 2, 1, 3)
        .reshape(seq_count, block_rows, heads_here * HEAD_DIM)
        .astype(jnp.bfloat16)
    )
    attn_tokens = lax.all_to_all(attn_send, "head", split_axis=1, concat_axis=2, tiled=True)
    attn_flat = attn_tokens.reshape(-1, model_width)
    resid_one = flat_rows.astype(jnp.float32) + plain_dot(attn_flat, w_output) + b_output
    normed_one, norm_one_pull = jax.vjp(layer_norm, resid_one, gain_one, shift_one)
    normed_low = normed_one.astype(jnp.bfloat16)
    pre_act = plain_dot(normed_low, w_expand) + b_expand
    hidden_f32, gelu_pull = jax.vjp(gelu_curve, pre_act)
    hidden = hidden_f32.astype(jnp.bfloat16)
    resid_two = normed_one + plain_dot(hidden, w_reduce) + b_reduce
    result, norm_two_pull = jax.vjp(layer_norm, resid_two, gain_two, shift_two)
    layer_output = result.astype(jnp.bfloat16).reshape(layer_input.shape)
    tok_first = (lax.axis_index("blk") * head_count + lax.axis_index("head")) * tok_rows
    tok_seg = segment_ids(doc_lengths, tok_first + lax.iota(jnp.int32, tok_rows))
    live = (tok_seg > 0).astype(jnp.float32)
    grad_out = (cotangent.astype(jnp.float32) * live[..., None]).reshape(-1, model_width)
    grad_resid_two, grad_gain_two, grad_shift_two = norm_two_pull(grad_out)
    grad_ffn = grad_resid_two.astype(jnp.bfloat16)
    grad_w_reduce = left_dot(hidden, grad_ffn)
    grad_b_reduce = jnp.sum(grad_ffn.astype(jnp.float32), axis=0)
    (grad_pre,) = gelu_pull(right_dot(grad_ffn, w_reduce))
    grad_pre = grad_pre.astype(jnp.bfloat16)
    grad_w_expand = left_dot(normed_low, grad_pre)
    grad_b_expand = jnp.sum(grad_pre.astype(jnp.float32), axis=0)
    grad_normed = grad_resid_two + right_dot(grad_pre, w_expand)
    grad_resid_one, grad_gain_one, grad_shift_one = norm_one_pull(grad_normed)
    grad_branch = grad_resid_one.astype(jnp.bfloat16)
    grad_w_output = left_dot(attn_flat, grad_branch)
    grad_b_output = jnp.sum(grad_branch.astype(jnp.float32), axis=0)
    grad_attn = right_dot(grad_branch, w_output).astype(jnp.bfloat16).reshape(layer_input.shape)
    grad_attn_heads = lax.all_to_all(grad_attn, "head", split_axis=2, concat_axis=1, tiled=True)
    grad_attn_split = grad_attn_heads.reshape(seq_count, block_rows, heads_here, HEAD_DIM)
    row_delta = jnp.einsum("sqhd,shqd->shq", grad_attn_split.astype(jnp.float32), attn_heads)
    full_rows = blk_count * block_rows
    query_zero = jnp.zeros((seq_count, block_rows, heads_here, HEAD_DIM), jnp.float32)
    back_state = (
        query_zero,
        jnp.zeros((seq_count, full_rows, heads_here * HEAD_DIM), jnp.float32),
        jnp.zeros((seq_count, full_rows, heads_here * HEAD_DIM), jnp.float32),
    )
    fold_shard_piece = (
        lax.all_gather(key_heads, "blk", axis=1, tiled=True),
        lax.all_gather(value_heads, "blk", axis=1, tiled=True),
    )
    piece_rows = fold_shard_piece[0].shape[1]
    fold_block_width = math.gcd(piece_rows, 512)

    def advance(block_index, loop_state):
        grad_query, grad_keys, grad_values = loop_state
        key_offset, key_part, value_part, allowed, scores = key_block(
            fold_shard_piece, block_index, fold_block_width
        )
        probs, grad_scores = score_grads(
            scores, allowed, grad_attn_split, value_part, log_total, row_delta
        )
        grad_query = (
            grad_query
            + jnp.einsum(
                "shqk,skhd->sqhd", grad_scores, key_part, preferred_element_type=jnp.float32
            )
            * score_scale
        )
        key_term = (
            jnp.einsum(
                "shqk,sqhd->skhd", grad_scores, query_split, preferred_element_type=jnp.float32
            )
            * score_scale
        )
        value_term = jnp.einsum(
            "shqk,sqhd->skhd",
            probs.astype(jnp.bfloat16),
            grad_attn_split,
            preferred_element_type=jnp.float32,
        )
        grad_keys = lax.dynamic_update_slice_in_dim(
            grad_keys,
            key_term.reshape(seq_count, fold_block_width, heads_here * HEAD_DIM),
            key_offset,
            1,
        )
        grad_values = lax.dynamic_update_slice_in_dim(
            grad_values,
            value_term.reshape(seq_count, fold_block_width, heads_here * HEAD_DIM),
            key_offset,
            1,
        )
        return (grad_query, grad_keys, grad_values)

    back_out = lax.fori_loop(0, piece_rows // fold_block_width, advance, back_state)
    grad_query = back_out[0]
    key_share, value_share = (
        lax.psum_scatter(
            back_out[1].astype(jnp.bfloat16), "blk", scatter_dimension=1, tiled=True
        ).astype(jnp.float32),
        lax.psum_scatter(
            back_out[2].astype(jnp.bfloat16), "blk", scatter_dimension=1, tiled=True
        ).astype(jnp.float32),
    )
    query_send = grad_query.reshape(seq_count, block_rows, heads_here * HEAD_DIM).astype(
        jnp.bfloat16
    )
    query_back, key_back, value_back = (
        lax.all_to_all(query_send, "head", split_axis=1, concat_axis=2, tiled=True),
        lax.all_to_all(
            key_share.astype(jnp.bfloat16), "head", split_axis=1, concat_axis=2, tiled=True
        ),
        lax.all_to_all(
            value_share.astype(jnp.bfloat16), "head", split_axis=1, concat_axis=2, tiled=True
        ),
    )
    query_back = query_back.reshape(-1, model_width)
    key_back = key_back.reshape(-1, model_width)
    value_back = value_back.reshape(-1, model_width)
    grad_w_query = left_dot(flat_rows, query_back)
    grad_w_key = left_dot(flat_rows, key_back)
    grad_w_value = left_dot(flat_rows, value_back)
    grad_b_query = jnp.sum(query_back.astype(jnp.float32), axis=0)
    grad_b_value = jnp.sum(value_back.astype(jnp.float32), axis=0)
    grad_input = (
        grad_resid_one
        + right_dot(query_back, w_query)
        + right_dot(key_back, w_key)
        + right_dot(value_back, w_value)
    )
    grad_input = grad_input.reshape(layer_input.shape)
    shares_all = (
        lax.psum_scatter(grad_w_query, ("seq", "blk", "head"), scatter_dimension=0, tiled=True),
        lax.psum_scatter(grad_w_key, ("seq", "blk", "head"), scatter_dimension=0, tiled=True),
        lax.psum_scatter(grad_w_value, ("seq", "blk", "head"), scatter_dimension=0, tiled=True),
        lax.psum_scatter(grad_w_output, ("seq", "blk", "head"), scatter_dimension=0, tiled=True),
        lax.psum_scatter(grad_w_expand, ("seq", "blk", "head"), scatter_dimension=0, tiled=True),
        lax.psum_scatter(grad_w_reduce, ("seq", "blk", "head"), scatter_dimension=0, tiled=True),
        lax.psum_scatter(grad_b_query, ("seq", "blk", "head"), scatter_dimension=0, tiled=True),
        lax.psum_scatter(grad_b_value, ("seq", "blk", "head"), scatter_dimension=0, tiled=True),
        lax.psum_scatter(grad_b_output, ("seq", "blk", "head"), scatter_dimension=0, tiled=True),
        lax.psum_scatter(grad_b_expand, ("seq", "blk", "head"), scatter_dimension=0, tiled=True),
        lax.psum_scatter(grad_b_reduce, ("seq", "blk", "head"), scatter_dimension=0, tiled=True),
        lax.psum_scatter(grad_gain_one, ("seq", "blk", "head"), scatter_dimension=0, tiled=True),
        lax.psum_scatter(grad_shift_one, ("seq", "blk", "head"), scatter_dimension=0, tiled=True),
        lax.psum_scatter(grad_gain_two, ("seq", "blk", "head"), scatter_dimension=0, tiled=True),
        lax.psum_scatter(grad_shift_two, ("seq", "blk", "head"), scatter_dimension=0, tiled=True),
    )
    return (
        layer_output,
        grad_input,
        shares_all[0],
        shares_all[1],
        shares_all[2],
        shares_all[3],
        shares_all[4],
        shares_all[5],
        shares_all[6],
        shares_all[7],
        shares_all[8],
        shares_all[9],
        shares_all[10],
        shares_all[11],
        shares_all[12],
        shares_all[13],
        shares_all[14],
    )


MESH = pl.DeviceIdType.MESH
EVERY = ("seq", "blk", "head")
EDGE = 32
UNIT = 1024


class Place:
    def __init__(self, blks):
        self.blks = blks
        self.x = lax.axis_index("seq")
        self.z = lax.axis_index("blk")
        lane = lax.axis_index("head")
        self.y = lane // 2
        self.c = lax.rem(lane, 2)
        self.index = self.z * 4 + lane
        self.group = blks * 4

    def peer(self, step):
        index = lax.rem(self.index + step, self.group)
        return index, self.member(index)

    def member(self, index):
        return {"seq": self.x, "blk": index // 4, "head": lax.rem(index, 4)}

    def at(self, x=None, z=None, y=None, c=None):
        x = self.x if x is None else x
        z = self.z if z is None else z
        y = self.y if y is None else y
        c = self.c if c is None else c
        return {"seq": x, "blk": z, "head": y * 2 + c}

    def column(self):
        return [lax.rem(self.z + step, self.blks) for step in range(1, self.blks)]

    def near(self):
        return [self.at(z=z) for z in self.column()] + [
            self.at(x=1 - self.x),
            self.at(y=1 - self.y),
            self.at(c=1 - self.c),
        ]

    def others(self, devices):
        own = (self.x * self.blks + self.z) * 4 + self.y * 2 + self.c
        found = []
        for step in range(1, devices):
            index = lax.rem(own + step, devices)
            found.append(
                {
                    "seq": index // (self.blks * 4),
                    "blk": lax.rem(index // 4, self.blks),
                    "head": lax.rem(index, 4),
                }
            )
        return own, found


def greet(devices):
    barrier = pltpu.get_barrier_semaphore()
    for device in devices:
        pl.semaphore_signal(barrier, inc=1, device_id=device, device_id_type=MESH)
    pl.semaphore_wait(barrier, len(devices))


class Wires:
    def __init__(self, send, recv):
        self.send, self.recv, self.used = send, recv, 0

    def copy(self, source, target, device):
        slot = self.used
        self.used += 1
        return pltpu.make_async_remote_copy(
            src_ref=source,
            dst_ref=target,
            send_sem=self.send.at[slot],
            recv_sem=self.recv.at[slot],
            device_id=device,
            device_id_type=MESH,
        )


def view(ref, index, piece):
    rows, cols = piece
    return ref.at[tuple(index) + (pl.ds(*rows), pl.ds(*cols))]


ALL = slice(None)


def share_line(me, wires, ref, piece, source=None):
    own = view(ref, (me.x, me.z, me.y, me.c), piece)
    source = own if source is None else source
    return [wires.copy(source, own, me.at(z=peer)) for peer in me.column()]


class Gather:
    WIRES = 7

    def __init__(self, me, wires, ref, piece, turned, ready=False, source=None):
        x, z, y, c = me.x, me.z, me.y, me.c
        self.first = [] if ready else share_line(me, wires, ref, piece, source)
        line = view(ref, (x, ALL, y, c), piece)
        if turned:
            half, rest = view(ref, (ALL, ALL, y, c), piece), view(ref, (ALL, ALL, 1 - y, c), piece)
            self.second = wires.copy(line, line, me.at(x=1 - x))
            self.third = wires.copy(half, half, me.at(y=1 - y))
        else:
            half, rest = view(ref, (x, ALL, ALL, c), piece), view(ref, (1 - x, ALL, ALL, c), piece)
            self.second = wires.copy(line, line, me.at(y=1 - y))
            self.third = wires.copy(half, half, me.at(x=1 - x))
        self.near = wires.copy(half, half, me.at(c=1 - c))
        self.far = wires.copy(rest, rest, me.at(c=1 - c))

    def stage(self, index):
        if index == 0:
            for copy in self.first:
                copy.start()
        elif index == 1:
            for copy in self.first:
                copy.wait_recv()
            self.second.start()
        elif index == 2:
            self.second.wait_recv()
            self.third.start()
            self.near.start()
        elif index == 3:
            self.third.wait_recv()
            self.far.start()
        else:
            self.near.wait_recv()
            self.far.wait_recv()
            for copy in (*self.first, self.second, self.third, self.near, self.far):
                copy.wait_send()


class Relay(Gather):
    WIRES = 7

    def __init__(self, me, wires, ref, piece, turned, source):
        super().__init__(me, wires, ref, piece, turned, ready=True)
        x, z, y, c = me.x, me.z, me.y, me.c
        own = view(ref, (x, z, y, c), piece)
        beside = me.at(z=z + 1 - 2 * lax.rem(z, 2))
        pair = view(ref, (x, pl.ds(z // 2 * 2, 2), y, c), piece)
        other = view(ref, (x, pl.ds(2 - z // 2 * 2, 2), y, c), piece)
        self.inner = (z == 1) | (z == 2)
        self.own = wires.copy(source, own, beside)
        self.cross = wires.copy(pair, pair, me.at(z=lax.rem(3 - z, 4)))
        self.outward = wires.copy(other, other, beside)

    def stage(self, index):
        if index == 0:
            self.own.start()
        elif index == 1:
            self.own.wait_recv()

            @pl.when(self.inner)
            def _():
                self.cross.start()

        elif index == 2:

            @pl.when(self.inner)
            def _():
                self.cross.wait_recv()
                self.outward.start()

        elif index == 3:

            @pl.when(jnp.logical_not(self.inner))
            def _():
                self.outward.wait_recv()

            super().stage(1)
        elif index < 6:
            super().stage(index - 2)
        else:

            @pl.when(self.inner)
            def _():
                self.cross.wait_send()
                self.outward.wait_send()

            self.own.wait_send()
            super().stage(4)


class Reduce:
    WIRES = 6

    def __init__(self, me, wires, ref, piece, turned, own, own_sem, r0, r1, r2, r3, out, out_piece):
        x, z, y, c = me.x, me.z, me.y, me.c
        self.place, self.turned, self.out, self.out_piece = me, turned, out, out_piece
        self.r0, self.r1, self.r2, self.r3 = r0, r1, r2, r3
        if own is None:
            self.load = None
            self.own = lambda at: ref[at + (c, pl.ds(*piece[0]), pl.ds(*piece[1]))]
        else:
            self.load = pltpu.make_async_copy(view(ref, (ALL, ALL, ALL, c), piece), own, own_sem)
            self.own = lambda at: own[at]
        self.zero = wires.copy(view(ref, (ALL, ALL, ALL, 1 - c), piece), r0, me.at(c=1 - c))
        if turned:
            self.one = wires.copy(r0.at[:, :, 1 - y], r1, me.at(y=1 - y))
            self.two = wires.copy(r0.at[1 - x, :, y], r2, me.at(x=1 - x))
        else:
            self.one = wires.copy(r0.at[1 - x], r1, me.at(x=1 - x))
            self.two = wires.copy(r0.at[x, :, 1 - y], r2, me.at(y=1 - y))
        self.three = [
            wires.copy(r0.at[x, peer, y], r3.at[slot], me.at(z=peer))
            for slot, peer in enumerate(me.column())
        ]

    def stage(self, index):
        x, z, y = self.place.x, self.place.z, self.place.y
        blks = self.place.blks
        r0 = self.r0

        def add(target, term):
            total = r0[target].astype(jnp.float32) + term.astype(jnp.float32)
            r0[target] = total.astype(r0.dtype)

        if index == 0:
            self.zero.start()
        elif index == 1:
            self.load.start()
        elif index == 2:
            if self.load is not None:
                self.load.wait()
            self.zero.wait_recv()

            @pl.loop(0, 4 * blks)
            def _(i):
                at = (i // (2 * blks), lax.rem(i // 2, blks), lax.rem(i, 2))
                add(at, self.own(at))

            self.one.start()
        elif index == 3:
            self.one.wait_recv()

            @pl.loop(0, 2 * blks)
            def _(i):
                if self.turned:
                    a, b = i // blks, lax.rem(i, blks)
                    add((a, b, y), self.r1[a, b])
                else:
                    a, b = i // 2, lax.rem(i, 2)
                    add((x, a, b), self.r1[a, b])

            self.two.start()
        elif index == 4:
            self.two.wait_recv()

            @pl.loop(0, blks)
            def _(i):
                add((x, i, y), self.r2[i])

            for copy in self.three:
                copy.start()
        else:
            for copy in self.three:
                copy.wait_recv()
            total = r0[x, z, y].astype(jnp.float32)
            for slot in range(blks - 1):
                total = total + self.r3[slot].astype(jnp.float32)
            rows, cols = self.out_piece
            self.out[rows[0] : rows[0] + rows[1], cols[0] : cols[0] + cols[1]] = total
            for copy in (self.zero, self.one, self.two, *self.three):
                copy.wait_send()


def reduce_scratch(units, blks, cols=UNIT, dtype=jnp.bfloat16):
    turned = units // 2
    return [
        pltpu.VMEM((units, 2, blks, 2, EDGE, cols), dtype),
        pltpu.VMEM((units - turned, blks, 2, EDGE, cols), dtype),
        pltpu.VMEM((turned, 2, blks, EDGE, cols), dtype),
        pltpu.VMEM((units, blks, EDGE, cols), dtype),
        pltpu.VMEM((units, blks - 1, EDGE, cols), dtype),
        pltpu.SemaphoreType.DMA((Reduce.WIRES * units,)),
        pltpu.SemaphoreType.DMA((Reduce.WIRES * units,)),
    ]


def weight_units(edges):
    columns = []
    for which, (rows, cols) in enumerate(edges):
        columns.append(
            [
                (which, ((row, EDGE), (col, UNIT)))
                for row in range(0, rows, EDGE)
                for col in range(0, cols, UNIT)
            ]
        )
    most = max(len(column) for column in columns)
    return [column[place] for place in range(most) for column in columns if place < len(column)]


LOG2E = 1.4426950408889634
BY_LAST = (((1,), (1,)), ((), ()))


def lanes(ref, lead, first, width):
    return ref.at[tuple(lead) + (pl.ds(pl.multiple_of(first, width), width),)]


def wire(source, target, send_sem, recv_sem, device):
    return pltpu.make_async_remote_copy(
        src_ref=source,
        dst_ref=target,
        send_sem=send_sem,
        recv_sem=recv_sem,
        device_id=device,
        device_id_type=MESH,
    )


def TURNED(number):
    return number % 2 == 1


def SCHEDULE(number):
    if number < 2:
        return (-2, -1, -0.9, -0.8, 1)
    begin = (number - 2) // 2
    return (begin, begin + 1, begin + 2, begin + 4, begin + 7)


def attn_fwd_kernel(
    blks, rows, cols, count, *refs
):
    x_ref, vec_ref, down_ref, across_ref, wq, wk, wv = refs[:7]
    shares, refs = refs[7 : 7 + count], refs[7 + count :]
    p_ref, tail_ref, o_ref, inv_ref, kept_ref, tokens_ref, qkv_out, vec_out = refs[:8]
    wholes, refs = refs[8 : 8 + count], refs[8 + count :]
    (
    weights, vecs, qkv_ref, land, keys, values, s0, s1, m0, m1,
    own_sem, kv_send, kv_recv, q_send, q_recv, o_send, o_recv, send, recv,
    ) = refs
    step, steps = pl.program_id(0), pl.num_programs(0)
    length, long = land.shape[2], p_ref.shape[1]
    width = 2 * rows
    tail, chunks = length - long, long // cols
    main = long // width
    scale = LOG2E * HEAD_DIM**-0.5

    me = Place(blks)
    group = me.group

    def block_at(turn):
        return lax.rem(lax.rem(me.index, main) + turn, main)

    def ahead(block):
        return lax.rem(block + group - me.index, group)

    swaps = [[], [], []]
    for tensor, send_sem, recv_sem in ((0, q_send, q_recv), (1, kv_send, kv_recv), (2, kv_send, kv_recv)):
        for ahead_by in range(1, group):
            peer, device = me.peer(group - ahead_by)
            slot = ahead_by + (group if tensor == 2 else 0)
            swaps[tensor].append(
                wire(
                    qkv_ref.at[tensor, peer],
                    lanes(land, (tensor, ALL), me.index * width, width),
                    send_sem.at[slot],
                    recv_sem.at[slot],
                    device,
                )
            )
    keep = pltpu.make_async_copy(land, kept_ref, own_sem.at[1])

    def await_queries(block):
        @pl.when(block != me.index)
        def _():
            wire(
                qkv_ref.at[0, block],
                lanes(land, (0, ALL), block * width, width),
                q_send.at[0],
                q_recv.at[ahead(block)],
                me.member(block),
            ).wait_recv()

    def send_block(block, slot, start):
        source = lanes(o_ref, (ALL,), block * width, width)
        remote = wire(
            source,
            tokens_ref.at[me.index],
            o_send.at[slot],
            o_recv.at[lax.rem(me.index + group - block, group)],
            me.member(block),
        )
        local = pltpu.make_async_copy(source, tokens_ref.at[me.index], own_sem.at[2])

        @pl.when(block != me.index)
        def _():
            if start:
                remote.start()
            else:
                remote.wait_send()

        @pl.when(block == me.index)
        def _():
            if start:
                local.start()
            else:
                local.wait()

    wires = Wires(send, recv)
    here = (me.x, me.z, me.y, me.c)
    half = UNIT // 2
    fronts = []
    for unit, ref in enumerate((wq, wk, wv)):
        for side in range(2):
            piece = ((0, EDGE), (unit * UNIT + side * half, half))
            source = ref.at[:, pl.ds(side * half, half)]
            fronts.append(Gather(me, wires, weights, piece, side == 1, source=source))
    vectors = Gather(me, wires, vecs, ((0, EDGE), (0, vecs.shape[5])), False)
    units = weight_units([share.shape for share in shares])
    plan = [
        Relay(
            me,
            wires,
            wholes[which],
            piece,
            TURNED(number),
            source=shares[which].at[pl.ds(*piece[0]), pl.ds(*piece[1])],
        )
        for number, (which, piece) in enumerate(units)
    ]
    targets = [weights.at[here + (ALL, pl.ds(unit * UNIT, UNIT))] for unit in range(3)]
    targets += [whole.at[here] for whole in wholes]
    local = [
        pltpu.make_async_copy(source, target, own_sem.at[3 + number])
        for number, (source, target) in enumerate(zip((wq, wk, wv) + tuple(shares), targets))
    ]
    keep_weights = pltpu.make_async_copy(weights, qkv_out, own_sem.at[9])
    keep_vectors = pltpu.make_async_copy(vecs, vec_out, own_sem.at[10])
    moves = {}
    for number in range(len(units)):
        for stage, at in enumerate(SCHEDULE(number), 1):
            moves.setdefault(at, []).append((plan[number], stage))

    def front(tensor, *stages):
        for stage in stages:
            for unit in fronts[2 * tensor : 2 * tensor + 2]:
                unit.stage(stage)

    def project(tensor, column):
        for first in range(0, UNIT, 256):
            taken = weights[:, :, :, :, :, tensor * UNIT + first : tensor * UNIT + first + 256]
            found = jnp.dot(
                x_ref[...], taken.reshape(UNIT, 256), preferred_element_type=jnp.float32
            ).T
            if column is not None:
                bias = vecs[...].reshape(UNIT, vecs.shape[5])[first : first + 256]
                found = found + bias[:, column : column + 1].astype(jnp.float32)
            heads = first // HEAD_DIM, (first + 256) // HEAD_DIM
            qkv_ref[tensor, heads[0] : heads[1]] = found.astype(jnp.bfloat16).reshape(
                heads[1] - heads[0], HEAD_DIM, width
            )
        own = pl.ds(pl.multiple_of(me.index * width, width), width)
        land[tensor, :, own] = qkv_ref[tensor, me.index]

    def take_queries(start):
        part = land[0, :, pl.ds(pl.multiple_of(start, rows), rows)].astype(jnp.float32) * scale
        high = part.astype(jnp.bfloat16).astype(jnp.float32)
        return jnp.concatenate([high, part - high], 0).T.astype(jnp.bfloat16)

    def score(queries, store, j, peak):
        found = jnp.dot(
            queries, keys[:, j * cols : (j + 1) * cols], preferred_element_type=jnp.float32
        )
        store[:, j * cols : (j + 1) * cols] = found
        for first in range(0, cols, 128):
            piece = found[:, first : first + 128]
            peak = piece if peak is None else jnp.maximum(peak, piece)
        return peak

    def keep_peak(store, peak):
        store[...] = jnp.broadcast_to(jnp.max(peak, axis=1, keepdims=True), store.shape)

    def weigh(store, peak, j, row, total):
        weights = jnp.exp2(store[:, j * cols : (j + 1) * cols] - peak[:, :1]).astype(jnp.bfloat16)
        p_ref[row : row + rows, j * cols : (j + 1) * cols] = weights
        term = lax.dot_general(
            values[:, j * cols : (j + 1) * cols],
            weights,
            BY_LAST,
            preferred_element_type=jnp.float32,
        )
        return term if total is None else total + term

    def finish(total, start):
        place = pl.ds(pl.multiple_of(start, rows), rows)
        inverse = 1.0 / total[HEAD_DIM : HEAD_DIM + 1]
        o_ref[:, place] = (total[:HEAD_DIM] * inverse).astype(jnp.bfloat16)
        inv_ref[:, place] = jnp.broadcast_to(inverse, (8, rows))

    @pl.when(step == 0)
    def _():
        for copy in local:
            copy.start()
        turned = jnp.concatenate(
            [vec_ref[...].astype(jnp.float32), jnp.zeros((112, 128), jnp.float32)], 0
        ).T
        vecs[here] = turned[:EDGE].astype(jnp.bfloat16)
        greet([me.peer(by)[1] for by in range(1, group)] + [me.at(x=1 - me.x)])
        vectors.stage(0)
        for tensor in (1, 2, 0):
            front(tensor, 0)
        for unit in plan:
            unit.stage(0)
        for copy in local:
            copy.wait()
        vectors.stage(1)
        front(1, 1)
        front(1, 2)
        vectors.stage(2)
        front(2, 1)
        front(1, 3)
        front(2, 2)
        vectors.stage(3)
        front(0, 1)
        front(1, 4)
        project(1, None)
        for copy in swaps[1]:
            copy.start()
        front(2, 3)
        front(0, 2)
        vectors.stage(4)
        front(2, 4)
        project(2, 1)
        for copy in swaps[2]:
            copy.start()
        front(0, 3)
        for unit, stage in moves.get(-2, []):
            unit.stage(stage)
        front(0, 4)
        keep_weights.start()
        keep_vectors.start()
        project(0, 0)
        for copy in swaps[0]:
            copy.start()
        for at in (-1, -0.9, -0.8, -0.7, -0.6):
            for unit, stage in moves.get(at, []):
                unit.stage(stage)
        for copy in swaps[1] + swaps[2]:
            copy.wait_recv()
        keys[0:HEAD_DIM, :] = land[1]
        keys[HEAD_DIM:, :] = land[1]
        values[0:HEAD_DIM, :] = land[2]
        values[HEAD_DIM:, :] = (
            (lax.broadcasted_iota(jnp.int32, (16, length), 0) == 0)
            .astype(jnp.float32)
            .astype(jnp.bfloat16)
        )
        await_queries(block_at(0))
        queries, peak = take_queries(block_at(0) * width), None
        for j in range(chunks):
            peak = score(queries, s0, j, peak)
        keep_peak(m0, peak)

    for at, todo in sorted((entry for entry in moves.items() if entry[0] >= 0), key=lambda entry: entry[0]):

        @pl.when(step == at)
        def _():
            for unit, stage in todo:
                unit.stage(stage)

    block = block_at(step)
    later = block_at(jnp.minimum(step + 1, steps - 1))

    @pl.when(step < steps - 1)
    def _():
        await_queries(later)

    for half, (old, old_peak, new, new_peak) in enumerate(((s0, m0, s1, m1), (s1, m1, s0, m0))):
        queries = take_queries(block * width + rows if half == 0 else later * width)
        total, peak = None, None
        for j in range(chunks):
            total = weigh(old, old_peak, j, half * rows, total)
            peak = score(queries, new, j, peak)
        keep_peak(new_peak, peak)
        finish(total, block * width + half * rows)
    send_block(block, step, True)

    @pl.when(step == steps - 1)
    def _():
        for number in range(tail // width):
            await_queries(main + number)
        keep.start()
        for first in range(0, tail, rows):
            queries = take_queries(long + first)
            found = jnp.dot(queries, keys[:, long:], preferred_element_type=jnp.float32)
            allowed = down_ref[first : first + rows, :1] == across_ref[:1, :]
            found = jnp.where(allowed, found, -1e30)
            peak = jnp.max(found, axis=1, keepdims=True)
            weights = jnp.exp2(found - peak).astype(jnp.bfloat16)
            tail_ref[first : first + rows, :] = weights
            total = lax.dot_general(
                values[:, long:], weights, BY_LAST, preferred_element_type=jnp.float32
            )
            finish(total, long + first)
            if (first + rows) % width == 0:
                number = main + first // width
                send_block(number, number, True)
        for unit in plan:
            unit.stage(6)
        for copy in swaps[0] + swaps[1] + swaps[2]:
            copy.wait_send()
        keep_weights.wait()
        keep_vectors.wait()
        for turn in range(main):
            send_block(block_at(turn), turn, False)
        for number in range(main, group):
            send_block(number, number, False)
        for ahead_by in range(1, group):
            source, device = me.peer(ahead_by)
            wire(
                lanes(o_ref, (ALL,), source * width, width),
                tokens_ref.at[source],
                o_send.at[0],
                o_recv.at[ahead_by],
                device,
            ).wait_recv()
        keep.wait()


def once(shape):
    return pl.BlockSpec(shape, lambda step: (0,) * len(shape), pipeline_mode=pl.Buffered(1))


def attn_fwd(x, vec, seg, fronts, shares, collective_id, cols=1024):
    seqs, blks, heads = (lax.axis_size(name) for name in EVERY)
    lead = (seqs, blks, heads // 2, 2)
    group, width = blks * heads, x.shape[0]
    rows = width // 2
    length = group * width
    tail = seg.shape[0]
    long = length - tail
    down = jnp.broadcast_to(seg[:, None], (tail, 128))
    across = jnp.broadcast_to(seg[None, :], (8, tail))
    anywhere = pl.BlockSpec(memory_space=pl.ANY)
    count = len(weight_units([share.shape for share in shares])) if shares else 0
    wires = Gather.WIRES * (count + 7)
    kept = jax.ShapeDtypeStruct((3, HEAD_DIM, length), jnp.bfloat16)
    gathered = jax.ShapeDtypeStruct(lead + (EDGE, 3 * UNIT), jnp.bfloat16)
    vectors = jax.ShapeDtypeStruct(lead + (EDGE, 128), jnp.bfloat16)
    pair = [pltpu.SemaphoreType.DMA((group,))] * 2
    return pl.pallas_call(
        functools.partial(attn_fwd_kernel, blks, rows, cols, len(shares)),
        grid=(long // width,),
        in_specs=[once(x.shape), once(vec.shape), once((tail, 128)), once((8, tail))]
        + [once(share.shape) for share in fronts + shares],
        out_specs=[
            pl.BlockSpec((width, long), lambda step: (step, 0)),
            once((tail, tail)),
            once((HEAD_DIM, length)),
            once((8, length)),
        ]
        + [anywhere] * (4 + len(shares)),
        out_shape=[
            jax.ShapeDtypeStruct((long, long), jnp.bfloat16),
            jax.ShapeDtypeStruct((tail, tail), jnp.bfloat16),
            jax.ShapeDtypeStruct((HEAD_DIM, length), jnp.bfloat16),
            jax.ShapeDtypeStruct((8, length), jnp.float32),
            kept,
            jax.ShapeDtypeStruct((group, HEAD_DIM, width), jnp.bfloat16),
            gathered,
            vectors,
        ]
        + [jax.ShapeDtypeStruct(lead + share.shape, share.dtype) for share in shares],
        scratch_shapes=[
            pltpu.VMEM(gathered.shape, gathered.dtype),
            pltpu.VMEM(vectors.shape, vectors.dtype),
            pltpu.VMEM((3, group, HEAD_DIM, width), jnp.bfloat16),
            pltpu.VMEM(kept.shape, kept.dtype),
            pltpu.VMEM((2 * HEAD_DIM, length), jnp.bfloat16),
            pltpu.VMEM((HEAD_DIM + 16, length), jnp.bfloat16),
            pltpu.VMEM((rows, long), jnp.float32),
            pltpu.VMEM((rows, long), jnp.float32),
            pltpu.VMEM((rows, 128), jnp.float32),
            pltpu.VMEM((rows, 128), jnp.float32),
            pltpu.SemaphoreType.DMA((11,)),
            pltpu.SemaphoreType.DMA((2 * group,)),
            pltpu.SemaphoreType.DMA((2 * group,)),
            *pair,
            *pair,
            pltpu.SemaphoreType.DMA((wires,)),
            pltpu.SemaphoreType.DMA((wires,)),
        ],
        compiler_params=pltpu.CompilerParams(
            collective_id=collective_id, has_side_effects=True, vmem_limit_bytes=62 * 2**20
        ),
        cost_estimate=pl.CostEstimate(
            flops=4 * long * long * HEAD_DIM,
            bytes_accessed=2 * long * long,
            transcendentals=long * long,
        ),
        name="attn_fwd",
    )(x, vec, down, across, *fronts, *shares)


def attn_bwd_kernel(
    blks, rows, cols, p_ref, tail_ref, qkv_ref, o_ref, inv_ref, grads_ref, wo, we, wr,
    dkv_ref, tokens_ref, go, ge, gr,
    land, dq_out, values, dk_sum, dv_sum, own, r0, r1a, r1b, r2, r3, send, recv,
    own_sem, do_send, do_recv, dq_send, dq_recv,
):
    step, steps = pl.program_id(0), pl.num_programs(0)
    length, long = land.shape[1], p_ref.shape[1]
    tail, chunks = length - long, long // cols
    main = long // rows
    scale = HEAD_DIM**-0.5

    me = Place(blks)
    group = me.group

    def block_at(turn):
        return lax.rem(lax.rem(me.index, main) + turn, main)

    do_copies = []
    for ahead_by in range(1, group):
        peer, device = me.peer(group - ahead_by)
        do_copies.append(
            wire(
                grads_ref.at[peer],
                lanes(land, (ALL,), me.index * rows, rows),
                do_send.at[ahead_by],
                do_recv.at[ahead_by],
                device,
            )
        )
    own_in = pltpu.make_async_copy(
        grads_ref.at[me.index], lanes(land, (ALL,), me.index * rows, rows), own_sem.at[2]
    )

    def await_grads(block):
        @pl.when(block != me.index)
        def _():
            wire(
                grads_ref.at[block],
                lanes(land, (ALL,), block * rows, rows),
                do_send.at[0],
                do_recv.at[lax.rem(block + group - me.index, group)],
                me.member(block),
            ).wait_recv()

    def send_block(block, slot, start):
        source = lanes(dq_out, (ALL,), block * rows, rows)
        remote = wire(
            source,
            tokens_ref.at[me.index],
            dq_send.at[slot],
            dq_recv.at[lax.rem(me.index + group - block, group)],
            me.member(block),
        )
        local = pltpu.make_async_copy(source, tokens_ref.at[me.index], own_sem.at[3])

        @pl.when(block != me.index)
        def _():
            if start:
                remote.start()
            else:
                remote.wait_send()

        @pl.when(block == me.index)
        def _():
            if start:
                local.start()
            else:
                local.wait()

    wires = Wires(send, recv)
    partials, totals = (wo, we, wr), (go, ge, gr)
    units = weight_units([partial.shape[4:] for partial in partials])
    plan, moves = [], {}
    for number, (which, piece) in enumerate(units):
        turned = number % 2 == 1
        unit = Reduce(
            me,
            wires,
            partials[which],
            piece,
            turned,
            own.at[number % 2],
            own_sem.at[number % 2],
            r0.at[number],
            (r1b if turned else r1a).at[number // 2],
            r2.at[number],
            r3.at[number],
            totals[which],
            piece,
        )
        plan.append(unit)
        pair = number // 2
        for stage, at in enumerate((0, pair, pair + 1, 2 * pair + 4, 2 * pair + 6)):
            moves.setdefault(min(at, main - 1), []).append((stage, number, unit))

    def prepare(start, width):
        place = pl.ds(pl.multiple_of(start, width), width)
        grads, inverse = land[:, place].astype(jnp.float32), inv_ref[:1, place]
        delta = -jnp.sum(grads * o_ref[:, place].astype(jnp.float32), axis=0, keepdims=True)
        delta = delta * inverse
        high = delta.astype(jnp.bfloat16).astype(jnp.float32)
        row = lax.broadcasted_iota(jnp.int32, (16, width), 0)
        extra = jnp.where(row == 0, high, jnp.where(row == 1, delta - high, 0.0))
        grads = grads * inverse
        wide = jnp.concatenate([grads, extra], 0).T.astype(jnp.bfloat16)
        return wide, grads.astype(jnp.bfloat16), qkv_ref[0, :, place]

    def part(wide, grads, queries, weights, keys_here, values_here, dq):
        dp = jnp.dot(wide, values_here, preferred_element_type=jnp.float32)
        ds = (weights.astype(jnp.float32) * dp).astype(jnp.bfloat16)
        dv = jnp.dot(grads, weights, preferred_element_type=jnp.float32)
        dk = jnp.dot(queries, ds, preferred_element_type=jnp.float32)
        term = lax.dot_general(keys_here, ds, BY_LAST, preferred_element_type=jnp.float32)
        return (term if dq is None else dq + term), dk, dv

    @pl.when(step == 0)
    def _():
        own_in.start()
        greet([me.peer(by)[1] for by in range(1, group)] + [me.at(x=1 - me.x)])
        for copy in do_copies:
            copy.start()

    for at, todo in sorted(moves.items()):

        @pl.when(step == at)
        def _():
            for stage, number, unit in sorted(todo, key=lambda entry: (-entry[0], entry[1])):
                unit.stage(stage)

    @pl.when(step == 0)
    def _():
        values[0:HEAD_DIM, :] = qkv_ref[2]
        values[HEAD_DIM:, :] = (
            (lax.broadcasted_iota(jnp.int32, (16, length), 0) < 2)
            .astype(jnp.float32)
            .astype(jnp.bfloat16)
        )
        dk_sum[...] = jnp.zeros_like(dk_sum)
        dv_sum[...] = jnp.zeros_like(dv_sum)
        own_in.wait()

    block = block_at(step)
    await_grads(block)
    wide, grads, queries = prepare(block * rows, rows)
    dq = None
    for j in range(chunks):
        here = slice(j * cols, (j + 1) * cols)
        dq, dk, dv = part(
            wide, grads, queries, p_ref[:, here], qkv_ref[1, :, here], values[:, here], dq
        )
        dk_sum[:, here] += dk
        dv_sum[:, here] += dv
    dq_out[:, pl.ds(pl.multiple_of(block * rows, rows), rows)] = (dq * scale).astype(jnp.bfloat16)
    send_block(block, step, True)

    @pl.when(step == steps - 1)
    def _():
        for number in range(main, group):
            await_grads(number)
            first = (number - main) * rows
            wide, grads, queries = prepare(long + first, rows)
            dq, dk, dv = part(
                wide,
                grads,
                queries,
                tail_ref[first : first + rows, :],
                qkv_ref[1, :, long:],
                values[:, long:],
                None,
            )
            dk_sum[:, long:] += dk
            dv_sum[:, long:] += dv
            dq_out[:, long + first : long + first + rows] = (dq * scale).astype(jnp.bfloat16)
            send_block(number, number, True)
        dkv_ref[0] = (dk_sum[...] * scale).astype(jnp.bfloat16)
        dkv_ref[1] = dv_sum[...].astype(jnp.bfloat16)
        for unit in plan:
            unit.stage(5)
        for copy in do_copies:
            copy.wait_send()
        for turn in range(main):
            send_block(block_at(turn), turn, False)
        for number in range(main, group):
            send_block(number, number, False)
        for ahead_by in range(1, group):
            source, device = me.peer(ahead_by)
            wire(
                lanes(dq_out, (ALL,), source * rows, rows),
                tokens_ref.at[source],
                dq_send.at[0],
                dq_recv.at[ahead_by],
                device,
            ).wait_recv()


def attn_bwd(
    probs, tail_probs, kept, attn, inv_total, grad_attn, long, partials, collective_id, cols=1024
):
    blks = lax.axis_size("blk")
    lead = (lax.axis_size("seq"), blks, lax.axis_size("head") // 2, 2)
    devices = math.prod(lead)
    length = kept.shape[2]
    tail = length - long
    group, _, rows = grad_attn.shape
    anywhere = pl.BlockSpec(memory_space=pl.ANY)
    edges = [(partial.shape[0] // devices, partial.shape[1]) for partial in partials]
    units = len(weight_units(edges))
    pair = [pltpu.SemaphoreType.DMA((group,))] * 2
    return pl.pallas_call(
        functools.partial(attn_bwd_kernel, blks, rows, cols),
        grid=(long // rows,),
        in_specs=[
            pl.BlockSpec((rows, long), lambda step: (step, 0)),
            once((tail, tail)),
            once(kept.shape),
            once((HEAD_DIM, length)),
            once((8, length)),
        ]
        + [anywhere] * 4,
        out_specs=[once((2, HEAD_DIM, length)), anywhere] + [once(edge) for edge in edges],
        out_shape=[
            jax.ShapeDtypeStruct((2, HEAD_DIM, length), jnp.bfloat16),
            jax.ShapeDtypeStruct((group, HEAD_DIM, rows), jnp.bfloat16),
        ]
        + [jax.ShapeDtypeStruct(edge, jnp.float32) for edge in edges],
        scratch_shapes=[
            pltpu.VMEM((HEAD_DIM, length), jnp.bfloat16),
            pltpu.VMEM((HEAD_DIM, length), jnp.bfloat16),
            pltpu.VMEM((HEAD_DIM + 16, length), jnp.bfloat16),
            pltpu.VMEM((HEAD_DIM, length), jnp.float32),
            pltpu.VMEM((HEAD_DIM, length), jnp.float32),
            pltpu.VMEM((2, 2, blks, 2, EDGE, UNIT), jnp.bfloat16),
            *reduce_scratch(units, blks),
            pltpu.SemaphoreType.DMA((4,)),
            *pair,
            *pair,
        ],
        compiler_params=pltpu.CompilerParams(
            collective_id=collective_id, has_side_effects=True, vmem_limit_bytes=62 * 2**20
        ),
        cost_estimate=pl.CostEstimate(
            flops=8 * long * long * HEAD_DIM, bytes_accessed=2 * long * long, transcendentals=0
        ),
        name="attn_bwd",
    )(
        probs, tail_probs, kept, attn, inv_total, grad_attn,
        *[partial.reshape(lead + edge) for partial, edge in zip(partials, edges)],
    )


def last_kernel(
    blks, devices, dkv_ref, dq_ref, x_ref, w_ref, base_ref, sums_ref,
    dw_out, dx_out, sums_out,
    grads, x, xt, weights, base, turned_dx, partial, bias, landed,
    r0, r1a, r1b, r2, r3, send, recv,
    own_sem, kv_send, kv_recv, sums_send, sums_recv,
):
    me = Place(blks)
    group = me.group
    width = x.shape[0]
    depth = x.shape[1]
    index, others = me.others(devices)
    loads = [
        pltpu.make_async_copy(source, target, own_sem.at[number])
        for number, (source, target) in enumerate(
            (
                (x_ref, x),
                (dq_ref, grads.at[0]),
                (w_ref, weights),
                (base_ref, base),
                (sums_ref, bias),
                (dkv_ref.at[0, :, pl.ds(pl.multiple_of(me.index * width, width), width)], grads.at[1, me.index]),
                (dkv_ref.at[1, :, pl.ds(pl.multiple_of(me.index * width, width), width)], grads.at[2, me.index]),
            )
        )
    ]
    for copy in loads:
        copy.start()
    greet(others)
    kv_copies = [[], []]
    for which in range(2):
        for ahead_by in range(1, group):
            peer, device = me.peer(group - ahead_by)
            slot = which * group + ahead_by
            copy = wire(
                lanes(dkv_ref, (which, ALL), peer * width, width),
                grads.at[which + 1, me.index],
                kv_send.at[slot],
                kv_recv.at[slot],
                device,
            )
            copy.start()
            kv_copies[which].append(copy)

    wires = Wires(send, recv)
    plan = []
    for number in range(6):
        tensor, half = number // 2, number % 2
        plan.append(
            Reduce(
                me,
                wires,
                partial.at[tensor],
                ((0, EDGE), (half * UNIT // 2, UNIT // 2)),
                half == 1,
                None,
                None,
                r0.at[number],
                (r1b if half else r1a).at[tensor],
                r2.at[number],
                r3.at[number],
                dw_out,
                ((0, EDGE), (tensor * UNIT + half * UNIT // 2, UNIT // 2)),
            )
        )

    def work(tensor):
        taken = grads[tensor].reshape(depth, width)
        for first in range(0, depth, 256):
            term = lax.dot_general(
                xt[first : first + 256, :], taken, BY_LAST, preferred_element_type=jnp.float32
            ).astype(jnp.bfloat16)
            for share in range(first // EDGE, (first + 256) // EDGE):
                at = (share // (blks * 4), share // 4 % blks, share // 2 % 2, share % 2)
                partial[(tensor,) + at] = term[share * EDGE - first : (share + 1) * EDGE - first]
        for unit in plan[2 * tensor : 2 * tensor + 2]:
            unit.stage(0)

    def work_input(tensor):
        taken = grads[tensor].reshape(depth, width)
        for first in range(0, depth, 256):
            term = jnp.dot(
                weights[first : first + 256, tensor * depth : (tensor + 1) * depth],
                taken,
                preferred_element_type=jnp.float32,
            )
            if tensor == 0:
                turned_dx[first : first + 256, :] = term
            elif tensor == 1:
                turned_dx[first : first + 256, :] += term
            else:
                total = turned_dx[first : first + 256, :] + term
                dx_out[:, first : first + 256] = base[:, first : first + 256] + total.T

    def stages(tensor, *which):
        for stage in which:
            for unit in plan[2 * tensor : 2 * tensor + 2]:
                unit.stage(stage)

    def note_bias(tensor, row):
        ones = jnp.ones((8, width), jnp.bfloat16)
        found = lax.dot_general(
            ones, grads[tensor].reshape(depth, width), BY_LAST, preferred_element_type=jnp.float32
        )
        per = 128 * devices // depth
        for owner in range(devices):
            first = owner // per * 128
            bias[owner, row : row + 1, :] = found[:1, first : first + 128]

    loads[0].wait()
    xt[...] = x[...].astype(jnp.float32).T.astype(jnp.bfloat16)
    loads[1].wait()
    work(0)
    stages(0, 2)
    loads[4].wait()
    note_bias(0, 3)
    loads[2].wait()
    work_input(0)
    stages(0, 3)
    loads[5].wait()
    for copy in kv_copies[0]:
        copy.wait_recv()
    work(1)
    stages(0, 4)
    stages(1, 2)
    work_input(1)
    stages(1, 3)
    loads[6].wait()
    for copy in kv_copies[1]:
        copy.wait_recv()
    work(2)
    note_bias(2, 4)
    small = []
    for slot, device in enumerate(others):
        peer = (device["seq"] * blks + device["blk"]) * 4 + device["head"]
        copy = wire(
            bias.at[peer], landed.at[slot], sums_send.at[slot], sums_recv.at[slot], device
        )
        small.append(copy)
    stages(2, 2)
    for copy in small:
        copy.start()
    stages(1, 4)
    loads[3].wait()
    work_input(2)
    stages(2, 3)
    stages(0, 5)
    stages(2, 4)
    for copy in small:
        copy.wait()
    sums_out[...] = jnp.sum(landed[...], axis=0) + bias[index]
    stages(1, 5)
    stages(2, 5)
    for copy in kv_copies[0] + kv_copies[1]:
        copy.wait_send()


def last_reduce(dkv, dq, x, w_qkv, base, sums, collective_id):
    seqs, blks, heads = (lax.axis_size(name) for name in EVERY)
    devices = seqs * blks * heads
    group = blks * heads
    width, depth = x.shape
    half = UNIT // 2
    return pl.pallas_call(
        functools.partial(last_kernel, blks, devices),
        out_shape=[
            jax.ShapeDtypeStruct((EDGE, 3 * depth), jnp.float32),
            jax.ShapeDtypeStruct((width, depth), jnp.float32),
            jax.ShapeDtypeStruct(sums.shape[1:], jnp.float32),
        ],
        in_specs=[pl.BlockSpec(memory_space=pl.ANY)] * 6,
        out_specs=[pl.BlockSpec(memory_space=pltpu.VMEM)] * 3,
        scratch_shapes=[
            pltpu.VMEM((3, group, HEAD_DIM, width), jnp.bfloat16),
            pltpu.VMEM((width, depth), jnp.bfloat16),
            pltpu.VMEM((depth, width), jnp.bfloat16),
            pltpu.VMEM((depth, 3 * depth), jnp.bfloat16),
            pltpu.VMEM((width, depth), jnp.float32),
            pltpu.VMEM((depth, width), jnp.float32),
            pltpu.VMEM((3, seqs, blks, heads // 2, 2, EDGE, UNIT), jnp.bfloat16),
            pltpu.VMEM(sums.shape, jnp.float32),
            pltpu.VMEM((devices - 1,) + sums.shape[1:], jnp.float32),
            *reduce_scratch(6, blks, half),
            pltpu.SemaphoreType.DMA((7,)),
            pltpu.SemaphoreType.DMA((2 * group,)),
            pltpu.SemaphoreType.DMA((2 * group,)),
            pltpu.SemaphoreType.DMA((devices,)),
            pltpu.SemaphoreType.DMA((devices,)),
        ],
        compiler_params=pltpu.CompilerParams(
            collective_id=collective_id, has_side_effects=True, vmem_limit_bytes=56 * 2**20
        ),
        name="last_reduce",
    )(dkv, dq, x, w_qkv, base, sums)


def tail_segments(doc_lengths, first, rows):
    return segment_ids(doc_lengths, first + lax.iota(jnp.int32, rows))


BESIDE = ()


def shards_heads(
    layer_input,
    weight_query,
    weight_key,
    weight_value,
    weight_output,
    weight_expand,
    weight_reduce,
    bias_query,
    bias_value,
    bias_output,
    bias_expand,
    bias_reduce,
    first_gain,
    first_shift,
    second_gain,
    second_shift,
    cotangent,
    doc_lengths,
):
    tok_rows, model_width = layer_input.shape[1:]
    head_count = lax.axis_size("head")
    blk_count = lax.axis_size("blk")
    count = head_count * blk_count
    seq_len = tok_rows * count
    long_rows = seq_len - seq_len // blk_count // 2
    flat_rows = layer_input.reshape(tok_rows, model_width)

    vectors = (
        bias_query,
        bias_value,
        bias_output,
        bias_reduce,
        first_gain,
        first_shift,
        second_gain,
        second_shift,
        bias_expand,
    )
    sizes = [vector.shape[0] for vector in vectors]
    lane = 128
    rows = [vector.reshape(1, -1) for vector in vectors[:-1]] + [bias_expand.reshape(-1, sizes[0])]
    vec, at = jnp.zeros((16, lane), layer_input.dtype), 0
    for row in rows:
        count_here = row.shape[0]
        vec = vec + jnp.pad(row, ((at, 16 - at - count_here), (0, lane - sizes[0])))
        at = at + count_here
    seg = tail_segments(doc_lengths, long_rows, seq_len - long_rows)[0]
    rest = (weight_output, weight_expand, weight_reduce)
    beside = {which: lax.all_gather(rest[which], EVERY, axis=0, tiled=True) for which in BESIDE}
    (
        probs, tail_probs, attn, inv_total, kept, attn_flat, w_qkv, vec, *wholes,
    ) = attn_fwd(
        flat_rows,
        vec,
        seg,
        (weight_query, weight_key, weight_value),
        tuple(share for which, share in enumerate(rest) if which not in BESIDE),
        5,
    )
    attn_flat = attn_flat.reshape(model_width, tok_rows)
    w_qkv = w_qkv.reshape(model_width, 3 * model_width)
    vec = vec.reshape(-1, sizes[0], lane)[:, :, :16].transpose(2, 0, 1).astype(jnp.float32)
    _, _, b_output, b_reduce, gain_one, shift_one, gain_two, shift_two = [
        vec[number].reshape(-1) for number in range(8)
    ]
    b_expand = vec[8:at].transpose(1, 0, 2).reshape(-1)
    w_output, w_expand, w_reduce = [
        beside[which] if which in BESIDE else wholes.pop(0).reshape(-1, share.shape[1])
        for which, share in enumerate(rest)
    ]

    resid_one = flat_rows.astype(jnp.float32) + left_dot(attn_flat, w_output) + b_output
    normed_one, norm_one_pull = jax.vjp(layer_norm, resid_one, gain_one, shift_one)
    normed_low = normed_one.astype(jnp.bfloat16)
    pre_act = plain_dot(normed_low, w_expand) + b_expand
    hidden_f32, gelu_pull = jax.vjp(gelu_curve, pre_act)
    hidden = hidden_f32.astype(jnp.bfloat16)
    resid_two = normed_one + plain_dot(hidden, w_reduce) + b_reduce
    result, norm_two_pull = jax.vjp(layer_norm, resid_two, gain_two, shift_two)
    layer_output = result.astype(jnp.bfloat16).reshape(layer_input.shape)
    tok_first = (lax.axis_index("blk") * head_count + lax.axis_index("head")) * tok_rows
    tok_seg = segment_ids(doc_lengths, tok_first + lax.iota(jnp.int32, tok_rows))
    live = (tok_seg > 0).astype(jnp.float32)
    grad_out = (cotangent.astype(jnp.float32) * live[..., None]).reshape(-1, model_width)
    grad_resid_two, grad_gain_two, grad_shift_two = norm_two_pull(grad_out)
    grad_ffn = grad_resid_two.astype(jnp.bfloat16)
    grad_w_reduce = left_dot(hidden, grad_ffn)
    grad_b_reduce = jnp.sum(grad_ffn.astype(jnp.float32), axis=0)
    (grad_pre,) = gelu_pull(right_dot(grad_ffn, w_reduce))
    grad_pre = grad_pre.astype(jnp.bfloat16)
    grad_w_expand = left_dot(normed_low, grad_pre)
    grad_b_expand = jnp.sum(grad_pre.astype(jnp.float32), axis=0)
    grad_normed = grad_resid_two + right_dot(grad_pre, w_expand)
    grad_resid_one, grad_gain_one, grad_shift_one = norm_one_pull(grad_normed)
    grad_branch = grad_resid_one.astype(jnp.bfloat16)
    grad_w_output = plain_dot(attn_flat, grad_branch)
    grad_b_output = jnp.sum(grad_branch.astype(jnp.float32), axis=0)
    grad_attn = right_dot(w_output, grad_branch).astype(jnp.bfloat16)
    grad_attn = grad_attn.reshape(HEADS, HEAD_DIM, tok_rows)

    grad_kv, grad_query, grad_w_output, grad_w_expand, grad_w_reduce = attn_bwd(
        probs,
        tail_probs,
        kept,
        attn,
        inv_total,
        grad_attn,
        long_rows,
        [grad.astype(jnp.bfloat16) for grad in (grad_w_output, grad_w_expand, grad_w_reduce)],
        6,
    )

    sums = (
        jnp.zeros_like(b_output),
        jnp.zeros_like(b_output),
        grad_b_output,
        grad_b_reduce,
        grad_gain_one,
        grad_shift_one,
        grad_gain_two,
        grad_shift_two,
        grad_b_expand,
    )
    sums = jnp.concatenate([term.reshape(-1, size) for term, size in zip(sums, sizes)], axis=1)
    sums = jnp.pad(sums, ((0, 0), (0, 8 * lane - sums.shape[1]))).reshape(-1, 8, lane)
    grad_w_qkv, grad_input, sums = last_reduce(
        grad_kv, grad_query, flat_rows, w_qkv, grad_resid_one, sums, 7
    )
    owner = (lax.axis_index("seq") * blk_count + lax.axis_index("blk")) * head_count
    owner = owner + lax.axis_index("head")
    within = lax.rem(owner, lane // sizes[0]) * sizes[0]
    g_query = lax.dynamic_slice_in_dim(sums[3], within, sizes[0])
    g_value = lax.dynamic_slice_in_dim(sums[4], within, sizes[1])
    sums = sums.reshape(-1)
    parts, start = [], 0
    for size in sizes:
        parts.append(sums[start : start + size])
        start += size
    g_output, g_reduce, g_gain_one, g_shift_one, g_gain_two, g_shift_two, g_expand = parts[2:]
    return (
        layer_output,
        grad_input.reshape(layer_input.shape),
        grad_w_qkv[:, :model_width],
        grad_w_qkv[:, model_width : 2 * model_width],
        grad_w_qkv[:, 2 * model_width :],
        grad_w_output,
        grad_w_expand,
        grad_w_reduce,
        g_query,
        g_value,
        g_output,
        g_expand,
        g_reduce,
        g_gain_one,
        g_shift_one,
        g_gain_two,
        g_shift_two,
    )


def solution(mesh):
    placed = (
        P("seq", ("blk", "head"), None),
        P(("seq", "blk", "head"), None),
        P(("seq", "blk", "head"), None),
        P(("seq", "blk", "head"), None),
        P(("seq", "blk", "head"), None),
        P(("seq", "blk", "head"), None),
        P(("seq", "blk", "head"), None),
        P(("seq", "blk", "head")),
        P(("seq", "blk", "head")),
        P(("seq", "blk", "head")),
        P(("seq", "blk", "head")),
        P(("seq", "blk", "head")),
        P(("seq", "blk", "head")),
        P(("seq", "blk", "head")),
        P(("seq", "blk", "head")),
        P(("seq", "blk", "head")),
        P("seq", ("blk", "head"), None),
        P("seq", None),
    )
    group = mesh.shape["blk"] * mesh.shape["head"]
    body = shards_heads if group == HEADS else shards_general
    return jax.shard_map(
        body,
        mesh=mesh,
        in_specs=placed,
        out_specs=(
            P("seq", ("blk", "head"), None),
            P("seq", ("blk", "head"), None),
            P(("seq", "blk", "head"), None),
            P(("seq", "blk", "head"), None),
            P(("seq", "blk", "head"), None),
            P(("seq", "blk", "head"), None),
            P(("seq", "blk", "head"), None),
            P(("seq", "blk", "head"), None),
            P(("seq", "blk", "head")),
            P(("seq", "blk", "head")),
            P(("seq", "blk", "head")),
            P(("seq", "blk", "head")),
            P(("seq", "blk", "head")),
            P(("seq", "blk", "head")),
            P(("seq", "blk", "head")),
            P(("seq", "blk", "head")),
            P(("seq", "blk", "head")),
        ),
        check_vma=False,
    )
```

```python
import functools
import math

import jax
import jax.numpy as jnp
from jax import lax
from jax.experimental import pallas as pl
from jax.experimental.pallas import tpu as pltpu
from jax.sharding import PartitionSpec as P

HEADS = 16
HEAD_DIM = 64


NORM_EPS = 1e-05
INV_ROOT2 = 0.7071067811865476


def segment_ids(doc_lengths, positions):
    ends = jnp.cumsum(doc_lengths, axis=-1)
    counted = jnp.sum((ends[:, None, :] <= positions[None, :, None]).astype(jnp.int32), axis=-1)
    return jnp.where(positions[None, :] < ends[:, -1:], counted + 1, 0)


def layer_norm(values, gain, shift):
    center = values - jnp.mean(values, axis=-1, keepdims=True)
    spread = jnp.mean(center * center, axis=-1, keepdims=True)
    return center * lax.rsqrt(spread + NORM_EPS) * gain + shift


def gelu_curve(values):
    return 0.5 * values * (1.0 + lax.erf(values * INV_ROOT2))


def plain_dot(left, right):
    return jnp.dot(left, right, preferred_element_type=jnp.float32)


def left_dot(left, right):
    return lax.dot_general(
        left, right, (((0,), (0,)), ((), ())), preferred_element_type=jnp.float32
    )


def right_dot(left, right):
    return lax.dot_general(
        left, right, (((1,), (1,)), ((), ())), preferred_element_type=jnp.float32
    )


def score_grads(scores, allowed, grad_part, value_part, lse_part, delta_part):
    probs = jnp.where(allowed, jnp.exp(scores - lse_part[..., None]), 0.0)
    grad_probs = jnp.einsum(
        "sqhd,skhd->shqk", grad_part, value_part, preferred_element_type=jnp.float32
    )
    grad_scores = (probs * (grad_probs - delta_part[..., None])).astype(jnp.bfloat16)
    return (probs, grad_scores)


def shards_general(
    layer_input,
    weight_query,
    weight_key,
    weight_value,
    weight_output,
    weight_expand,
    weight_reduce,
    bias_query,
    bias_value,
    bias_output,
    bias_expand,
    bias_reduce,
    first_gain,
    first_shift,
    second_gain,
    second_shift,
    cotangent,
    doc_lengths,
):
    seq_count, tok_rows, model_width = layer_input.shape
    head_count = lax.axis_size("head")
    blk_count = lax.axis_size("blk")
    heads_here = HEADS // head_count
    score_scale = HEAD_DIM ** (-0.5)
    gathered = (
        lax.all_gather(weight_query, ("seq", "blk", "head"), axis=0, tiled=True),
        lax.all_gather(weight_key, ("seq", "blk", "head"), axis=0, tiled=True),
        lax.all_gather(weight_value, ("seq", "blk", "head"), axis=0, tiled=True),
        lax.all_gather(weight_output, ("seq", "blk", "head"), axis=0, tiled=True),
        lax.all_gather(weight_expand, ("seq", "blk", "head"), axis=0, tiled=True),
        lax.all_gather(weight_reduce, ("seq", "blk", "head"), axis=0, tiled=True),
        lax.all_gather(bias_query, ("seq", "blk", "head"), axis=0, tiled=True),
        lax.all_gather(bias_value, ("seq", "blk", "head"), axis=0, tiled=True),
        lax.all_gather(bias_output, ("seq", "blk", "head"), axis=0, tiled=True),
        lax.all_gather(bias_expand, ("seq", "blk", "head"), axis=0, tiled=True),
        lax.all_gather(bias_reduce, ("seq", "blk", "head"), axis=0, tiled=True),
        lax.all_gather(first_gain, ("seq", "blk", "head"), axis=0, tiled=True),
        lax.all_gather(first_shift, ("seq", "blk", "head"), axis=0, tiled=True),
        lax.all_gather(second_gain, ("seq", "blk", "head"), axis=0, tiled=True),
        lax.all_gather(second_shift, ("seq", "blk", "head"), axis=0, tiled=True),
    )
    w_query, w_key, w_value, w_output, w_expand, w_reduce = gathered[:6]
    b_query, b_value, b_output, b_expand, b_reduce, gain_one, shift_one, gain_two, shift_two = [
        vector.astype(jnp.float32) for vector in gathered[6:]
    ]
    flat_rows = layer_input.reshape(-1, model_width)
    queries = (
        (plain_dot(flat_rows, w_query) + b_query).astype(jnp.bfloat16).reshape(layer_input.shape)
    )
    key_rows = plain_dot(flat_rows, w_key).astype(jnp.bfloat16).reshape(layer_input.shape)
    value_rows = (
        (plain_dot(flat_rows, w_value) + b_value).astype(jnp.bfloat16).reshape(layer_input.shape)
    )
    query_heads, key_heads, value_heads = (
        lax.all_to_all(queries, "head", split_axis=2, concat_axis=1, tiled=True),
        lax.all_to_all(key_rows, "head", split_axis=2, concat_axis=1, tiled=True),
        lax.all_to_all(value_rows, "head", split_axis=2, concat_axis=1, tiled=True),
    )
    block_rows = query_heads.shape[1]
    block_first = lax.axis_index("blk") * block_rows
    query_seg = segment_ids(doc_lengths, block_first + lax.iota(jnp.int32, block_rows))
    query_split = query_heads.reshape(seq_count, block_rows, heads_here, HEAD_DIM)

    def key_block(shard_piece, block_index, block_width):
        key_offset = block_index * block_width
        key_part = lax.dynamic_slice_in_dim(shard_piece[0], key_offset, block_width, 1).reshape(
            seq_count, block_width, heads_here, HEAD_DIM
        )
        value_part = lax.dynamic_slice_in_dim(shard_piece[1], key_offset, block_width, 1).reshape(
            seq_count, block_width, heads_here, HEAD_DIM
        )
        key_seg = segment_ids(doc_lengths, key_offset + lax.iota(jnp.int32, block_width))
        allowed = query_seg[:, None, :, None] == key_seg[:, None, None, :]
        scores = (
            jnp.einsum("sqhd,skhd->shqk", query_split, key_part, preferred_element_type=jnp.float32)
            * score_scale
        )
        return (key_offset, key_part, value_part, allowed, scores)

    stat_shape = (seq_count, heads_here, block_rows)
    start_state = (
        jnp.full(stat_shape, -1e30, jnp.float32),
        jnp.zeros(stat_shape, jnp.float32),
        jnp.zeros(stat_shape + (HEAD_DIM,), jnp.float32),
    )
    shard_piece = (
        lax.all_gather(key_heads, "blk", axis=1, tiled=True),
        lax.all_gather(value_heads, "blk", axis=1, tiled=True),
    )
    piece_rows = shard_piece[0].shape[1]
    block_width = math.gcd(piece_rows, 512)

    def advance(block_index, loop_state):
        running_max, row_total, accum = loop_state
        key_offset, key_part, value_part, allowed, scores = key_block(
            shard_piece, block_index, block_width
        )
        scores = jnp.where(allowed, scores, -1e30)
        new_max = jnp.maximum(running_max, jnp.max(scores, axis=-1))
        rescale = jnp.exp(running_max - new_max)
        weights = jnp.where(allowed, jnp.exp(scores - new_max[..., None]), 0.0)
        row_total = row_total * rescale + jnp.sum(weights, axis=-1)
        accum = accum * rescale[..., None] + jnp.einsum(
            "shqk,skhd->shqd",
            weights.astype(jnp.bfloat16),
            value_part,
            preferred_element_type=jnp.float32,
        )
        return (new_max, row_total, accum)

    running_max, row_total, accum = lax.fori_loop(
        0, piece_rows // block_width, advance, start_state
    )
    log_total = running_max + jnp.log(row_total)
    attn_heads = accum / row_total[..., None]
    attn_send = (
        attn_heads.transpose(0, 2, 1, 3)
        .reshape(seq_count, block_rows, heads_here * HEAD_DIM)
        .astype(jnp.bfloat16)
    )
    attn_tokens = lax.all_to_all(attn_send, "head", split_axis=1, concat_axis=2, tiled=True)
    attn_flat = attn_tokens.reshape(-1, model_width)
    resid_one = flat_rows.astype(jnp.float32) + plain_dot(attn_flat, w_output) + b_output
    normed_one, norm_one_pull = jax.vjp(layer_norm, resid_one, gain_one, shift_one)
    normed_low = normed_one.astype(jnp.bfloat16)
    pre_act = plain_dot(normed_low, w_expand) + b_expand
    hidden_f32, gelu_pull = jax.vjp(gelu_curve, pre_act)
    hidden = hidden_f32.astype(jnp.bfloat16)
    resid_two = normed_one + plain_dot(hidden, w_reduce) + b_reduce
    result, norm_two_pull = jax.vjp(layer_norm, resid_two, gain_two, shift_two)
    layer_output = result.astype(jnp.bfloat16).reshape(layer_input.shape)
    tok_first = (lax.axis_index("blk") * head_count + lax.axis_index("head")) * tok_rows
    tok_seg = segment_ids(doc_lengths, tok_first + lax.iota(jnp.int32, tok_rows))
    live = (tok_seg > 0).astype(jnp.float32)
    grad_out = (cotangent.astype(jnp.float32) * live[..., None]).reshape(-1, model_width)
    grad_resid_two, grad_gain_two, grad_shift_two = norm_two_pull(grad_out)
    grad_ffn = grad_resid_two.astype(jnp.bfloat16)
    grad_w_reduce = left_dot(hidden, grad_ffn)
    grad_b_reduce = jnp.sum(grad_ffn.astype(jnp.float32), axis=0)
    (grad_pre,) = gelu_pull(right_dot(grad_ffn, w_reduce))
    grad_pre = grad_pre.astype(jnp.bfloat16)
    grad_w_expand = left_dot(normed_low, grad_pre)
    grad_b_expand = jnp.sum(grad_pre.astype(jnp.float32), axis=0)
    grad_normed = grad_resid_two + right_dot(grad_pre, w_expand)
    grad_resid_one, grad_gain_one, grad_shift_one = norm_one_pull(grad_normed)
    grad_branch = grad_resid_one.astype(jnp.bfloat16)
    grad_w_output = left_dot(attn_flat, grad_branch)
    grad_b_output = jnp.sum(grad_branch.astype(jnp.float32), axis=0)
    grad_attn = right_dot(grad_branch, w_output).astype(jnp.bfloat16).reshape(layer_input.shape)
    grad_attn_heads = lax.all_to_all(grad_attn, "head", split_axis=2, concat_axis=1, tiled=True)
    grad_attn_split = grad_attn_heads.reshape(seq_count, block_rows, heads_here, HEAD_DIM)
    row_delta = jnp.einsum("sqhd,shqd->shq", grad_attn_split.astype(jnp.float32), attn_heads)
    full_rows = blk_count * block_rows
    query_zero = jnp.zeros((seq_count, block_rows, heads_here, HEAD_DIM), jnp.float32)
    back_state = (
        query_zero,
        jnp.zeros((seq_count, full_rows, heads_here * HEAD_DIM), jnp.float32),
        jnp.zeros((seq_count, full_rows, heads_here * HEAD_DIM), jnp.float32),
    )
    fold_shard_piece = (
        lax.all_gather(key_heads, "blk", axis=1, tiled=True),
        lax.all_gather(value_heads, "blk", axis=1, tiled=True),
    )
    piece_rows = fold_shard_piece[0].shape[1]
    fold_block_width = math.gcd(piece_rows, 512)

    def advance(block_index, loop_state):
        grad_query, grad_keys, grad_values = loop_state
        key_offset, key_part, value_part, allowed, scores = key_block(
            fold_shard_piece, block_index, fold_block_width
        )
        probs, grad_scores = score_grads(
            scores, allowed, grad_attn_split, value_part, log_total, row_delta
        )
        grad_query = (
            grad_query
            + jnp.einsum(
                "shqk,skhd->sqhd", grad_scores, key_part, preferred_element_type=jnp.float32
            )
            * score_scale
        )
        key_term = (
            jnp.einsum(
                "shqk,sqhd->skhd", grad_scores, query_split, preferred_element_type=jnp.float32
            )
            * score_scale
        )
        value_term = jnp.einsum(
            "shqk,sqhd->skhd",
            probs.astype(jnp.bfloat16),
            grad_attn_split,
            preferred_element_type=jnp.float32,
        )
        grad_keys = lax.dynamic_update_slice_in_dim(
            grad_keys,
            key_term.reshape(seq_count, fold_block_width, heads_here * HEAD_DIM),
            key_offset,
            1,
        )
        grad_values = lax.dynamic_update_slice_in_dim(
            grad_values,
            value_term.reshape(seq_count, fold_block_width, heads_here * HEAD_DIM),
            key_offset,
            1,
        )
        return (grad_query, grad_keys, grad_values)

    back_out = lax.fori_loop(0, piece_rows // fold_block_width, advance, back_state)
    grad_query = back_out[0]
    key_share, value_share = (
        lax.psum_scatter(
            back_out[1].astype(jnp.bfloat16), "blk", scatter_dimension=1, tiled=True
        ).astype(jnp.float32),
        lax.psum_scatter(
            back_out[2].astype(jnp.bfloat16), "blk", scatter_dimension=1, tiled=True
        ).astype(jnp.float32),
    )
    query_send = grad_query.reshape(seq_count, block_rows, heads_here * HEAD_DIM).astype(
        jnp.bfloat16
    )
    query_back, key_back, value_back = (
        lax.all_to_all(query_send, "head", split_axis=1, concat_axis=2, tiled=True),
        lax.all_to_all(
            key_share.astype(jnp.bfloat16), "head", split_axis=1, concat_axis=2, tiled=True
        ),
        lax.all_to_all(
            value_share.astype(jnp.bfloat16), "head", split_axis=1, concat_axis=2, tiled=True
        ),
    )
    query_back = query_back.reshape(-1, model_width)
    key_back = key_back.reshape(-1, model_width)
    value_back = value_back.reshape(-1, model_width)
    grad_w_query = left_dot(flat_rows, query_back)
    grad_w_key = left_dot(flat_rows, key_back)
    grad_w_value = left_dot(flat_rows, value_back)
    grad_b_query = jnp.sum(query_back.astype(jnp.float32), axis=0)
    grad_b_value = jnp.sum(value_back.astype(jnp.float32), axis=0)
    grad_input = (
        grad_resid_one
        + right_dot(query_back, w_query)
        + right_dot(key_back, w_key)
        + right_dot(value_back, w_value)
    )
    grad_input = grad_input.reshape(layer_input.shape)
    shares_all = (
        lax.psum_scatter(grad_w_query, ("seq", "blk", "head"), scatter_dimension=0, tiled=True),
        lax.psum_scatter(grad_w_key, ("seq", "blk", "head"), scatter_dimension=0, tiled=True),
        lax.psum_scatter(grad_w_value, ("seq", "blk", "head"), scatter_dimension=0, tiled=True),
        lax.psum_scatter(grad_w_output, ("seq", "blk", "head"), scatter_dimension=0, tiled=True),
        lax.psum_scatter(grad_w_expand, ("seq", "blk", "head"), scatter_dimension=0, tiled=True),
        lax.psum_scatter(grad_w_reduce, ("seq", "blk", "head"), scatter_dimension=0, tiled=True),
        lax.psum_scatter(grad_b_query, ("seq", "blk", "head"), scatter_dimension=0, tiled=True),
        lax.psum_scatter(grad_b_value, ("seq", "blk", "head"), scatter_dimension=0, tiled=True),
        lax.psum_scatter(grad_b_output, ("seq", "blk", "head"), scatter_dimension=0, tiled=True),
        lax.psum_scatter(grad_b_expand, ("seq", "blk", "head"), scatter_dimension=0, tiled=True),
        lax.psum_scatter(grad_b_reduce, ("seq", "blk", "head"), scatter_dimension=0, tiled=True),
        lax.psum_scatter(grad_gain_one, ("seq", "blk", "head"), scatter_dimension=0, tiled=True),
        lax.psum_scatter(grad_shift_one, ("seq", "blk", "head"), scatter_dimension=0, tiled=True),
        lax.psum_scatter(grad_gain_two, ("seq", "blk", "head"), scatter_dimension=0, tiled=True),
        lax.psum_scatter(grad_shift_two, ("seq", "blk", "head"), scatter_dimension=0, tiled=True),
    )
    return (
        layer_output,
        grad_input,
        shares_all[0],
        shares_all[1],
        shares_all[2],
        shares_all[3],
        shares_all[4],
        shares_all[5],
        shares_all[6],
        shares_all[7],
        shares_all[8],
        shares_all[9],
        shares_all[10],
        shares_all[11],
        shares_all[12],
        shares_all[13],
        shares_all[14],
    )


MESH = pl.DeviceIdType.MESH
EVERY = ("seq", "blk", "head")
EDGE = 32
UNIT = 1024


class Place:
    def __init__(self, blks):
        self.blks = blks
        self.x = lax.axis_index("seq")
        self.z = lax.axis_index("blk")
        lane = lax.axis_index("head")
        self.y = lane // 2
        self.c = lax.rem(lane, 2)
        self.index = self.z * 4 + lane
        self.group = blks * 4

    def peer(self, step):
        index = lax.rem(self.index + step, self.group)
        return index, self.member(index)

    def member(self, index):
        return {"seq": self.x, "blk": index // 4, "head": lax.rem(index, 4)}

    def at(self, x=None, z=None, y=None, c=None):
        x = self.x if x is None else x
        z = self.z if z is None else z
        y = self.y if y is None else y
        c = self.c if c is None else c
        return {"seq": x, "blk": z, "head": y * 2 + c}

    def column(self):
        return [lax.rem(self.z + step, self.blks) for step in range(1, self.blks)]

    def near(self):
        return [self.at(z=z) for z in self.column()] + [
            self.at(x=1 - self.x),
            self.at(y=1 - self.y),
            self.at(c=1 - self.c),
        ]

    def others(self, devices):
        own = (self.x * self.blks + self.z) * 4 + self.y * 2 + self.c
        found = []
        for step in range(1, devices):
            index = lax.rem(own + step, devices)
            found.append(
                {
                    "seq": index // (self.blks * 4),
                    "blk": lax.rem(index // 4, self.blks),
                    "head": lax.rem(index, 4),
                }
            )
        return own, found


def greet(devices):
    barrier = pltpu.get_barrier_semaphore()
    for device in devices:
        pl.semaphore_signal(barrier, inc=1, device_id=device, device_id_type=MESH)
    pl.semaphore_wait(barrier, len(devices))


class Wires:
    def __init__(self, send, recv):
        self.send, self.recv, self.used = send, recv, 0

    def copy(self, source, target, device):
        slot = self.used
        self.used += 1
        return pltpu.make_async_remote_copy(
            src_ref=source,
            dst_ref=target,
            send_sem=self.send.at[slot],
            recv_sem=self.recv.at[slot],
            device_id=device,
            device_id_type=MESH,
        )


def view(ref, index, piece):
    rows, cols = piece
    return ref.at[tuple(index) + (pl.ds(*rows), pl.ds(*cols))]


ALL = slice(None)


def share_line(me, wires, ref, piece, source=None):
    own = view(ref, (me.x, me.z, me.y, me.c), piece)
    source = own if source is None else source
    return [wires.copy(source, own, me.at(z=peer)) for peer in me.column()]


class Gather:
    WIRES = 7

    def __init__(self, me, wires, ref, piece, turned, ready=False, source=None):
        x, z, y, c = me.x, me.z, me.y, me.c
        self.first = [] if ready else share_line(me, wires, ref, piece, source)
        line = view(ref, (x, ALL, y, c), piece)
        if turned:
            half, rest = view(ref, (ALL, ALL, y, c), piece), view(ref, (ALL, ALL, 1 - y, c), piece)
            self.second = wires.copy(line, line, me.at(x=1 - x))
            self.third = wires.copy(half, half, me.at(y=1 - y))
        else:
            half, rest = view(ref, (x, ALL, ALL, c), piece), view(ref, (1 - x, ALL, ALL, c), piece)
            self.second = wires.copy(line, line, me.at(y=1 - y))
            self.third = wires.copy(half, half, me.at(x=1 - x))
        self.near = wires.copy(half, half, me.at(c=1 - c))
        self.far = wires.copy(rest, rest, me.at(c=1 - c))

    def stage(self, index):
        if index == 0:
            for copy in self.first:
                copy.start()
        elif index == 1:
            for copy in self.first:
                copy.wait_recv()
            self.second.start()
        elif index == 2:
            self.second.wait_recv()
            self.third.start()
            self.near.start()
        elif index == 3:
            self.third.wait_recv()
            self.far.start()
        else:
            self.near.wait_recv()
            self.far.wait_recv()
            for copy in (*self.first, self.second, self.third, self.near, self.far):
                copy.wait_send()


class Relay(Gather):
    WIRES = 7

    def __init__(self, me, wires, ref, piece, turned, source):
        super().__init__(me, wires, ref, piece, turned, ready=True)
        x, z, y, c = me.x, me.z, me.y, me.c
        own = view(ref, (x, z, y, c), piece)
        beside = me.at(z=z + 1 - 2 * lax.rem(z, 2))
        pair = view(ref, (x, pl.ds(z // 2 * 2, 2), y, c), piece)
        other = view(ref, (x, pl.ds(2 - z // 2 * 2, 2), y, c), piece)
        self.inner = (z == 1) | (z == 2)
        self.own = wires.copy(source, own, beside)
        self.cross = wires.copy(pair, pair, me.at(z=lax.rem(3 - z, 4)))
        self.outward = wires.copy(other, other, beside)

    def stage(self, index):
        if index == 0:
            self.own.start()
        elif index == 1:
            self.own.wait_recv()

            @pl.when(self.inner)
            def _():
                self.cross.start()

        elif index == 2:

            @pl.when(self.inner)
            def _():
                self.cross.wait_recv()
                self.outward.start()

        elif index == 3:

            @pl.when(jnp.logical_not(self.inner))
            def _():
                self.outward.wait_recv()

            super().stage(1)
        elif index < 6:
            super().stage(index - 2)
        else:

            @pl.when(self.inner)
            def _():
                self.cross.wait_send()
                self.outward.wait_send()

            self.own.wait_send()
            super().stage(4)


class Reduce:
    WIRES = 6

    def __init__(self, me, wires, ref, piece, turned, own, own_sem, r0, r1, r2, r3, out, out_piece):
        x, z, y, c = me.x, me.z, me.y, me.c
        self.place, self.turned, self.out, self.out_piece = me, turned, out, out_piece
        self.r0, self.r1, self.r2, self.r3 = r0, r1, r2, r3
        if own is None:
            self.load = None
            self.own = lambda at: ref[at + (c, pl.ds(*piece[0]), pl.ds(*piece[1]))]
        else:
            self.load = pltpu.make_async_copy(view(ref, (ALL, ALL, ALL, c), piece), own, own_sem)
            self.own = lambda at: own[at]
        self.zero = wires.copy(view(ref, (ALL, ALL, ALL, 1 - c), piece), r0, me.at(c=1 - c))
        if turned:
            self.one = wires.copy(r0.at[:, :, 1 - y], r1, me.at(y=1 - y))
            self.two = wires.copy(r0.at[1 - x, :, y], r2, me.at(x=1 - x))
        else:
            self.one = wires.copy(r0.at[1 - x], r1, me.at(x=1 - x))
            self.two = wires.copy(r0.at[x, :, 1 - y], r2, me.at(y=1 - y))
        self.three = [
            wires.copy(r0.at[x, peer, y], r3.at[slot], me.at(z=peer))
            for slot, peer in enumerate(me.column())
        ]

    def stage(self, index):
        x, z, y = self.place.x, self.place.z, self.place.y
        blks = self.place.blks
        r0 = self.r0

        def add(target, term):
            total = r0[target].astype(jnp.float32) + term.astype(jnp.float32)
            r0[target] = total.astype(r0.dtype)

        if index == 0:
            self.zero.start()
        elif index == 1:
            self.load.start()
        elif index == 2:
            if self.load is not None:
                self.load.wait()
            self.zero.wait_recv()

            @pl.loop(0, 4 * blks)
            def _(i):
                at = (i // (2 * blks), lax.rem(i // 2, blks), lax.rem(i, 2))
                add(at, self.own(at))

            self.one.start()
        elif index == 3:
            self.one.wait_recv()

            @pl.loop(0, 2 * blks)
            def _(i):
                if self.turned:
                    a, b = i // blks, lax.rem(i, blks)
                    add((a, b, y), self.r1[a, b])
                else:
                    a, b = i // 2, lax.rem(i, 2)
                    add((x, a, b), self.r1[a, b])

            self.two.start()
        elif index == 4:
            self.two.wait_recv()

            @pl.loop(0, blks)
            def _(i):
                add((x, i, y), self.r2[i])

            for copy in self.three:
                copy.start()
        else:
            for copy in self.three:
                copy.wait_recv()
            total = r0[x, z, y].astype(jnp.float32)
            for slot in range(blks - 1):
                total = total + self.r3[slot].astype(jnp.float32)
            rows, cols = self.out_piece
            self.out[rows[0] : rows[0] + rows[1], cols[0] : cols[0] + cols[1]] = total
            for copy in (self.zero, self.one, self.two, *self.three):
                copy.wait_send()


def reduce_scratch(units, blks, cols=UNIT, dtype=jnp.bfloat16):
    turned = units // 2
    return [
        pltpu.VMEM((units, 2, blks, 2, EDGE, cols), dtype),
        pltpu.VMEM((units - turned, blks, 2, EDGE, cols), dtype),
        pltpu.VMEM((turned, 2, blks, EDGE, cols), dtype),
        pltpu.VMEM((units, blks, EDGE, cols), dtype),
        pltpu.VMEM((units, blks - 1, EDGE, cols), dtype),
        pltpu.SemaphoreType.DMA((Reduce.WIRES * units,)),
        pltpu.SemaphoreType.DMA((Reduce.WIRES * units,)),
    ]


def weight_units(edges):
    columns = []
    for which, (rows, cols) in enumerate(edges):
        columns.append(
            [
                (which, ((row, EDGE), (col, UNIT)))
                for row in range(0, rows, EDGE)
                for col in range(0, cols, UNIT)
            ]
        )
    most = max([len(column) for column in columns] + [0])
    return [column[place] for place in range(most) for column in columns if place < len(column)]


LOG2E = 1.4426950408889634
BY_LAST = (((1,), (1,)), ((), ()))


def lanes(ref, lead, first, width):
    return ref.at[tuple(lead) + (pl.ds(pl.multiple_of(first, width), width),)]


def wire(source, target, send_sem, recv_sem, device):
    return pltpu.make_async_remote_copy(
        src_ref=source,
        dst_ref=target,
        send_sem=send_sem,
        recv_sem=recv_sem,
        device_id=device,
        device_id_type=MESH,
    )


def TURNED(number):
    return number % 2 == 1


def SCHEDULE(number):
    return (-4, -2, -1, -0.9 if number < 4 else number / 2, 5 + number)


def home(block, main):
    return jnp.where(block < main, block // 2 + main // 2 * lax.rem(block, 2), block)


def cuts(width, cols):
    return [(first, min(first + cols, width)) for first in range(0, width, cols)]


def attn_fwd_kernel(
    blks, rows, cols, count, *refs
):
    x_ref, vec_ref, down_ref, across_ref, wq, wk, wv = refs[:7]
    shares, refs = refs[7 : 7 + count], refs[7 + count :]
    p_ref, tail_ref, o_ref, inv_ref, kept_ref, tokens_ref, qkv_out, vec_out = refs[:8]
    wholes, refs = refs[8 : 8 + count], refs[8 + count :]
    (
    weights, vecs, qkv_ref, land, keys, values, s0, s1, m0, m1, now, peaks, acc, top,
    own_sem, kv_send, kv_recv, q_send, q_recv, o_send, o_recv, send, recv,
    ) = refs
    step, steps = pl.program_id(0), pl.num_programs(0)
    length, part = land.shape[2], p_ref.shape[1]
    long = 2 * part
    width = 2 * rows
    tail, pieces = length - long, cuts(part, cols)
    main = long // width
    side, turn = step // main, lax.rem(step, main)
    scale = LOG2E * HEAD_DIM**-0.5

    me = Place(blks)
    group = me.group

    def block_at(turn):
        return lax.rem(lax.rem(me.index, main) + turn, main)

    def ahead(block):
        return lax.rem(block + group - me.index, group)

    def spot(tensor, block):
        return home(block, main) if tensor else block

    early = (me.index < main) & (lax.rem(me.index, 2) == 0)
    swaps = [[], [], []]
    for tensor, send_sem, recv_sem in ((0, q_send, q_recv), (1, kv_send, kv_recv), (2, kv_send, kv_recv)):
        for ahead_by in range(1, group):
            peer, device = me.peer(group - ahead_by)
            slot = ahead_by + (group if tensor == 2 else 0)
            swaps[tensor].append(
                wire(
                    qkv_ref.at[tensor, peer],
                    lanes(land, (tensor, ALL), spot(tensor, me.index) * width, width),
                    send_sem.at[slot],
                    recv_sem.at[slot],
                    device,
                )
            )
    keep = pltpu.make_async_copy(land, kept_ref, own_sem.at[1])

    def await_from(tensor, block):
        @pl.when(block != me.index)
        def _():
            send_sem, recv_sem = (kv_send, kv_recv) if tensor else (q_send, q_recv)
            wire(
                qkv_ref.at[tensor, block],
                lanes(land, (tensor, ALL), spot(tensor, block) * width, width),
                send_sem.at[0],
                recv_sem.at[ahead(block) + (group if tensor == 2 else 0)],
                me.member(block),
            ).wait_recv()

    def await_keys(first):
        for block in range(first, main, 2):
            await_from(1, block)
            await_from(2, block)
        here = slice(first * part, (first + 1) * part)
        keys[first, 0:HEAD_DIM, :] = land[1, :, here]
        keys[first, HEAD_DIM:, :] = land[1, :, here]
        values[first, 0:HEAD_DIM, :] = land[2, :, here]
        values[first, HEAD_DIM:, :] = ones_row(part)

    def ones_row(columns):
        return (
            (lax.broadcasted_iota(jnp.int32, (16, columns), 0) == 0)
            .astype(jnp.float32)
            .astype(jnp.bfloat16)
        )

    def send_block(block, slot, start):
        source = lanes(o_ref, (ALL,), block * width, width)
        remote = wire(
            source,
            tokens_ref.at[me.index],
            o_send.at[slot],
            o_recv.at[lax.rem(me.index + group - block, group)],
            me.member(block),
        )
        local = pltpu.make_async_copy(source, tokens_ref.at[me.index], own_sem.at[2])

        @pl.when(block != me.index)
        def _():
            if start:
                remote.start()
            else:
                remote.wait_send()

        @pl.when(block == me.index)
        def _():
            if start:
                local.start()
            else:
                local.wait()

    wires = Wires(send, recv)
    here = (me.x, me.z, me.y, me.c)
    half = UNIT // 2
    fronts = []
    for unit, ref in enumerate((wq, wk, wv)):
        for flank in range(2):
            piece = ((0, EDGE), (unit * UNIT + flank * half, half))
            source = ref.at[:, pl.ds(flank * half, half)]
            fronts.append(Gather(me, wires, weights, piece, flank == 1, source=source))
    vectors = Gather(me, wires, vecs, ((0, EDGE), (0, vecs.shape[5])), False)
    units = weight_units([share.shape for share in shares])
    plan = [
        Relay(
            me,
            wires,
            wholes[which],
            piece,
            TURNED(number),
            source=shares[which].at[pl.ds(*piece[0]), pl.ds(*piece[1])],
        )
        for number, (which, piece) in enumerate(units)
    ]
    targets = [weights.at[here + (ALL, pl.ds(unit * UNIT, UNIT))] for unit in range(3)]
    targets += [whole.at[here] for whole in wholes]
    local = [
        pltpu.make_async_copy(source, target, own_sem.at[3 + number])
        for number, (source, target) in enumerate(zip((wq, wk, wv) + tuple(shares), targets))
    ]
    keep_weights = pltpu.make_async_copy(weights, qkv_out, own_sem.at[9])
    keep_vectors = pltpu.make_async_copy(vecs, vec_out, own_sem.at[10])
    moves = {}
    for number in range(len(units)):
        for stage, at in enumerate(SCHEDULE(number), 1):
            at = min(int(2 * at), 2 * main - 1) if at >= 0 else at
            moves.setdefault(at, []).append((plan[number], stage))

    def pace(at):
        for unit, stage in moves.get(at, []):
            unit.stage(stage)

    def front(tensor, *stages):
        for stage in stages:
            for unit in fronts[2 * tensor : 2 * tensor + 2]:
                unit.stage(stage)

    def project(tensor, column):
        for first in range(0, UNIT, 256):
            taken = weights[:, :, :, :, :, tensor * UNIT + first : tensor * UNIT + first + 256]
            found = jnp.dot(
                x_ref[...], taken.reshape(UNIT, 256), preferred_element_type=jnp.float32
            ).T
            if column is not None:
                bias = vecs[...].reshape(UNIT, vecs.shape[5])[first : first + 256]
                found = found + bias[:, column : column + 1].astype(jnp.float32)
            heads = first // HEAD_DIM, (first + 256) // HEAD_DIM
            qkv_ref[tensor, heads[0] : heads[1]] = found.astype(jnp.bfloat16).reshape(
                heads[1] - heads[0], HEAD_DIM, width
            )
        own = pl.ds(pl.multiple_of(spot(tensor, me.index) * width, width), width)
        land[tensor, :, own] = qkv_ref[tensor, me.index]

    def take_queries(start):
        part = land[0, :, pl.ds(pl.multiple_of(start, rows), rows)].astype(jnp.float32) * scale
        high = part.astype(jnp.bfloat16).astype(jnp.float32)
        return jnp.concatenate([high, part - high], 0).T.astype(jnp.bfloat16)

    def score(queries, at, store, piece, peak):
        found = jnp.dot(
            queries, keys[at, :, piece[0] : piece[1]], preferred_element_type=jnp.float32
        )
        store[:, piece[0] : piece[1]] = found
        for first in range(0, piece[1] - piece[0], 128):
            some = found[:, first : first + 128]
            peak = some if peak is None else jnp.maximum(peak, some)
        return peak

    def keep_peak(store, peak):
        store[...] = jnp.broadcast_to(jnp.max(peak, axis=1, keepdims=True), store.shape)

    def weigh(store, peak, piece, row, total):
        weights = jnp.exp2(store[:, piece[0] : piece[1]] - peak[:, :1]).astype(jnp.bfloat16)
        p_ref[row : row + rows, piece[0] : piece[1]] = weights
        term = lax.dot_general(
            values[side, :, piece[0] : piece[1]],
            weights,
            BY_LAST,
            preferred_element_type=jnp.float32,
        )
        return term if total is None else total + term

    @pl.when(step == 0)
    def _():
        for copy in local:
            copy.start()
        turned = jnp.concatenate(
            [vec_ref[...].astype(jnp.float32), jnp.zeros((112, 128), jnp.float32)], 0
        ).T
        vecs[here] = turned[:EDGE].astype(jnp.bfloat16)
        greet([me.peer(by)[1] for by in range(1, group)] + [me.at(x=1 - me.x)])
        vectors.stage(0)
        front(1, 0)
        for copy in local:
            copy.wait()
        vectors.stage(1)
        front(1, 1)
        front(2, 0)
        front(1, 2)
        front(0, 0)
        for unit in plan:
            unit.stage(0)
        vectors.stage(2)
        front(2, 1)
        pace(-5)
        front(1, 3)
        front(2, 2)
        vectors.stage(3)
        front(0, 1)
        pace(-4)
        front(1, 4)
        project(1, None)

        @pl.when(early)
        def _():
            for copy in swaps[1]:
                copy.start()

        pace(-3)
        front(2, 3)
        front(0, 2)
        vectors.stage(4)
        front(2, 4)
        project(2, 1)

        @pl.when(early)
        def _():
            for copy in swaps[2]:
                copy.start()

        front(0, 3)
        pace(-2)
        front(0, 4)
        keep_weights.start()
        keep_vectors.start()
        project(0, 0)
        for copy in swaps[0]:
            copy.start()

        @pl.when(jnp.logical_not(early))
        def _():
            for copy in swaps[1] + swaps[2]:
                copy.start()

        for at in (-1, -0.9, -0.8, -0.7, -0.6):
            pace(at)
        await_keys(0)
        await_from(0, block_at(0))
        queries, peak = take_queries(block_at(0) * width), None
        for piece in pieces:
            peak = score(queries, 0, s0, piece, peak)
        keep_peak(m0, peak)

    for at, todo in sorted((entry for entry in moves.items() if entry[0] >= 0), key=lambda entry: entry[0]):

        @pl.when(step == at)
        def _():
            for unit, stage in todo:
                unit.stage(stage)

    @pl.when(step == main - 1)
    def _():
        await_keys(1)

    next_step = jnp.minimum(step + 1, steps - 1)
    block = block_at(turn)
    later, later_side = block_at(lax.rem(next_step, main)), next_step // main
    place = pl.ds(pl.multiple_of(block * width, width), width)

    @pl.when(step < main - 1)
    def _():
        await_from(0, later)

    for half, (old, old_peak, new, new_peak) in enumerate(((s0, m0, s1, m1), (s1, m1, s0, m0))):
        queries = take_queries(block * width + rows if half == 0 else later * width)
        at = side if half == 0 else later_side
        total, peak = None, None
        for piece in pieces:
            total = weigh(old, old_peak, piece, half * rows, total)
            peak = score(queries, at, new, piece, peak)
        here = slice(half * rows, (half + 1) * rows)
        peaks[:, here] = old_peak[...].T[0:8]
        now[:, here] = total
        keep_peak(new_peak, peak)

    @pl.when(side == 0)
    def _():
        acc[:, place] = now[...]
        top[:, place] = peaks[...]

    @pl.when(side == 1)
    def _():
        first, second = top[0:1, place], peaks[0:1, :]
        peak = jnp.maximum(first, second)
        first, second = jnp.exp2(first - peak), jnp.exp2(second - peak)
        total = acc[:, place] * first + now[...] * second
        inverse = 1.0 / total[HEAD_DIM : HEAD_DIM + 1]
        o_ref[:, place] = (total[:HEAD_DIM] * inverse).astype(jnp.bfloat16)
        row = lax.broadcasted_iota(jnp.int32, (8, width), 0)
        inv_ref[:, place] = jnp.where(row == 0, first * inverse, second * inverse)
        send_block(block, turn, True)

    @pl.when(step == steps - 1)
    def _():
        for block in range(main, group):
            for tensor in range(3):
                await_from(tensor, block)
        keep.start()
        tail_keys = jnp.concatenate([land[1, :, long:], land[1, :, long:]], 0)
        tail_values = jnp.concatenate([land[2, :, long:], ones_row(tail)], 0)
        for first in range(0, tail, rows):
            queries = take_queries(long + first)
            found = jnp.dot(queries, tail_keys, preferred_element_type=jnp.float32)
            allowed = down_ref[first : first + rows, :1] == across_ref[:1, :]
            found = jnp.where(allowed, found, -1e30)
            peak = jnp.max(found, axis=1, keepdims=True)
            weights = jnp.exp2(found - peak).astype(jnp.bfloat16)
            tail_ref[first : first + rows, :] = weights
            total = lax.dot_general(
                tail_values, weights, BY_LAST, preferred_element_type=jnp.float32
            )
            here = slice(long + first, long + first + rows)
            inverse = 1.0 / total[HEAD_DIM : HEAD_DIM + 1]
            o_ref[:, here] = (total[:HEAD_DIM] * inverse).astype(jnp.bfloat16)
            inv_ref[:, here] = jnp.broadcast_to(inverse, (8, rows))
            if (first + rows) % width == 0:
                number = main + first // width
                send_block(number, number, True)
        for unit in plan:
            unit.stage(6)
        for copy in swaps[0] + swaps[1] + swaps[2]:
            copy.wait_send()
        keep_weights.wait()
        keep_vectors.wait()
        for number in range(main):
            send_block(block_at(number), number, False)
        for number in range(main, group):
            send_block(number, number, False)
        for ahead_by in range(1, group):
            source, device = me.peer(ahead_by)
            wire(
                lanes(o_ref, (ALL,), source * width, width),
                tokens_ref.at[source],
                o_send.at[0],
                o_recv.at[ahead_by],
                device,
            ).wait_recv()
        keep.wait()


def once(shape):
    return pl.BlockSpec(shape, lambda step: (0,) * len(shape), pipeline_mode=pl.Buffered(1))


def attn_fwd(x, vec, seg, fronts, shares, collective_id, cols=1024):
    seqs, blks, heads = (lax.axis_size(name) for name in EVERY)
    lead = (seqs, blks, heads // 2, 2)
    group, width = blks * heads, x.shape[0]
    rows = width // 2
    length = group * width
    tail = seg.shape[0]
    long = length - tail
    main = long // width
    down = jnp.broadcast_to(seg[:, None], (tail, 128))
    across = jnp.broadcast_to(seg[None, :], (8, tail))
    anywhere = pl.BlockSpec(memory_space=pl.ANY)
    count = len(weight_units([share.shape for share in shares])) if shares else 0
    wires = Gather.WIRES * (count + 7)
    kept = jax.ShapeDtypeStruct((3, HEAD_DIM, length), jnp.bfloat16)
    gathered = jax.ShapeDtypeStruct(lead + (EDGE, 3 * UNIT), jnp.bfloat16)
    vectors = jax.ShapeDtypeStruct(lead + (EDGE, 128), jnp.bfloat16)
    pair = [pltpu.SemaphoreType.DMA((group,))] * 2
    return pl.pallas_call(
        functools.partial(attn_fwd_kernel, blks, rows, cols, len(shares)),
        grid=(2 * (long // width),),
        in_specs=[once(x.shape), once(vec.shape), once((tail, 128)), once((8, tail))]
        + [once(share.shape) for share in fronts + shares],
        out_specs=[
            pl.BlockSpec((width, long // 2), lambda step: (lax.rem(step, main), step // main)),
            once((tail, tail)),
            once((HEAD_DIM, length)),
            once((8, length)),
        ]
        + [anywhere] * (4 + len(shares)),
        out_shape=[
            jax.ShapeDtypeStruct((long, long), jnp.bfloat16),
            jax.ShapeDtypeStruct((tail, tail), jnp.bfloat16),
            jax.ShapeDtypeStruct((HEAD_DIM, length), jnp.bfloat16),
            jax.ShapeDtypeStruct((8, length), jnp.float32),
            kept,
            jax.ShapeDtypeStruct((group, HEAD_DIM, width), jnp.bfloat16),
            gathered,
            vectors,
        ]
        + [jax.ShapeDtypeStruct(lead + share.shape, share.dtype) for share in shares],
        scratch_shapes=[
            pltpu.VMEM(gathered.shape, gathered.dtype),
            pltpu.VMEM(vectors.shape, vectors.dtype),
            pltpu.VMEM((3, group, HEAD_DIM, width), jnp.bfloat16),
            pltpu.VMEM(kept.shape, kept.dtype),
            pltpu.VMEM((2, 2 * HEAD_DIM, long // 2), jnp.bfloat16),
            pltpu.VMEM((2, HEAD_DIM + 16, long // 2), jnp.bfloat16),
            pltpu.VMEM((rows, long // 2), jnp.float32),
            pltpu.VMEM((rows, long // 2), jnp.float32),
            pltpu.VMEM((rows, 128), jnp.float32),
            pltpu.VMEM((rows, 128), jnp.float32),
            pltpu.VMEM((HEAD_DIM + 16, width), jnp.float32),
            pltpu.VMEM((8, width), jnp.float32),
            pltpu.VMEM((HEAD_DIM + 16, long), jnp.float32),
            pltpu.VMEM((8, long), jnp.float32),
            pltpu.SemaphoreType.DMA((11,)),
            pltpu.SemaphoreType.DMA((2 * group,)),
            pltpu.SemaphoreType.DMA((2 * group,)),
            *pair,
            *pair,
            pltpu.SemaphoreType.DMA((wires,)),
            pltpu.SemaphoreType.DMA((wires,)),
        ],
        compiler_params=pltpu.CompilerParams(
            collective_id=collective_id, has_side_effects=True, vmem_limit_bytes=62 * 2**20
        ),
        cost_estimate=pl.CostEstimate(
            flops=4 * long * long * HEAD_DIM,
            bytes_accessed=2 * long * long,
            transcendentals=long * long,
        ),
        name="attn_fwd",
    )(x, vec, down, across, *fronts, *shares)


def attn_bwd_kernel(
    blks, rows, cols, count, *refs
):
    p_ref, tail_ref, qkv_ref, o_ref, inv_ref, grads_ref = refs[:6]
    partials, refs = refs[6 : 6 + count], refs[6 + count :]
    dkv_ref, tokens_ref, kv_tokens = refs[:3]
    totals, refs = refs[3 : 3 + count], refs[3 + count :]
    (
    land, dq_out, dq_sum, keys, values, dk_sum, dv_sum, tail_dkv, early_dkv, own, r0, r1a, r1b, r2, r3, send, recv,
    own_sem, do_send, do_recv, dq_send, dq_recv, kv_send, kv_recv,
    ) = refs
    step, steps = pl.program_id(0), pl.num_programs(0)
    length, part = land.shape[1], p_ref.shape[1]
    long = 2 * part
    tail, pieces = length - long, cuts(part, cols)
    main = long // rows
    side, turn = step // main, lax.rem(step, main)
    scale = HEAD_DIM**-0.5

    me = Place(blks)
    group = me.group

    def block_at(turn):
        return lax.rem(lax.rem(me.index, main) + turn, main)

    do_copies = []
    for ahead_by in range(1, group):
        peer, device = me.peer(group - ahead_by)
        do_copies.append(
            wire(
                grads_ref.at[peer],
                lanes(land, (ALL,), me.index * rows, rows),
                do_send.at[ahead_by],
                do_recv.at[ahead_by],
                device,
            )
        )
    own_in = pltpu.make_async_copy(
        grads_ref.at[me.index], lanes(land, (ALL,), me.index * rows, rows), own_sem.at[2]
    )

    def await_grads(block):
        @pl.when(block != me.index)
        def _():
            wire(
                grads_ref.at[block],
                lanes(land, (ALL,), block * rows, rows),
                do_send.at[0],
                do_recv.at[lax.rem(block + group - me.index, group)],
                me.member(block),
            ).wait_recv()

    def send_block(block, slot, start):
        source = lanes(dq_out, (ALL,), block * rows, rows)
        remote = wire(
            source,
            tokens_ref.at[me.index],
            dq_send.at[slot],
            dq_recv.at[lax.rem(me.index + group - block, group)],
            me.member(block),
        )
        local = pltpu.make_async_copy(source, tokens_ref.at[me.index], own_sem.at[3])

        @pl.when(block != me.index)
        def _():
            if start:
                remote.start()
            else:
                remote.wait_send()

        @pl.when(block == me.index)
        def _():
            if start:
                local.start()
            else:
                local.wait()

    early = (me.index >= main) | (lax.rem(me.index, 2) == 0)

    def early_sends():
        for number in range(main // 2):
            block = 2 * lax.rem(number + me.index // 2, main // 2)
            yield number, block, lanes(early_dkv, (ALL, ALL), block // 2 * rows, rows)
        for block in range(main, group):
            source = tail_dkv.at[:, :, pl.ds((block - main) * rows, rows)]
            yield main // 2 + block - main, block, source

    def send_early(start):
        for slot, block, source in early_sends():
            remote = wire(
                source,
                kv_tokens.at[:, me.index],
                kv_send.at[slot],
                kv_recv.at[lax.rem(me.index + group - block, group)],
                me.member(block),
            )
            local = pltpu.make_async_copy(source, kv_tokens.at[:, me.index], own_sem.at[4])

            @pl.when(block != me.index)
            def _():
                if start:
                    remote.start()
                else:
                    remote.wait_send()

            @pl.when(block == me.index)
            def _():
                if start:
                    local.start()
                else:
                    local.wait()

    wires = Wires(send, recv)
    units = weight_units([partial.shape[4:] for partial in partials])
    plan, moves = [], {}
    for number, (which, piece) in enumerate(units):
        turned = number % 2 == 1
        unit = Reduce(
            me,
            wires,
            partials[which],
            piece,
            turned,
            own.at[number % 2],
            own_sem.at[number % 2],
            r0.at[number],
            (r1b if turned else r1a).at[number // 2],
            r2.at[number],
            r3.at[number],
            totals[which],
            piece,
        )
        plan.append(unit)
        pair = number // 2
        for stage, at in enumerate((1.5 * pair, 1.5 * pair, 1.5 * pair + 1, 2 * pair + 4, 2 * pair + 6)):
            moves.setdefault(min(int(2 * at), 2 * main - 1), []).append((stage, number, unit))

    def prepare(start, width, at):
        place = pl.ds(pl.multiple_of(start, width), width)
        grads = land[:, place].astype(jnp.float32)
        inverse = jnp.where(at == 0, inv_ref[0:1, place], inv_ref[1:2, place])
        delta = -jnp.sum(grads * o_ref[:, place].astype(jnp.float32), axis=0, keepdims=True)
        delta = delta * inverse
        high = delta.astype(jnp.bfloat16).astype(jnp.float32)
        row = lax.broadcasted_iota(jnp.int32, (16, width), 0)
        extra = jnp.where(row == 0, high, jnp.where(row == 1, delta - high, 0.0))
        grads = grads * inverse
        wide = jnp.concatenate([grads, extra], 0).T.astype(jnp.bfloat16)
        return wide, grads.astype(jnp.bfloat16), qkv_ref[0, :, place]

    def terms(wide, grads, queries, weights, keys_here, values_here, dq):
        dp = jnp.dot(wide, values_here, preferred_element_type=jnp.float32)
        ds = (weights.astype(jnp.float32) * dp).astype(jnp.bfloat16)
        dv = jnp.dot(grads, weights, preferred_element_type=jnp.float32)
        dk = jnp.dot(queries, ds, preferred_element_type=jnp.float32)
        term = lax.dot_general(keys_here, ds, BY_LAST, preferred_element_type=jnp.float32)
        return (term if dq is None else dq + term), dk, dv

    def ones_rows(columns):
        return (
            (lax.broadcasted_iota(jnp.int32, (16, columns), 0) < 2)
            .astype(jnp.float32)
            .astype(jnp.bfloat16)
        )

    @pl.when(step == 0)
    def _():
        own_in.start()
        greet([me.peer(by)[1] for by in range(1, group)] + [me.at(x=1 - me.x)])
        for copy in do_copies:
            copy.start()

    for at, todo in sorted(moves.items()):

        @pl.when(step == at)
        def _():
            for stage, number, unit in sorted(todo, key=lambda entry: (-entry[0], entry[1])):
                unit.stage(stage)

    @pl.when(step == 0)
    def _():
        for at in range(2):
            here = slice(at * part, (at + 1) * part)
            keys[at] = qkv_ref[1, :, here]
            values[at, 0:HEAD_DIM, :] = qkv_ref[2, :, here]
            values[at, HEAD_DIM:, :] = ones_rows(part)
        dk_sum[...] = jnp.zeros_like(dk_sum)
        dv_sum[...] = jnp.zeros_like(dv_sum)
        own_in.wait()

    block = block_at(turn)
    place = pl.ds(pl.multiple_of(block * rows, rows), rows)

    @pl.when(side == 0)
    def _():
        await_grads(block)

    wide, grads, queries = prepare(block * rows, rows, side)
    dq = None
    for first, end in pieces:
        dq, dk, dv = terms(
            wide,
            grads,
            queries,
            p_ref[:, first:end],
            keys[side, :, first:end],
            values[side, :, first:end],
            dq,
        )
        dk_sum[side, :, first:end] += dk
        dv_sum[side, :, first:end] += dv

    @pl.when(side == 0)
    def _():
        dq_sum[:, place] = dq

    @pl.when(side == 1)
    def _():
        dq_out[:, place] = ((dq_sum[:, place] + dq) * scale).astype(jnp.bfloat16)
        send_block(block, turn, True)

    @pl.when(step == main - 1)
    def _():
        tail_keys = qkv_ref[1, :, long:]
        tail_values = jnp.concatenate([qkv_ref[2, :, long:], ones_rows(tail)], 0)
        dk_total, dv_total = None, None
        for number in range(main, group):
            await_grads(number)
            first = (number - main) * rows
            wide, grads, queries = prepare(long + first, rows, 0)
            dq, dk, dv = terms(
                wide,
                grads,
                queries,
                tail_ref[first : first + rows, :],
                tail_keys,
                tail_values,
                None,
            )
            dk_total = dk if dk_total is None else dk_total + dk
            dv_total = dv if dv_total is None else dv_total + dv
            dq_out[:, long + first : long + first + rows] = (dq * scale).astype(jnp.bfloat16)
            send_block(number, number, True)
        tail_dkv[0] = (dk_total * scale).astype(jnp.bfloat16)
        tail_dkv[1] = dv_total.astype(jnp.bfloat16)
        early_dkv[0] = (dk_sum[0] * scale).astype(jnp.bfloat16)
        early_dkv[1] = dv_sum[0].astype(jnp.bfloat16)
        send_early(True)

    @pl.when(step == steps - 1)
    def _():
        dkv_ref[0] = (dk_sum[1] * scale).astype(jnp.bfloat16)
        dkv_ref[1] = dv_sum[1].astype(jnp.bfloat16)
        for unit in plan:
            unit.stage(5)
        for copy in do_copies:
            copy.wait_send()
        for number in range(main):
            send_block(block_at(number), number, False)
        for number in range(main, group):
            send_block(number, number, False)
        send_early(False)
        for ahead_by in range(1, group):
            source, device = me.peer(ahead_by)
            wire(
                lanes(dq_out, (ALL,), source * rows, rows),
                tokens_ref.at[source],
                dq_send.at[0],
                dq_recv.at[ahead_by],
                device,
            ).wait_recv()

        @pl.when(early)
        def _():
            for ahead_by in range(1, group):
                source, device = me.peer(ahead_by)
                wire(
                    tail_dkv.at[:, :, pl.ds(0, rows)],
                    kv_tokens.at[:, source],
                    kv_send.at[0],
                    kv_recv.at[ahead_by],
                    device,
                ).wait_recv()


def attn_bwd(
    probs, tail_probs, kept, attn, inv_total, grad_attn, long, partials, collective_id, cols=1024
):
    blks = lax.axis_size("blk")
    lead = (lax.axis_size("seq"), blks, lax.axis_size("head") // 2, 2)
    devices = math.prod(lead)
    length = kept.shape[2]
    tail = length - long
    group, _, rows = grad_attn.shape
    main, part = long // rows, long // 2
    anywhere = pl.BlockSpec(memory_space=pl.ANY)
    edges = [(partial.shape[0] // devices, partial.shape[1]) for partial in partials]
    units = len(weight_units(edges))
    pair = [pltpu.SemaphoreType.DMA((group,))] * 2
    return pl.pallas_call(
        functools.partial(attn_bwd_kernel, blks, rows, cols, len(partials)),
        grid=(2 * main,),
        in_specs=[
            pl.BlockSpec((rows, part), lambda step: (lax.rem(step, main), step // main)),
            once((tail, tail)),
            once(kept.shape),
            once((HEAD_DIM, length)),
            once((8, length)),
        ]
        + [anywhere] * (1 + len(partials)),
        out_specs=[once((2, HEAD_DIM, part)), anywhere, anywhere] + [once(edge) for edge in edges],
        out_shape=[
            jax.ShapeDtypeStruct((2, HEAD_DIM, part), jnp.bfloat16),
            jax.ShapeDtypeStruct((group, HEAD_DIM, rows), jnp.bfloat16),
            jax.ShapeDtypeStruct((2, group, HEAD_DIM, rows), jnp.bfloat16),
        ]
        + [jax.ShapeDtypeStruct(edge, jnp.float32) for edge in edges],
        scratch_shapes=[
            pltpu.VMEM((HEAD_DIM, length), jnp.bfloat16),
            pltpu.VMEM((HEAD_DIM, length), jnp.bfloat16),
            pltpu.VMEM((HEAD_DIM, long), jnp.float32),
            pltpu.VMEM((2, HEAD_DIM, part), jnp.bfloat16),
            pltpu.VMEM((2, HEAD_DIM + 16, part), jnp.bfloat16),
            pltpu.VMEM((2, HEAD_DIM, part), jnp.float32),
            pltpu.VMEM((2, HEAD_DIM, part), jnp.float32),
            pltpu.VMEM((2, HEAD_DIM, tail), jnp.bfloat16),
            pltpu.VMEM((2, HEAD_DIM, part), jnp.bfloat16),
            pltpu.VMEM((2, 2, blks, 2, EDGE, UNIT), jnp.bfloat16),
            *reduce_scratch(max(units, 2), blks),
            pltpu.SemaphoreType.DMA((5,)),
            *pair,
            *pair,
            *pair,
        ],
        compiler_params=pltpu.CompilerParams(
            collective_id=collective_id, has_side_effects=True, vmem_limit_bytes=62 * 2**20
        ),
        cost_estimate=pl.CostEstimate(
            flops=8 * long * long * HEAD_DIM, bytes_accessed=2 * long * long, transcendentals=0
        ),
        name="attn_bwd",
    )(
        probs, tail_probs, kept, attn, inv_total, grad_attn,
        *[partial.reshape(lead + edge) for partial, edge in zip(partials, edges)],
    )


def last_kernel(
    blks, devices, dkv_ref, kv_tokens, dq_ref, x_ref, w_ref, base_ref, sums_ref,
    dw_out, dx_out, sums_out,
    grads, x, xt, weights, base, turned_dx, partial, bias, landed,
    r0, r1a, r1b, r2, r3, send, recv,
    own_sem, kv_send, kv_recv, sums_send, sums_recv,
):
    me = Place(blks)
    group = me.group
    width = x.shape[0]
    depth = x.shape[1]
    index, others = me.others(devices)
    loads = [
        pltpu.make_async_copy(source, target, own_sem.at[number])
        for number, (source, target) in enumerate(
            (
                (x_ref, x),
                (dq_ref, grads.at[0]),
                (w_ref, weights),
                (base_ref, base),
                (sums_ref, bias),
            )
        )
    ]
    for copy in loads:
        copy.start()
    greet(others)
    main = 2 * (dkv_ref.shape[2] // width)
    odd = (me.index < main) & (lax.rem(me.index, 2) == 1)

    def late_sends(which, start):
        for number in range(main // 2):
            block = 2 * lax.rem(number + me.index // 2, main // 2) + 1
            source = lanes(dkv_ref, (which, ALL), block // 2 * width, width)
            remote = wire(
                source,
                grads.at[which + 1, me.index],
                kv_send.at[which * group + number],
                kv_recv.at[which * group + lax.rem(me.index + group - block, group)],
                me.member(block),
            )
            local = pltpu.make_async_copy(
                source, grads.at[which + 1, me.index], own_sem.at[5 + which]
            )

            @pl.when(block != me.index)
            def _():
                if start:
                    remote.start()
                else:
                    remote.wait_send()

            if start:

                @pl.when(block == me.index)
                def _():
                    local.start()

    def await_late(which):
        @pl.when(odd)
        def _():
            pltpu.make_async_copy(
                dkv_ref.at[which, :, pl.ds(0, width)],
                grads.at[which + 1, me.index],
                own_sem.at[5 + which],
            ).wait()
            for ahead_by in range(1, group):
                source, device = me.peer(ahead_by)
                wire(
                    dkv_ref.at[which, :, pl.ds(0, width)],
                    grads.at[which + 1, source],
                    kv_send.at[0],
                    kv_recv.at[which * group + ahead_by],
                    device,
                ).wait_recv()

        @pl.when(jnp.logical_not(odd))
        def _():
            pltpu.make_async_copy(
                kv_tokens.at[pl.ds(which, 1)],
                grads.at[pl.ds(which + 1, 1)],
                own_sem.at[5 + which],
            ).wait()

    for which in range(2):
        late_sends(which, True)

        @pl.when(jnp.logical_not(odd))
        def _():
            pltpu.make_async_copy(
                kv_tokens.at[pl.ds(which, 1)],
                grads.at[pl.ds(which + 1, 1)],
                own_sem.at[5 + which],
            ).start()

    wires = Wires(send, recv)
    plan = []
    for number in range(6):
        tensor, half = number // 2, number % 2
        plan.append(
            Reduce(
                me,
                wires,
                partial.at[tensor],
                ((0, EDGE), (half * UNIT // 2, UNIT // 2)),
                half == 1,
                None,
                None,
                r0.at[number],
                (r1b if half else r1a).at[tensor],
                r2.at[number],
                r3.at[number],
                dw_out,
                ((0, EDGE), (tensor * UNIT + half * UNIT // 2, UNIT // 2)),
            )
        )

    def work(tensor):
        taken = grads[tensor].reshape(depth, width)
        for first in range(0, depth, 256):
            term = lax.dot_general(
                xt[first : first + 256, :], taken, BY_LAST, preferred_element_type=jnp.float32
            ).astype(jnp.bfloat16)
            for share in range(first // EDGE, (first + 256) // EDGE):
                at = (share // (blks * 4), share // 4 % blks, share // 2 % 2, share % 2)
                partial[(tensor,) + at] = term[share * EDGE - first : (share + 1) * EDGE - first]
        for unit in plan[2 * tensor : 2 * tensor + 2]:
            unit.stage(0)

    def work_input(tensor):
        taken = grads[tensor].reshape(depth, width)
        for first in range(0, depth, 256):
            term = jnp.dot(
                weights[first : first + 256, tensor * depth : (tensor + 1) * depth],
                taken,
                preferred_element_type=jnp.float32,
            )
            if tensor == 0:
                turned_dx[first : first + 256, :] = term
            elif tensor == 1:
                turned_dx[first : first + 256, :] += term
            else:
                total = turned_dx[first : first + 256, :] + term
                dx_out[:, first : first + 256] = base[:, first : first + 256] + total.T

    def stages(tensor, *which):
        for stage in which:
            for unit in plan[2 * tensor : 2 * tensor + 2]:
                unit.stage(stage)

    def note_bias(tensor, row):
        ones = jnp.ones((8, width), jnp.bfloat16)
        found = lax.dot_general(
            ones, grads[tensor].reshape(depth, width), BY_LAST, preferred_element_type=jnp.float32
        )
        per = 128 * devices // depth
        for owner in range(devices):
            first = owner // per * 128
            bias[owner, row : row + 1, :] = found[:1, first : first + 128]

    loads[0].wait()
    xt[...] = x[...].astype(jnp.float32).T.astype(jnp.bfloat16)
    loads[1].wait()
    work(0)
    stages(0, 2)
    loads[4].wait()
    note_bias(0, 3)
    loads[2].wait()
    work_input(0)
    stages(0, 3)
    await_late(0)
    work(1)
    stages(0, 4)
    stages(1, 2)
    work_input(1)
    stages(1, 3)
    await_late(1)
    work(2)
    note_bias(2, 4)
    small = []
    for slot, device in enumerate(others):
        peer = (device["seq"] * blks + device["blk"]) * 4 + device["head"]
        copy = wire(
            bias.at[peer], landed.at[slot], sums_send.at[slot], sums_recv.at[slot], device
        )
        small.append(copy)
    stages(2, 2)
    for copy in small:
        copy.start()
    stages(1, 4)
    loads[3].wait()
    work_input(2)
    stages(2, 3)
    stages(0, 5)
    stages(2, 4)
    for copy in small:
        copy.wait()
    sums_out[...] = jnp.sum(landed[...], axis=0) + bias[index]
    stages(1, 5)
    stages(2, 5)
    for which in range(2):
        late_sends(which, False)


def last_reduce(dkv, kv_tokens, dq, x, w_qkv, base, sums, collective_id):
    seqs, blks, heads = (lax.axis_size(name) for name in EVERY)
    devices = seqs * blks * heads
    group = blks * heads
    width, depth = x.shape
    half = UNIT // 2
    return pl.pallas_call(
        functools.partial(last_kernel, blks, devices),
        out_shape=[
            jax.ShapeDtypeStruct((EDGE, 3 * depth), jnp.float32),
            jax.ShapeDtypeStruct((width, depth), jnp.float32),
            jax.ShapeDtypeStruct(sums.shape[1:], jnp.float32),
        ],
        in_specs=[pl.BlockSpec(memory_space=pl.ANY)] * 7,
        out_specs=[pl.BlockSpec(memory_space=pltpu.VMEM)] * 3,
        scratch_shapes=[
            pltpu.VMEM((3, group, HEAD_DIM, width), jnp.bfloat16),
            pltpu.VMEM((width, depth), jnp.bfloat16),
            pltpu.VMEM((depth, width), jnp.bfloat16),
            pltpu.VMEM((depth, 3 * depth), jnp.bfloat16),
            pltpu.VMEM((width, depth), jnp.float32),
            pltpu.VMEM((depth, width), jnp.float32),
            pltpu.VMEM((3, seqs, blks, heads // 2, 2, EDGE, UNIT), jnp.bfloat16),
            pltpu.VMEM(sums.shape, jnp.float32),
            pltpu.VMEM((devices - 1,) + sums.shape[1:], jnp.float32),
            *reduce_scratch(6, blks, half),
            pltpu.SemaphoreType.DMA((7,)),
            pltpu.SemaphoreType.DMA((2 * group,)),
            pltpu.SemaphoreType.DMA((2 * group,)),
            pltpu.SemaphoreType.DMA((devices,)),
            pltpu.SemaphoreType.DMA((devices,)),
        ],
        compiler_params=pltpu.CompilerParams(
            collective_id=collective_id, has_side_effects=True, vmem_limit_bytes=56 * 2**20
        ),
        name="last_reduce",
    )(dkv, kv_tokens, dq, x, w_qkv, base, sums)


def tail_segments(doc_lengths, first, rows):
    return segment_ids(doc_lengths, first + lax.iota(jnp.int32, rows))


BESIDE = ()


AFTER = ()


def shards_heads(
    layer_input,
    weight_query,
    weight_key,
    weight_value,
    weight_output,
    weight_expand,
    weight_reduce,
    bias_query,
    bias_value,
    bias_output,
    bias_expand,
    bias_reduce,
    first_gain,
    first_shift,
    second_gain,
    second_shift,
    cotangent,
    doc_lengths,
):
    tok_rows, model_width = layer_input.shape[1:]
    head_count = lax.axis_size("head")
    blk_count = lax.axis_size("blk")
    count = head_count * blk_count
    seq_len = tok_rows * count
    long_rows = seq_len - seq_len // blk_count // 2
    flat_rows = layer_input.reshape(tok_rows, model_width)

    vectors = (
        bias_query,
        bias_value,
        bias_output,
        bias_reduce,
        first_gain,
        first_shift,
        second_gain,
        second_shift,
        bias_expand,
    )
    sizes = [vector.shape[0] for vector in vectors]
    lane = 128
    rows = [vector.reshape(1, -1) for vector in vectors[:-1]] + [bias_expand.reshape(-1, sizes[0])]
    vec, at = jnp.zeros((16, lane), layer_input.dtype), 0
    for row in rows:
        count_here = row.shape[0]
        vec = vec + jnp.pad(row, ((at, 16 - at - count_here), (0, lane - sizes[0])))
        at = at + count_here
    seg = tail_segments(doc_lengths, long_rows, seq_len - long_rows)[0]
    rest = (weight_output, weight_expand, weight_reduce)
    beside = {which: lax.all_gather(rest[which], EVERY, axis=0, tiled=True) for which in BESIDE}
    (
        probs, tail_probs, attn, inv_total, kept, attn_flat, w_qkv, vec, *wholes,
    ) = attn_fwd(
        flat_rows,
        vec,
        seg,
        (weight_query, weight_key, weight_value),
        tuple(share for which, share in enumerate(rest) if which not in BESIDE),
        5,
    )
    attn_flat = attn_flat.reshape(model_width, tok_rows)
    w_qkv = w_qkv.reshape(model_width, 3 * model_width)
    vec = vec.reshape(-1, sizes[0], lane)[:, :, :16].transpose(2, 0, 1).astype(jnp.float32)
    _, _, b_output, b_reduce, gain_one, shift_one, gain_two, shift_two = [
        vec[number].reshape(-1) for number in range(8)
    ]
    b_expand = vec[8:at].transpose(1, 0, 2).reshape(-1)
    w_output, w_expand, w_reduce = [
        beside[which] if which in BESIDE else wholes.pop(0).reshape(-1, share.shape[1])
        for which, share in enumerate(rest)
    ]

    resid_one = flat_rows.astype(jnp.float32) + left_dot(attn_flat, w_output) + b_output
    normed_one, norm_one_pull = jax.vjp(layer_norm, resid_one, gain_one, shift_one)
    normed_low = normed_one.astype(jnp.bfloat16)
    pre_act = plain_dot(normed_low, w_expand) + b_expand
    hidden_f32, gelu_pull = jax.vjp(gelu_curve, pre_act)
    hidden = hidden_f32.astype(jnp.bfloat16)
    resid_two = normed_one + plain_dot(hidden, w_reduce) + b_reduce
    result, norm_two_pull = jax.vjp(layer_norm, resid_two, gain_two, shift_two)
    layer_output = result.astype(jnp.bfloat16).reshape(layer_input.shape)
    tok_first = (lax.axis_index("blk") * head_count + lax.axis_index("head")) * tok_rows
    tok_seg = segment_ids(doc_lengths, tok_first + lax.iota(jnp.int32, tok_rows))
    live = (tok_seg > 0).astype(jnp.float32)
    grad_out = (cotangent.astype(jnp.float32) * live[..., None]).reshape(-1, model_width)
    grad_resid_two, grad_gain_two, grad_shift_two = norm_two_pull(grad_out)
    grad_ffn = grad_resid_two.astype(jnp.bfloat16)
    grad_w_reduce = left_dot(hidden, grad_ffn)
    grad_b_reduce = jnp.sum(grad_ffn.astype(jnp.float32), axis=0)
    (grad_pre,) = gelu_pull(right_dot(grad_ffn, w_reduce))
    grad_pre = grad_pre.astype(jnp.bfloat16)
    grad_w_expand = left_dot(normed_low, grad_pre)
    grad_b_expand = jnp.sum(grad_pre.astype(jnp.float32), axis=0)
    grad_normed = grad_resid_two + right_dot(grad_pre, w_expand)
    grad_resid_one, grad_gain_one, grad_shift_one = norm_one_pull(grad_normed)
    grad_branch = grad_resid_one.astype(jnp.bfloat16)
    grad_w_output = plain_dot(attn_flat, grad_branch)
    grad_b_output = jnp.sum(grad_branch.astype(jnp.float32), axis=0)
    grad_attn = right_dot(w_output, grad_branch).astype(jnp.bfloat16)
    grad_attn = grad_attn.reshape(HEADS, HEAD_DIM, tok_rows)

    grads = [grad.astype(jnp.bfloat16) for grad in (grad_w_output, grad_w_expand, grad_w_reduce)]
    beside = {
        which: lax.psum_scatter(grads[which], EVERY, scatter_dimension=0, tiled=True).astype(
            jnp.float32
        )
        for which in AFTER
    }
    grad_kv, grad_query, kv_tokens, *totals = attn_bwd(
        probs,
        tail_probs,
        kept,
        attn,
        inv_total,
        grad_attn,
        long_rows,
        [grad for which, grad in enumerate(grads) if which not in AFTER],
        6,
    )
    grad_w_output, grad_w_expand, grad_w_reduce = [
        beside[which] if which in AFTER else totals.pop(0) for which in range(3)
    ]

    sums = (
        jnp.zeros_like(b_output),
        jnp.zeros_like(b_output),
        grad_b_output,
        grad_b_reduce,
        grad_gain_one,
        grad_shift_one,
        grad_gain_two,
        grad_shift_two,
        grad_b_expand,
    )
    sums = jnp.concatenate([term.reshape(-1, size) for term, size in zip(sums, sizes)], axis=1)
    sums = jnp.pad(sums, ((0, 0), (0, 8 * lane - sums.shape[1]))).reshape(-1, 8, lane)
    grad_w_qkv, grad_input, sums = last_reduce(
        grad_kv, kv_tokens, grad_query, flat_rows, w_qkv, grad_resid_one, sums, 7
    )
    owner = (lax.axis_index("seq") * blk_count + lax.axis_index("blk")) * head_count
    owner = owner + lax.axis_index("head")
    within = lax.rem(owner, lane // sizes[0]) * sizes[0]
    g_query = lax.dynamic_slice_in_dim(sums[3], within, sizes[0])
    g_value = lax.dynamic_slice_in_dim(sums[4], within, sizes[1])
    sums = sums.reshape(-1)
    parts, start = [], 0
    for size in sizes:
        parts.append(sums[start : start + size])
        start += size
    g_output, g_reduce, g_gain_one, g_shift_one, g_gain_two, g_shift_two, g_expand = parts[2:]
    return (
        layer_output,
        grad_input.reshape(layer_input.shape),
        grad_w_qkv[:, :model_width],
        grad_w_qkv[:, model_width : 2 * model_width],
        grad_w_qkv[:, 2 * model_width :],
        grad_w_output,
        grad_w_expand,
        grad_w_reduce,
        g_query,
        g_value,
        g_output,
        g_expand,
        g_reduce,
        g_gain_one,
        g_shift_one,
        g_gain_two,
        g_shift_two,
    )


def solution(mesh):
    placed = (
        P("seq", ("blk", "head"), None),
        P(("seq", "blk", "head"), None),
        P(("seq", "blk", "head"), None),
        P(("seq", "blk", "head"), None),
        P(("seq", "blk", "head"), None),
        P(("seq", "blk", "head"), None),
        P(("seq", "blk", "head"), None),
        P(("seq", "blk", "head")),
        P(("seq", "blk", "head")),
        P(("seq", "blk", "head")),
        P(("seq", "blk", "head")),
        P(("seq", "blk", "head")),
        P(("seq", "blk", "head")),
        P(("seq", "blk", "head")),
        P(("seq", "blk", "head")),
        P(("seq", "blk", "head")),
        P("seq", ("blk", "head"), None),
        P("seq", None),
    )
    group = mesh.shape["blk"] * mesh.shape["head"]
    body = shards_heads if group == HEADS else shards_general
    return jax.shard_map(
        body,
        mesh=mesh,
        in_specs=placed,
        out_specs=(
            P("seq", ("blk", "head"), None),
            P("seq", ("blk", "head"), None),
            P(("seq", "blk", "head"), None),
            P(("seq", "blk", "head"), None),
            P(("seq", "blk", "head"), None),
            P(("seq", "blk", "head"), None),
            P(("seq", "blk", "head"), None),
            P(("seq", "blk", "head"), None),
            P(("seq", "blk", "head")),
            P(("seq", "blk", "head")),
            P(("seq", "blk", "head")),
            P(("seq", "blk", "head")),
            P(("seq", "blk", "head")),
            P(("seq", "blk", "head")),
            P(("seq", "blk", "head")),
            P(("seq", "blk", "head")),
            P(("seq", "blk", "head")),
        ),
        check_vma=False,
    )
```

```python
import functools
import math

import jax
import jax.numpy as jnp
from jax import lax
from jax.experimental import pallas as pl
from jax.experimental.pallas import tpu as pltpu
from jax.sharding import PartitionSpec as P

HEADS = 16
HEAD_DIM = 64


NORM_EPS = 1e-05
INV_ROOT2 = 0.7071067811865476


def segment_ids(doc_lengths, positions):
    ends = jnp.cumsum(doc_lengths, axis=-1)
    counted = jnp.sum((ends[:, None, :] <= positions[None, :, None]).astype(jnp.int32), axis=-1)
    return jnp.where(positions[None, :] < ends[:, -1:], counted + 1, 0)


def layer_norm(values, gain, shift):
    center = values - jnp.mean(values, axis=-1, keepdims=True)
    spread = jnp.mean(center * center, axis=-1, keepdims=True)
    return center * lax.rsqrt(spread + NORM_EPS) * gain + shift


def gelu_curve(values):
    return 0.5 * values * (1.0 + lax.erf(values * INV_ROOT2))


def plain_dot(left, right):
    return jnp.dot(left, right, preferred_element_type=jnp.float32)


def left_dot(left, right):
    return lax.dot_general(
        left, right, (((0,), (0,)), ((), ())), preferred_element_type=jnp.float32
    )


def right_dot(left, right):
    return lax.dot_general(
        left, right, (((1,), (1,)), ((), ())), preferred_element_type=jnp.float32
    )


def score_grads(scores, allowed, grad_part, value_part, lse_part, delta_part):
    probs = jnp.where(allowed, jnp.exp(scores - lse_part[..., None]), 0.0)
    grad_probs = jnp.einsum(
        "sqhd,skhd->shqk", grad_part, value_part, preferred_element_type=jnp.float32
    )
    grad_scores = (probs * (grad_probs - delta_part[..., None])).astype(jnp.bfloat16)
    return (probs, grad_scores)


def shards_general(
    layer_input,
    weight_query,
    weight_key,
    weight_value,
    weight_output,
    weight_expand,
    weight_reduce,
    bias_query,
    bias_value,
    bias_output,
    bias_expand,
    bias_reduce,
    first_gain,
    first_shift,
    second_gain,
    second_shift,
    cotangent,
    doc_lengths,
):
    seq_count, tok_rows, model_width = layer_input.shape
    head_count = lax.axis_size("head")
    blk_count = lax.axis_size("blk")
    heads_here = HEADS // head_count
    score_scale = HEAD_DIM ** (-0.5)
    gathered = (
        lax.all_gather(weight_query, ("seq", "blk", "head"), axis=0, tiled=True),
        lax.all_gather(weight_key, ("seq", "blk", "head"), axis=0, tiled=True),
        lax.all_gather(weight_value, ("seq", "blk", "head"), axis=0, tiled=True),
        lax.all_gather(weight_output, ("seq", "blk", "head"), axis=0, tiled=True),
        lax.all_gather(weight_expand, ("seq", "blk", "head"), axis=0, tiled=True),
        lax.all_gather(weight_reduce, ("seq", "blk", "head"), axis=0, tiled=True),
        lax.all_gather(bias_query, ("seq", "blk", "head"), axis=0, tiled=True),
        lax.all_gather(bias_value, ("seq", "blk", "head"), axis=0, tiled=True),
        lax.all_gather(bias_output, ("seq", "blk", "head"), axis=0, tiled=True),
        lax.all_gather(bias_expand, ("seq", "blk", "head"), axis=0, tiled=True),
        lax.all_gather(bias_reduce, ("seq", "blk", "head"), axis=0, tiled=True),
        lax.all_gather(first_gain, ("seq", "blk", "head"), axis=0, tiled=True),
        lax.all_gather(first_shift, ("seq", "blk", "head"), axis=0, tiled=True),
        lax.all_gather(second_gain, ("seq", "blk", "head"), axis=0, tiled=True),
        lax.all_gather(second_shift, ("seq", "blk", "head"), axis=0, tiled=True),
    )
    w_query, w_key, w_value, w_output, w_expand, w_reduce = gathered[:6]
    b_query, b_value, b_output, b_expand, b_reduce, gain_one, shift_one, gain_two, shift_two = [
        vector.astype(jnp.float32) for vector in gathered[6:]
    ]
    flat_rows = layer_input.reshape(-1, model_width)
    queries = (
        (plain_dot(flat_rows, w_query) + b_query).astype(jnp.bfloat16).reshape(layer_input.shape)
    )
    key_rows = plain_dot(flat_rows, w_key).astype(jnp.bfloat16).reshape(layer_input.shape)
    value_rows = (
        (plain_dot(flat_rows, w_value) + b_value).astype(jnp.bfloat16).reshape(layer_input.shape)
    )
    query_heads, key_heads, value_heads = (
        lax.all_to_all(queries, "head", split_axis=2, concat_axis=1, tiled=True),
        lax.all_to_all(key_rows, "head", split_axis=2, concat_axis=1, tiled=True),
        lax.all_to_all(value_rows, "head", split_axis=2, concat_axis=1, tiled=True),
    )
    block_rows = query_heads.shape[1]
    block_first = lax.axis_index("blk") * block_rows
    query_seg = segment_ids(doc_lengths, block_first + lax.iota(jnp.int32, block_rows))
    query_split = query_heads.reshape(seq_count, block_rows, heads_here, HEAD_DIM)

    def key_block(shard_piece, block_index, block_width):
        key_offset = block_index * block_width
        key_part = lax.dynamic_slice_in_dim(shard_piece[0], key_offset, block_width, 1).reshape(
            seq_count, block_width, heads_here, HEAD_DIM
        )
        value_part = lax.dynamic_slice_in_dim(shard_piece[1], key_offset, block_width, 1).reshape(
            seq_count, block_width, heads_here, HEAD_DIM
        )
        key_seg = segment_ids(doc_lengths, key_offset + lax.iota(jnp.int32, block_width))
        allowed = query_seg[:, None, :, None] == key_seg[:, None, None, :]
        scores = (
            jnp.einsum("sqhd,skhd->shqk", query_split, key_part, preferred_element_type=jnp.float32)
            * score_scale
        )
        return (key_offset, key_part, value_part, allowed, scores)

    stat_shape = (seq_count, heads_here, block_rows)
    start_state = (
        jnp.full(stat_shape, -1e30, jnp.float32),
        jnp.zeros(stat_shape, jnp.float32),
        jnp.zeros(stat_shape + (HEAD_DIM,), jnp.float32),
    )
    shard_piece = (
        lax.all_gather(key_heads, "blk", axis=1, tiled=True),
        lax.all_gather(value_heads, "blk", axis=1, tiled=True),
    )
    piece_rows = shard_piece[0].shape[1]
    block_width = math.gcd(piece_rows, 512)

    def advance(block_index, loop_state):
        running_max, row_total, accum = loop_state
        key_offset, key_part, value_part, allowed, scores = key_block(
            shard_piece, block_index, block_width
        )
        scores = jnp.where(allowed, scores, -1e30)
        new_max = jnp.maximum(running_max, jnp.max(scores, axis=-1))
        rescale = jnp.exp(running_max - new_max)
        weights = jnp.where(allowed, jnp.exp(scores - new_max[..., None]), 0.0)
        row_total = row_total * rescale + jnp.sum(weights, axis=-1)
        accum = accum * rescale[..., None] + jnp.einsum(
            "shqk,skhd->shqd",
            weights.astype(jnp.bfloat16),
            value_part,
            preferred_element_type=jnp.float32,
        )
        return (new_max, row_total, accum)

    running_max, row_total, accum = lax.fori_loop(
        0, piece_rows // block_width, advance, start_state
    )
    log_total = running_max + jnp.log(row_total)
    attn_heads = accum / row_total[..., None]
    attn_send = (
        attn_heads.transpose(0, 2, 1, 3)
        .reshape(seq_count, block_rows, heads_here * HEAD_DIM)
        .astype(jnp.bfloat16)
    )
    attn_tokens = lax.all_to_all(attn_send, "head", split_axis=1, concat_axis=2, tiled=True)
    attn_flat = attn_tokens.reshape(-1, model_width)
    resid_one = flat_rows.astype(jnp.float32) + plain_dot(attn_flat, w_output) + b_output
    normed_one, norm_one_pull = jax.vjp(layer_norm, resid_one, gain_one, shift_one)
    normed_low = normed_one.astype(jnp.bfloat16)
    pre_act = plain_dot(normed_low, w_expand) + b_expand
    hidden_f32, gelu_pull = jax.vjp(gelu_curve, pre_act)
    hidden = hidden_f32.astype(jnp.bfloat16)
    resid_two = normed_one + plain_dot(hidden, w_reduce) + b_reduce
    result, norm_two_pull = jax.vjp(layer_norm, resid_two, gain_two, shift_two)
    layer_output = result.astype(jnp.bfloat16).reshape(layer_input.shape)
    tok_first = (lax.axis_index("blk") * head_count + lax.axis_index("head")) * tok_rows
    tok_seg = segment_ids(doc_lengths, tok_first + lax.iota(jnp.int32, tok_rows))
    live = (tok_seg > 0).astype(jnp.float32)
    grad_out = (cotangent.astype(jnp.float32) * live[..., None]).reshape(-1, model_width)
    grad_resid_two, grad_gain_two, grad_shift_two = norm_two_pull(grad_out)
    grad_ffn = grad_resid_two.astype(jnp.bfloat16)
    grad_w_reduce = left_dot(hidden, grad_ffn)
    grad_b_reduce = jnp.sum(grad_ffn.astype(jnp.float32), axis=0)
    (grad_pre,) = gelu_pull(right_dot(grad_ffn, w_reduce))
    grad_pre = grad_pre.astype(jnp.bfloat16)
    grad_w_expand = left_dot(normed_low, grad_pre)
    grad_b_expand = jnp.sum(grad_pre.astype(jnp.float32), axis=0)
    grad_normed = grad_resid_two + right_dot(grad_pre, w_expand)
    grad_resid_one, grad_gain_one, grad_shift_one = norm_one_pull(grad_normed)
    grad_branch = grad_resid_one.astype(jnp.bfloat16)
    grad_w_output = left_dot(attn_flat, grad_branch)
    grad_b_output = jnp.sum(grad_branch.astype(jnp.float32), axis=0)
    grad_attn = right_dot(grad_branch, w_output).astype(jnp.bfloat16).reshape(layer_input.shape)
    grad_attn_heads = lax.all_to_all(grad_attn, "head", split_axis=2, concat_axis=1, tiled=True)
    grad_attn_split = grad_attn_heads.reshape(seq_count, block_rows, heads_here, HEAD_DIM)
    row_delta = jnp.einsum("sqhd,shqd->shq", grad_attn_split.astype(jnp.float32), attn_heads)
    full_rows = blk_count * block_rows
    query_zero = jnp.zeros((seq_count, block_rows, heads_here, HEAD_DIM), jnp.float32)
    back_state = (
        query_zero,
        jnp.zeros((seq_count, full_rows, heads_here * HEAD_DIM), jnp.float32),
        jnp.zeros((seq_count, full_rows, heads_here * HEAD_DIM), jnp.float32),
    )
    fold_shard_piece = (
        lax.all_gather(key_heads, "blk", axis=1, tiled=True),
        lax.all_gather(value_heads, "blk", axis=1, tiled=True),
    )
    piece_rows = fold_shard_piece[0].shape[1]
    fold_block_width = math.gcd(piece_rows, 512)

    def advance(block_index, loop_state):
        grad_query, grad_keys, grad_values = loop_state
        key_offset, key_part, value_part, allowed, scores = key_block(
            fold_shard_piece, block_index, fold_block_width
        )
        probs, grad_scores = score_grads(
            scores, allowed, grad_attn_split, value_part, log_total, row_delta
        )
        grad_query = (
            grad_query
            + jnp.einsum(
                "shqk,skhd->sqhd", grad_scores, key_part, preferred_element_type=jnp.float32
            )
            * score_scale
        )
        key_term = (
            jnp.einsum(
                "shqk,sqhd->skhd", grad_scores, query_split, preferred_element_type=jnp.float32
            )
            * score_scale
        )
        value_term = jnp.einsum(
            "shqk,sqhd->skhd",
            probs.astype(jnp.bfloat16),
            grad_attn_split,
            preferred_element_type=jnp.float32,
        )
        grad_keys = lax.dynamic_update_slice_in_dim(
            grad_keys,
            key_term.reshape(seq_count, fold_block_width, heads_here * HEAD_DIM),
            key_offset,
            1,
        )
        grad_values = lax.dynamic_update_slice_in_dim(
            grad_values,
            value_term.reshape(seq_count, fold_block_width, heads_here * HEAD_DIM),
            key_offset,
            1,
        )
        return (grad_query, grad_keys, grad_values)

    back_out = lax.fori_loop(0, piece_rows // fold_block_width, advance, back_state)
    grad_query = back_out[0]
    key_share, value_share = (
        lax.psum_scatter(
            back_out[1].astype(jnp.bfloat16), "blk", scatter_dimension=1, tiled=True
        ).astype(jnp.float32),
        lax.psum_scatter(
            back_out[2].astype(jnp.bfloat16), "blk", scatter_dimension=1, tiled=True
        ).astype(jnp.float32),
    )
    query_send = grad_query.reshape(seq_count, block_rows, heads_here * HEAD_DIM).astype(
        jnp.bfloat16
    )
    query_back, key_back, value_back = (
        lax.all_to_all(query_send, "head", split_axis=1, concat_axis=2, tiled=True),
        lax.all_to_all(
            key_share.astype(jnp.bfloat16), "head", split_axis=1, concat_axis=2, tiled=True
        ),
        lax.all_to_all(
            value_share.astype(jnp.bfloat16), "head", split_axis=1, concat_axis=2, tiled=True
        ),
    )
    query_back = query_back.reshape(-1, model_width)
    key_back = key_back.reshape(-1, model_width)
    value_back = value_back.reshape(-1, model_width)
    grad_w_query = left_dot(flat_rows, query_back)
    grad_w_key = left_dot(flat_rows, key_back)
    grad_w_value = left_dot(flat_rows, value_back)
    grad_b_query = jnp.sum(query_back.astype(jnp.float32), axis=0)
    grad_b_value = jnp.sum(value_back.astype(jnp.float32), axis=0)
    grad_input = (
        grad_resid_one
        + right_dot(query_back, w_query)
        + right_dot(key_back, w_key)
        + right_dot(value_back, w_value)
    )
    grad_input = grad_input.reshape(layer_input.shape)
    shares_all = (
        lax.psum_scatter(grad_w_query, ("seq", "blk", "head"), scatter_dimension=0, tiled=True),
        lax.psum_scatter(grad_w_key, ("seq", "blk", "head"), scatter_dimension=0, tiled=True),
        lax.psum_scatter(grad_w_value, ("seq", "blk", "head"), scatter_dimension=0, tiled=True),
        lax.psum_scatter(grad_w_output, ("seq", "blk", "head"), scatter_dimension=0, tiled=True),
        lax.psum_scatter(grad_w_expand, ("seq", "blk", "head"), scatter_dimension=0, tiled=True),
        lax.psum_scatter(grad_w_reduce, ("seq", "blk", "head"), scatter_dimension=0, tiled=True),
        lax.psum_scatter(grad_b_query, ("seq", "blk", "head"), scatter_dimension=0, tiled=True),
        lax.psum_scatter(grad_b_value, ("seq", "blk", "head"), scatter_dimension=0, tiled=True),
        lax.psum_scatter(grad_b_output, ("seq", "blk", "head"), scatter_dimension=0, tiled=True),
        lax.psum_scatter(grad_b_expand, ("seq", "blk", "head"), scatter_dimension=0, tiled=True),
        lax.psum_scatter(grad_b_reduce, ("seq", "blk", "head"), scatter_dimension=0, tiled=True),
        lax.psum_scatter(grad_gain_one, ("seq", "blk", "head"), scatter_dimension=0, tiled=True),
        lax.psum_scatter(grad_shift_one, ("seq", "blk", "head"), scatter_dimension=0, tiled=True),
        lax.psum_scatter(grad_gain_two, ("seq", "blk", "head"), scatter_dimension=0, tiled=True),
        lax.psum_scatter(grad_shift_two, ("seq", "blk", "head"), scatter_dimension=0, tiled=True),
    )
    return (
        layer_output,
        grad_input,
        shares_all[0],
        shares_all[1],
        shares_all[2],
        shares_all[3],
        shares_all[4],
        shares_all[5],
        shares_all[6],
        shares_all[7],
        shares_all[8],
        shares_all[9],
        shares_all[10],
        shares_all[11],
        shares_all[12],
        shares_all[13],
        shares_all[14],
    )


MESH = pl.DeviceIdType.MESH
EVERY = ("seq", "blk", "head")
EDGE = 32
UNIT = 1024


class Place:
    def __init__(self, blks):
        self.blks = blks
        self.x = lax.axis_index("seq")
        self.z = lax.axis_index("blk")
        lane = lax.axis_index("head")
        self.y = lane // 2
        self.c = lax.rem(lane, 2)
        self.index = self.z * 4 + lane
        self.group = blks * 4

    def peer(self, step):
        index = lax.rem(self.index + step, self.group)
        return index, self.member(index)

    def member(self, index):
        return {"seq": self.x, "blk": index // 4, "head": lax.rem(index, 4)}

    def at(self, x=None, z=None, y=None, c=None):
        x = self.x if x is None else x
        z = self.z if z is None else z
        y = self.y if y is None else y
        c = self.c if c is None else c
        return {"seq": x, "blk": z, "head": y * 2 + c}

    def column(self):
        return [lax.rem(self.z + step, self.blks) for step in range(1, self.blks)]

    def near(self):
        return [self.at(z=z) for z in self.column()] + [
            self.at(x=1 - self.x),
            self.at(y=1 - self.y),
            self.at(c=1 - self.c),
        ]

    def others(self, devices):
        own = (self.x * self.blks + self.z) * 4 + self.y * 2 + self.c
        found = []
        for step in range(1, devices):
            index = lax.rem(own + step, devices)
            found.append(
                {
                    "seq": index // (self.blks * 4),
                    "blk": lax.rem(index // 4, self.blks),
                    "head": lax.rem(index, 4),
                }
            )
        return own, found


def greet(devices):
    barrier = pltpu.get_barrier_semaphore()
    for device in devices:
        pl.semaphore_signal(barrier, inc=1, device_id=device, device_id_type=MESH)
    pl.semaphore_wait(barrier, len(devices))


class Wires:
    def __init__(self, send, recv):
        self.send, self.recv, self.used = send, recv, 0

    def copy(self, source, target, device):
        slot = self.used
        self.used += 1
        return pltpu.make_async_remote_copy(
            src_ref=source,
            dst_ref=target,
            send_sem=self.send.at[slot],
            recv_sem=self.recv.at[slot],
            device_id=device,
            device_id_type=MESH,
        )


def view(ref, index, piece):
    rows, cols = piece
    return ref.at[tuple(index) + (pl.ds(*rows), pl.ds(*cols))]


ALL = slice(None)


def share_line(me, wires, ref, piece, source=None):
    own = view(ref, (me.x, me.z, me.y, me.c), piece)
    source = own if source is None else source
    return [wires.copy(source, own, me.at(z=peer)) for peer in me.column()]


class Gather:
    WIRES = 7

    def __init__(self, me, wires, ref, piece, turned, ready=False, source=None):
        x, z, y, c = me.x, me.z, me.y, me.c
        self.first = [] if ready else share_line(me, wires, ref, piece, source)
        line = view(ref, (x, ALL, y, c), piece)
        if turned:
            half, rest = view(ref, (ALL, ALL, y, c), piece), view(ref, (ALL, ALL, 1 - y, c), piece)
            self.second = wires.copy(line, line, me.at(x=1 - x))
            self.third = wires.copy(half, half, me.at(y=1 - y))
        else:
            half, rest = view(ref, (x, ALL, ALL, c), piece), view(ref, (1 - x, ALL, ALL, c), piece)
            self.second = wires.copy(line, line, me.at(y=1 - y))
            self.third = wires.copy(half, half, me.at(x=1 - x))
        self.near = wires.copy(half, half, me.at(c=1 - c))
        self.far = wires.copy(rest, rest, me.at(c=1 - c))

    def stage(self, index):
        if index == 0:
            for copy in self.first:
                copy.start()
        elif index == 1:
            for copy in self.first:
                copy.wait_recv()
            self.second.start()
        elif index == 2:
            self.second.wait_recv()
            self.third.start()
            self.near.start()
        elif index == 3:
            self.third.wait_recv()
            self.far.start()
        else:
            self.near.wait_recv()
            self.far.wait_recv()
            for copy in (*self.first, self.second, self.third, self.near, self.far):
                copy.wait_send()


class Relay(Gather):
    WIRES = 7

    def __init__(self, me, wires, ref, piece, turned, source):
        super().__init__(me, wires, ref, piece, turned, ready=True)
        x, z, y, c = me.x, me.z, me.y, me.c
        own = view(ref, (x, z, y, c), piece)
        beside = me.at(z=z + 1 - 2 * lax.rem(z, 2))
        pair = view(ref, (x, pl.ds(z // 2 * 2, 2), y, c), piece)
        other = view(ref, (x, pl.ds(2 - z // 2 * 2, 2), y, c), piece)
        self.inner = (z == 1) | (z == 2)
        self.own = wires.copy(source, own, beside)
        self.cross = wires.copy(pair, pair, me.at(z=lax.rem(3 - z, 4)))
        self.outward = wires.copy(other, other, beside)

    def stage(self, index):
        if index == 0:
            self.own.start()
        elif index == 1:
            self.own.wait_recv()

            @pl.when(self.inner)
            def _():
                self.cross.start()

        elif index == 2:

            @pl.when(self.inner)
            def _():
                self.cross.wait_recv()
                self.outward.start()

        elif index == 3:

            @pl.when(jnp.logical_not(self.inner))
            def _():
                self.outward.wait_recv()

            super().stage(1)
        elif index < 6:
            super().stage(index - 2)
        else:

            @pl.when(self.inner)
            def _():
                self.cross.wait_send()
                self.outward.wait_send()

            self.own.wait_send()
            super().stage(4)


class Reduce:
    WIRES = 6

    def __init__(self, me, wires, ref, piece, turned, own, own_sem, r0, r1, r2, r3, out, out_piece):
        x, z, y, c = me.x, me.z, me.y, me.c
        self.place, self.turned, self.out, self.out_piece = me, turned, out, out_piece
        self.r0, self.r1, self.r2, self.r3 = r0, r1, r2, r3
        if own is None:
            self.load = None
            self.own = lambda at: ref[at + (c, pl.ds(*piece[0]), pl.ds(*piece[1]))]
        else:
            self.load = pltpu.make_async_copy(view(ref, (ALL, ALL, ALL, c), piece), own, own_sem)
            self.own = lambda at: own[at]
        self.zero = wires.copy(view(ref, (ALL, ALL, ALL, 1 - c), piece), r0, me.at(c=1 - c))
        if turned:
            self.one = wires.copy(r0.at[:, :, 1 - y], r1, me.at(y=1 - y))
            self.two = wires.copy(r0.at[1 - x, :, y], r2, me.at(x=1 - x))
        else:
            self.one = wires.copy(r0.at[1 - x], r1, me.at(x=1 - x))
            self.two = wires.copy(r0.at[x, :, 1 - y], r2, me.at(y=1 - y))
        self.three = [
            wires.copy(r0.at[x, peer, y], r3.at[slot], me.at(z=peer))
            for slot, peer in enumerate(me.column())
        ]

    def stage(self, index):
        x, z, y = self.place.x, self.place.z, self.place.y
        blks = self.place.blks
        r0 = self.r0

        def add(target, term):
            total = r0[target].astype(jnp.float32) + term.astype(jnp.float32)
            r0[target] = total.astype(r0.dtype)

        if index == 0:
            self.zero.start()
        elif index == 1:
            self.load.start()
        elif index == 2:
            if self.load is not None:
                self.load.wait()
            self.zero.wait_recv()

            @pl.loop(0, 4 * blks)
            def _(i):
                at = (i // (2 * blks), lax.rem(i // 2, blks), lax.rem(i, 2))
                add(at, self.own(at))

            self.one.start()
        elif index == 3:
            self.one.wait_recv()

            @pl.loop(0, 2 * blks)
            def _(i):
                if self.turned:
                    a, b = i // blks, lax.rem(i, blks)
                    add((a, b, y), self.r1[a, b])
                else:
                    a, b = i // 2, lax.rem(i, 2)
                    add((x, a, b), self.r1[a, b])

            self.two.start()
        elif index == 4:
            self.two.wait_recv()

            @pl.loop(0, blks)
            def _(i):
                add((x, i, y), self.r2[i])

            for copy in self.three:
                copy.start()
        else:
            for copy in self.three:
                copy.wait_recv()
            total = r0[x, z, y].astype(jnp.float32)
            for slot in range(blks - 1):
                total = total + self.r3[slot].astype(jnp.float32)
            rows, cols = self.out_piece
            self.out[rows[0] : rows[0] + rows[1], cols[0] : cols[0] + cols[1]] = total
            for copy in (self.zero, self.one, self.two, *self.three):
                copy.wait_send()


def reduce_scratch(units, blks, cols=UNIT, dtype=jnp.bfloat16):
    turned = units // 2
    return [
        pltpu.VMEM((units, 2, blks, 2, EDGE, cols), dtype),
        pltpu.VMEM((units - turned, blks, 2, EDGE, cols), dtype),
        pltpu.VMEM((turned, 2, blks, EDGE, cols), dtype),
        pltpu.VMEM((units, blks, EDGE, cols), dtype),
        pltpu.VMEM((units, blks - 1, EDGE, cols), dtype),
        pltpu.SemaphoreType.DMA((Reduce.WIRES * units,)),
        pltpu.SemaphoreType.DMA((Reduce.WIRES * units,)),
    ]


def weight_units(edges):
    columns = []
    for which, (rows, cols) in enumerate(edges):
        columns.append(
            [
                (which, ((row, EDGE), (col, UNIT)))
                for row in range(0, rows, EDGE)
                for col in range(0, cols, UNIT)
            ]
        )
    most = max([len(column) for column in columns] + [0])
    return [column[place] for place in range(most) for column in columns if place < len(column)]


LOG2E = 1.4426950408889634
BY_LAST = (((1,), (1,)), ((), ()))


def lanes(ref, lead, first, width):
    return ref.at[tuple(lead) + (pl.ds(pl.multiple_of(first, width), width),)]


def wire(source, target, send_sem, recv_sem, device):
    return pltpu.make_async_remote_copy(
        src_ref=source,
        dst_ref=target,
        send_sem=send_sem,
        recv_sem=recv_sem,
        device_id=device,
        device_id_type=MESH,
    )


def TURNED(number):
    return number % 2 == 1


def SCHEDULE(number):
    return (-4, -2, -1, -0.9 if number < 4 else number / 2, 5 + number)


def home(block, main):
    return jnp.where(block < main, block // 2 + main // 2 * lax.rem(block, 2), block)


def cuts(width, cols):
    return [(first, min(first + cols, width)) for first in range(0, width, cols)]


def attn_fwd_kernel(
    blks, rows, cols, count, *refs
):
    x_ref, vec_ref, doc_ref, wq, wk, wv = refs[:6]
    shares, refs = refs[6 : 6 + count], refs[6 + count :]
    p_ref, tail_ref, o_ref, inv_ref, kept_ref, tokens_ref, qkv_out, vec_out = refs[:8]
    wholes, refs = refs[8 : 8 + count], refs[8 + count :]
    (
    weights, vecs, qkv_ref, land, keys, values, s0, s1, m0, m1, now, peaks, acc, top,
    own_sem, kv_send, kv_recv, q_send, q_recv, o_send, o_recv, send, recv,
    ) = refs
    step, steps = pl.program_id(0), pl.num_programs(0)
    length, part = land.shape[2], p_ref.shape[1]
    long = 2 * part
    width = 2 * rows
    tail, pieces = length - long, cuts(part, cols)
    main = long // width
    side, turn = step // main, lax.rem(step, main)
    scale = LOG2E * HEAD_DIM**-0.5

    me = Place(blks)
    group = me.group

    def block_at(turn):
        return lax.rem(lax.rem(me.index, main) + turn, main)

    def ahead(block):
        return lax.rem(block + group - me.index, group)

    def spot(tensor, block):
        return home(block, main) if tensor else block

    early = (me.index < main) & (lax.rem(me.index, 2) == 0)
    swaps = [[], [], []]
    for tensor, send_sem, recv_sem in ((0, q_send, q_recv), (1, kv_send, kv_recv), (2, kv_send, kv_recv)):
        for ahead_by in range(1, group):
            peer, device = me.peer(group - ahead_by)
            slot = ahead_by + (group if tensor == 2 else 0)
            swaps[tensor].append(
                wire(
                    qkv_ref.at[tensor, peer],
                    lanes(land, (tensor, ALL), spot(tensor, me.index) * width, width),
                    send_sem.at[slot],
                    recv_sem.at[slot],
                    device,
                )
            )
    keep = pltpu.make_async_copy(land, kept_ref, own_sem.at[1])

    def await_from(tensor, block):
        @pl.when(block != me.index)
        def _():
            send_sem, recv_sem = (kv_send, kv_recv) if tensor else (q_send, q_recv)
            wire(
                qkv_ref.at[tensor, block],
                lanes(land, (tensor, ALL), spot(tensor, block) * width, width),
                send_sem.at[0],
                recv_sem.at[ahead(block) + (group if tensor == 2 else 0)],
                me.member(block),
            ).wait_recv()

    def await_keys(first):
        for block in range(first, main, 2):
            await_from(1, block)
            await_from(2, block)
        here = slice(first * part, (first + 1) * part)
        keys[first, 0:HEAD_DIM, :] = land[1, :, here]
        keys[first, HEAD_DIM:, :] = land[1, :, here]
        values[first, 0:HEAD_DIM, :] = land[2, :, here]
        values[first, HEAD_DIM:, :] = ones_row(part)

    def ones_row(columns):
        return (
            (lax.broadcasted_iota(jnp.int32, (16, columns), 0) == 0)
            .astype(jnp.float32)
            .astype(jnp.bfloat16)
        )

    def send_block(block, slot, start):
        source = lanes(o_ref, (ALL,), block * width, width)
        remote = wire(
            source,
            tokens_ref.at[me.index],
            o_send.at[slot],
            o_recv.at[lax.rem(me.index + group - block, group)],
            me.member(block),
        )
        local = pltpu.make_async_copy(source, tokens_ref.at[me.index], own_sem.at[2])

        @pl.when(block != me.index)
        def _():
            if start:
                remote.start()
            else:
                remote.wait_send()

        @pl.when(block == me.index)
        def _():
            if start:
                local.start()
            else:
                local.wait()

    wires = Wires(send, recv)
    here = (me.x, me.z, me.y, me.c)
    half = UNIT // 2
    fronts = []
    for unit, ref in enumerate((wq, wk, wv)):
        for flank in range(2):
            piece = ((0, EDGE), (unit * UNIT + flank * half, half))
            source = ref.at[:, pl.ds(flank * half, half)]
            fronts.append(Gather(me, wires, weights, piece, flank == 1, source=source))
    vectors = Gather(me, wires, vecs, ((0, EDGE), (0, vecs.shape[5])), False)
    units = weight_units([share.shape for share in shares])
    plan = [
        Relay(
            me,
            wires,
            wholes[which],
            piece,
            TURNED(number),
            source=shares[which].at[pl.ds(*piece[0]), pl.ds(*piece[1])],
        )
        for number, (which, piece) in enumerate(units)
    ]
    targets = [weights.at[here + (ALL, pl.ds(unit * UNIT, UNIT))] for unit in range(3)]
    targets += [whole.at[here] for whole in wholes]
    local = [
        pltpu.make_async_copy(source, target, own_sem.at[3 + number])
        for number, (source, target) in enumerate(zip((wq, wk, wv) + tuple(shares), targets))
    ]
    keep_weights = pltpu.make_async_copy(weights, qkv_out, own_sem.at[9])
    keep_vectors = pltpu.make_async_copy(vecs, vec_out, own_sem.at[10])
    moves = {}
    for number in range(len(units)):
        for stage, at in enumerate(SCHEDULE(number), 1):
            at = min(int(2 * at), 2 * main - 1) if at >= 0 else at
            moves.setdefault(at, []).append((plan[number], stage))

    def pace(at):
        for unit, stage in moves.get(at, []):
            unit.stage(stage)

    def front(tensor, *stages):
        for stage in stages:
            for unit in fronts[2 * tensor : 2 * tensor + 2]:
                unit.stage(stage)

    def project(tensor, column):
        for first in range(0, UNIT, 256):
            taken = weights[:, :, :, :, :, tensor * UNIT + first : tensor * UNIT + first + 256]
            found = jnp.dot(
                x_ref[...], taken.reshape(UNIT, 256), preferred_element_type=jnp.float32
            ).T
            if column is not None:
                bias = vecs[...].reshape(UNIT, vecs.shape[5])[first : first + 256]
                found = found + bias[:, column : column + 1].astype(jnp.float32)
            heads = first // HEAD_DIM, (first + 256) // HEAD_DIM
            qkv_ref[tensor, heads[0] : heads[1]] = found.astype(jnp.bfloat16).reshape(
                heads[1] - heads[0], HEAD_DIM, width
            )
        own = pl.ds(pl.multiple_of(spot(tensor, me.index) * width, width), width)
        land[tensor, :, own] = qkv_ref[tensor, me.index]

    def take_queries(start):
        part = land[0, :, pl.ds(pl.multiple_of(start, rows), rows)].astype(jnp.float32) * scale
        high = part.astype(jnp.bfloat16).astype(jnp.float32)
        return jnp.concatenate([high, part - high], 0).T.astype(jnp.bfloat16)

    def score(queries, at, store, piece, peak):
        found = jnp.dot(
            queries, keys[at, :, piece[0] : piece[1]], preferred_element_type=jnp.float32
        )
        store[:, piece[0] : piece[1]] = found
        for first in range(0, piece[1] - piece[0], 128):
            some = found[:, first : first + 128]
            peak = some if peak is None else jnp.maximum(peak, some)
        return peak

    def keep_peak(store, peak):
        store[...] = jnp.broadcast_to(jnp.max(peak, axis=1, keepdims=True), store.shape)

    def weigh(store, peak, piece, row, total):
        weights = jnp.exp2(store[:, piece[0] : piece[1]] - peak[:, :1]).astype(jnp.bfloat16)
        p_ref[row : row + rows, piece[0] : piece[1]] = weights
        term = lax.dot_general(
            values[side, :, piece[0] : piece[1]],
            weights,
            BY_LAST,
            preferred_element_type=jnp.float32,
        )
        return term if total is None else total + term

    @pl.when(step == 0)
    def _():
        for copy in local:
            copy.start()
        turned = jnp.concatenate(
            [vec_ref[...].astype(jnp.float32), jnp.zeros((112, 128), jnp.float32)], 0
        ).T
        vecs[here] = turned[:EDGE].astype(jnp.bfloat16)
        greet([me.peer(by)[1] for by in range(1, group)] + [me.at(x=1 - me.x)])
        vectors.stage(0)
        front(1, 0)
        for copy in local:
            copy.wait()
        vectors.stage(1)
        front(1, 1)
        front(2, 0)
        front(1, 2)
        front(0, 0)
        for unit in plan:
            unit.stage(0)
        vectors.stage(2)
        front(2, 1)
        pace(-5)
        front(1, 3)
        front(2, 2)
        vectors.stage(3)
        front(0, 1)
        pace(-4)
        front(1, 4)
        project(1, None)

        @pl.when(early)
        def _():
            for copy in swaps[1]:
                copy.start()

        pace(-3)
        front(2, 3)
        front(0, 2)
        vectors.stage(4)
        front(2, 4)
        project(2, 1)

        @pl.when(early)
        def _():
            for copy in swaps[2]:
                copy.start()

        front(0, 3)
        pace(-2)
        front(0, 4)
        keep_weights.start()
        keep_vectors.start()
        project(0, 0)
        for copy in swaps[0]:
            copy.start()

        @pl.when(jnp.logical_not(early))
        def _():
            for copy in swaps[1] + swaps[2]:
                copy.start()

        for at in (-1, -0.9, -0.8, -0.7, -0.6):
            pace(at)
        await_keys(0)
        await_from(0, block_at(0))
        queries, peak = take_queries(block_at(0) * width), None
        for piece in pieces:
            peak = score(queries, 0, s0, piece, peak)
        keep_peak(m0, peak)

    for at, todo in sorted((entry for entry in moves.items() if entry[0] >= 0), key=lambda entry: entry[0]):

        @pl.when(step == at)
        def _():
            for unit, stage in todo:
                unit.stage(stage)

    @pl.when(step == main - 1)
    def _():
        await_keys(1)

    next_step = jnp.minimum(step + 1, steps - 1)
    block = block_at(turn)
    later, later_side = block_at(lax.rem(next_step, main)), next_step // main
    place = pl.ds(pl.multiple_of(block * width, width), width)

    @pl.when(step < main - 1)
    def _():
        await_from(0, later)

    for half, (old, old_peak, new, new_peak) in enumerate(((s0, m0, s1, m1), (s1, m1, s0, m0))):
        queries = take_queries(block * width + rows if half == 0 else later * width)
        at = side if half == 0 else later_side
        total, peak = None, None
        for piece in pieces:
            total = weigh(old, old_peak, piece, half * rows, total)
            peak = score(queries, at, new, piece, peak)
        here = slice(half * rows, (half + 1) * rows)
        peaks[:, here] = old_peak[...].T[0:8]
        now[:, here] = total
        keep_peak(new_peak, peak)

    @pl.when(side == 0)
    def _():
        acc[:, place] = now[...]
        top[:, place] = peaks[...]

    @pl.when(side == 1)
    def _():
        first, second = top[0:1, place], peaks[0:1, :]
        peak = jnp.maximum(first, second)
        first, second = jnp.exp2(first - peak), jnp.exp2(second - peak)
        total = acc[:, place] * first + now[...] * second
        inverse = 1.0 / total[HEAD_DIM : HEAD_DIM + 1]
        o_ref[:, place] = (total[:HEAD_DIM] * inverse).astype(jnp.bfloat16)
        row = lax.broadcasted_iota(jnp.int32, (8, width), 0)
        inv_ref[:, place] = jnp.where(row == 0, first * inverse, second * inverse)
        send_block(block, turn, True)

    @pl.when(step == steps - 1)
    def _():
        for block in range(main, group):
            for tensor in range(3):
                await_from(tensor, block)
        keep.start()
        tail_keys = jnp.concatenate([land[1, :, long:], land[1, :, long:]], 0)
        tail_values = jnp.concatenate([land[2, :, long:], ones_row(tail)], 0)
        spots = long + lax.broadcasted_iota(jnp.int32, (8, tail), 1)
        ended, end = jnp.zeros((8, tail), jnp.int32), jnp.int32(0)
        for number in range(doc_ref.shape[1]):
            end = end + doc_ref[0, number]
            ended = ended + (end <= spots).astype(jnp.int32)
        across = jnp.where(spots < end, ended + 1, 0).astype(jnp.float32)
        down = jnp.broadcast_to(across[:1], (128, tail)).T
        for first in range(0, tail, rows):
            queries = take_queries(long + first)
            found = jnp.dot(queries, tail_keys, preferred_element_type=jnp.float32)
            allowed = down[first : first + rows, :1] == across[:1, :]
            found = jnp.where(allowed, found, -1e30)
            peak = jnp.max(found, axis=1, keepdims=True)
            weights = jnp.exp2(found - peak).astype(jnp.bfloat16)
            tail_ref[first : first + rows, :] = weights
            total = lax.dot_general(
                tail_values, weights, BY_LAST, preferred_element_type=jnp.float32
            )
            here = slice(long + first, long + first + rows)
            inverse = 1.0 / total[HEAD_DIM : HEAD_DIM + 1]
            o_ref[:, here] = (total[:HEAD_DIM] * inverse).astype(jnp.bfloat16)
            inv_ref[:, here] = jnp.broadcast_to(inverse, (8, rows))
            if (first + rows) % width == 0:
                number = main + first // width
                send_block(number, number, True)
        for unit in plan:
            unit.stage(6)
        for copy in swaps[0] + swaps[1] + swaps[2]:
            copy.wait_send()
        keep_weights.wait()
        keep_vectors.wait()
        for number in range(main):
            send_block(block_at(number), number, False)
        for number in range(main, group):
            send_block(number, number, False)
        for ahead_by in range(1, group):
            source, device = me.peer(ahead_by)
            wire(
                lanes(o_ref, (ALL,), source * width, width),
                tokens_ref.at[source],
                o_send.at[0],
                o_recv.at[ahead_by],
                device,
            ).wait_recv()
        keep.wait()


def once(shape):
    return pl.BlockSpec(shape, lambda step: (0,) * len(shape), pipeline_mode=pl.Buffered(1))


def attn_fwd(x, vec, doc_lengths, long, fronts, shares, collective_id, cols=1024):
    seqs, blks, heads = (lax.axis_size(name) for name in EVERY)
    lead = (seqs, blks, heads // 2, 2)
    group, width = blks * heads, x.shape[0]
    rows = width // 2
    length = group * width
    tail = length - long
    main = long // width
    anywhere = pl.BlockSpec(memory_space=pl.ANY)
    count = len(weight_units([share.shape for share in shares])) if shares else 0
    wires = Gather.WIRES * (count + 7)
    kept = jax.ShapeDtypeStruct((3, HEAD_DIM, length), jnp.bfloat16)
    gathered = jax.ShapeDtypeStruct(lead + (EDGE, 3 * UNIT), jnp.bfloat16)
    vectors = jax.ShapeDtypeStruct(lead + (EDGE, 128), jnp.bfloat16)
    pair = [pltpu.SemaphoreType.DMA((group,))] * 2
    return pl.pallas_call(
        functools.partial(attn_fwd_kernel, blks, rows, cols, len(shares)),
        grid=(2 * (long // width),),
        in_specs=[once(x.shape), once(vec.shape), pl.BlockSpec(memory_space=pltpu.SMEM)]
        + [once(share.shape) for share in fronts + shares],
        out_specs=[
            pl.BlockSpec((width, long // 2), lambda step: (lax.rem(step, main), step // main)),
            once((tail, tail)),
            once((HEAD_DIM, length)),
            once((8, length)),
        ]
        + [anywhere] * (4 + len(shares)),
        out_shape=[
            jax.ShapeDtypeStruct((long, long), jnp.bfloat16),
            jax.ShapeDtypeStruct((tail, tail), jnp.bfloat16),
            jax.ShapeDtypeStruct((HEAD_DIM, length), jnp.bfloat16),
            jax.ShapeDtypeStruct((8, length), jnp.float32),
            kept,
            jax.ShapeDtypeStruct((group, HEAD_DIM, width), jnp.bfloat16),
            gathered,
            vectors,
        ]
        + [jax.ShapeDtypeStruct(lead + share.shape, share.dtype) for share in shares],
        scratch_shapes=[
            pltpu.VMEM(gathered.shape, gathered.dtype),
            pltpu.VMEM(vectors.shape, vectors.dtype),
            pltpu.VMEM((3, group, HEAD_DIM, width), jnp.bfloat16),
            pltpu.VMEM(kept.shape, kept.dtype),
            pltpu.VMEM((2, 2 * HEAD_DIM, long // 2), jnp.bfloat16),
            pltpu.VMEM((2, HEAD_DIM + 16, long // 2), jnp.bfloat16),
            pltpu.VMEM((rows, long // 2), jnp.float32),
            pltpu.VMEM((rows, long // 2), jnp.float32),
            pltpu.VMEM((rows, 128), jnp.float32),
            pltpu.VMEM((rows, 128), jnp.float32),
            pltpu.VMEM((HEAD_DIM + 16, width), jnp.float32),
            pltpu.VMEM((8, width), jnp.float32),
            pltpu.VMEM((HEAD_DIM + 16, long), jnp.float32),
            pltpu.VMEM((8, long), jnp.float32),
            pltpu.SemaphoreType.DMA((11,)),
            pltpu.SemaphoreType.DMA((2 * group,)),
            pltpu.SemaphoreType.DMA((2 * group,)),
            *pair,
            *pair,
            pltpu.SemaphoreType.DMA((wires,)),
            pltpu.SemaphoreType.DMA((wires,)),
        ],
        compiler_params=pltpu.CompilerParams(
            collective_id=collective_id, has_side_effects=True, vmem_limit_bytes=62 * 2**20
        ),
        cost_estimate=pl.CostEstimate(
            flops=4 * long * long * HEAD_DIM,
            bytes_accessed=2 * long * long,
            transcendentals=long * long,
        ),
        name="attn_fwd",
    )(x, vec, doc_lengths, *fronts, *shares)


def attn_bwd_kernel(
    blks, rows, cols, count, *refs
):
    p_ref, tail_ref, qkv_ref, o_ref, inv_ref, grads_ref = refs[:6]
    partials, refs = refs[6 : 6 + count], refs[6 + count :]
    dkv_ref, tokens_ref, kv_tokens = refs[:3]
    totals, refs = refs[3 : 3 + count], refs[3 + count :]
    (
    land, dq_out, dq_sum, keys, values, dk_sum, dv_sum, tail_dkv, early_dkv, own, r0, r1a, r1b, r2, r3, send, recv,
    own_sem, do_send, do_recv, dq_send, dq_recv, kv_send, kv_recv,
    ) = refs
    step, steps = pl.program_id(0), pl.num_programs(0)
    length, part = land.shape[1], p_ref.shape[1]
    long = 2 * part
    tail, pieces = length - long, cuts(part, cols)
    main = long // rows
    side, turn = step // main, lax.rem(step, main)
    scale = HEAD_DIM**-0.5

    me = Place(blks)
    group = me.group

    def block_at(turn):
        return lax.rem(lax.rem(me.index, main) + turn, main)

    do_copies = []
    for ahead_by in range(1, group):
        peer, device = me.peer(group - ahead_by)
        do_copies.append(
            wire(
                grads_ref.at[peer],
                lanes(land, (ALL,), me.index * rows, rows),
                do_send.at[ahead_by],
                do_recv.at[ahead_by],
                device,
            )
        )
    own_in = pltpu.make_async_copy(
        grads_ref.at[me.index], lanes(land, (ALL,), me.index * rows, rows), own_sem.at[2]
    )

    def await_grads(block):
        @pl.when(block != me.index)
        def _():
            wire(
                grads_ref.at[block],
                lanes(land, (ALL,), block * rows, rows),
                do_send.at[0],
                do_recv.at[lax.rem(block + group - me.index, group)],
                me.member(block),
            ).wait_recv()

    def send_block(block, slot, start):
        source = lanes(dq_out, (ALL,), block * rows, rows)
        remote = wire(
            source,
            tokens_ref.at[me.index],
            dq_send.at[slot],
            dq_recv.at[lax.rem(me.index + group - block, group)],
            me.member(block),
        )
        local = pltpu.make_async_copy(source, tokens_ref.at[me.index], own_sem.at[3])

        @pl.when(block != me.index)
        def _():
            if start:
                remote.start()
            else:
                remote.wait_send()

        @pl.when(block == me.index)
        def _():
            if start:
                local.start()
            else:
                local.wait()

    early = (me.index >= main) | (lax.rem(me.index, 2) == 0)

    def early_sends():
        for number in range(main // 2):
            block = 2 * lax.rem(number + me.index // 2, main // 2)
            yield number, block, lanes(early_dkv, (ALL, ALL), block // 2 * rows, rows)
        for block in range(main, group):
            source = tail_dkv.at[:, :, pl.ds((block - main) * rows, rows)]
            yield main // 2 + block - main, block, source

    def send_early(start):
        for slot, block, source in early_sends():
            remote = wire(
                source,
                kv_tokens.at[:, me.index],
                kv_send.at[slot],
                kv_recv.at[lax.rem(me.index + group - block, group)],
                me.member(block),
            )
            local = pltpu.make_async_copy(source, kv_tokens.at[:, me.index], own_sem.at[4])

            @pl.when(block != me.index)
            def _():
                if start:
                    remote.start()
                else:
                    remote.wait_send()

            @pl.when(block == me.index)
            def _():
                if start:
                    local.start()
                else:
                    local.wait()

    wires = Wires(send, recv)
    units = weight_units([partial.shape[4:] for partial in partials])
    plan, moves = [], {}
    for number, (which, piece) in enumerate(units):
        turned = number % 2 == 1
        unit = Reduce(
            me,
            wires,
            partials[which],
            piece,
            turned,
            own.at[number % 2],
            own_sem.at[number % 2],
            r0.at[number],
            (r1b if turned else r1a).at[number // 2],
            r2.at[number],
            r3.at[number],
            totals[which],
            piece,
        )
        plan.append(unit)
        pair = number // 2
        for stage, at in enumerate((1.5 * pair, 1.5 * pair, 1.5 * pair + 1, 2 * pair + 3.5, 2 * pair + 5.5)):
            moves.setdefault(min(int(2 * at), 2 * main - 1), []).append((stage, number, unit))

    def prepare(start, width, at):
        place = pl.ds(pl.multiple_of(start, width), width)
        grads = land[:, place].astype(jnp.float32)
        inverse = jnp.where(at == 0, inv_ref[0:1, place], inv_ref[1:2, place])
        delta = -jnp.sum(grads * o_ref[:, place].astype(jnp.float32), axis=0, keepdims=True)
        delta = delta * inverse
        high = delta.astype(jnp.bfloat16).astype(jnp.float32)
        row = lax.broadcasted_iota(jnp.int32, (16, width), 0)
        extra = jnp.where(row == 0, high, jnp.where(row == 1, delta - high, 0.0))
        grads = grads * inverse
        wide = jnp.concatenate([grads, extra], 0).T.astype(jnp.bfloat16)
        return wide, grads.astype(jnp.bfloat16), qkv_ref[0, :, place]

    def terms(wide, grads, queries, weights, keys_here, values_here, dq):
        dp = jnp.dot(wide, values_here, preferred_element_type=jnp.float32)
        ds = (weights.astype(jnp.float32) * dp).astype(jnp.bfloat16)
        dv = jnp.dot(grads, weights, preferred_element_type=jnp.float32)
        dk = jnp.dot(queries, ds, preferred_element_type=jnp.float32)
        term = lax.dot_general(keys_here, ds, BY_LAST, preferred_element_type=jnp.float32)
        return (term if dq is None else dq + term), dk, dv

    def ones_rows(columns):
        return (
            (lax.broadcasted_iota(jnp.int32, (16, columns), 0) < 2)
            .astype(jnp.float32)
            .astype(jnp.bfloat16)
        )

    @pl.when(step == 0)
    def _():
        own_in.start()
        greet([me.peer(by)[1] for by in range(1, group)] + [me.at(x=1 - me.x)])
        for copy in do_copies:
            copy.start()

    for at, todo in sorted(moves.items()):

        @pl.when(step == at)
        def _():
            for stage, number, unit in sorted(todo, key=lambda entry: (-entry[0], entry[1])):
                unit.stage(stage)

    @pl.when(step == 0)
    def _():
        for at in range(2):
            here = slice(at * part, (at + 1) * part)
            keys[at] = qkv_ref[1, :, here]
            values[at, 0:HEAD_DIM, :] = qkv_ref[2, :, here]
            values[at, HEAD_DIM:, :] = ones_rows(part)
        dk_sum[...] = jnp.zeros_like(dk_sum)
        dv_sum[...] = jnp.zeros_like(dv_sum)
        own_in.wait()

    block = block_at(turn)
    place = pl.ds(pl.multiple_of(block * rows, rows), rows)

    @pl.when(side == 0)
    def _():
        await_grads(block)

    wide, grads, queries = prepare(block * rows, rows, side)
    dq = None
    for first, end in pieces:
        dq, dk, dv = terms(
            wide,
            grads,
            queries,
            p_ref[:, first:end],
            keys[side, :, first:end],
            values[side, :, first:end],
            dq,
        )
        dk_sum[side, :, first:end] += dk
        dv_sum[side, :, first:end] += dv

    @pl.when(side == 0)
    def _():
        dq_sum[:, place] = dq

    @pl.when(side == 1)
    def _():
        dq_out[:, place] = ((dq_sum[:, place] + dq) * scale).astype(jnp.bfloat16)
        send_block(block, turn, True)

    @pl.when(step == main - 1)
    def _():
        tail_keys = qkv_ref[1, :, long:]
        tail_values = jnp.concatenate([qkv_ref[2, :, long:], ones_rows(tail)], 0)
        dk_total, dv_total = None, None
        for number in range(main, group):
            await_grads(number)
            first = (number - main) * rows
            wide, grads, queries = prepare(long + first, rows, 0)
            dq, dk, dv = terms(
                wide,
                grads,
                queries,
                tail_ref[first : first + rows, :],
                tail_keys,
                tail_values,
                None,
            )
            dk_total = dk if dk_total is None else dk_total + dk
            dv_total = dv if dv_total is None else dv_total + dv
            dq_out[:, long + first : long + first + rows] = (dq * scale).astype(jnp.bfloat16)
            send_block(number, number, True)
        tail_dkv[0] = (dk_total * scale).astype(jnp.bfloat16)
        tail_dkv[1] = dv_total.astype(jnp.bfloat16)
        early_dkv[0] = (dk_sum[0] * scale).astype(jnp.bfloat16)
        early_dkv[1] = dv_sum[0].astype(jnp.bfloat16)
        send_early(True)

    @pl.when(step == steps - 1)
    def _():
        dkv_ref[0] = (dk_sum[1] * scale).astype(jnp.bfloat16)
        dkv_ref[1] = dv_sum[1].astype(jnp.bfloat16)
        for unit in plan:
            unit.stage(5)
        for copy in do_copies:
            copy.wait_send()
        for number in range(main):
            send_block(block_at(number), number, False)
        for number in range(main, group):
            send_block(number, number, False)
        send_early(False)
        for ahead_by in range(1, group):
            source, device = me.peer(ahead_by)
            wire(
                lanes(dq_out, (ALL,), source * rows, rows),
                tokens_ref.at[source],
                dq_send.at[0],
                dq_recv.at[ahead_by],
                device,
            ).wait_recv()

        @pl.when(early)
        def _():
            for ahead_by in range(1, group):
                source, device = me.peer(ahead_by)
                wire(
                    tail_dkv.at[:, :, pl.ds(0, rows)],
                    kv_tokens.at[:, source],
                    kv_send.at[0],
                    kv_recv.at[ahead_by],
                    device,
                ).wait_recv()


def attn_bwd(
    probs, tail_probs, kept, attn, inv_total, grad_attn, long, partials, collective_id, cols=1024
):
    blks = lax.axis_size("blk")
    lead = (lax.axis_size("seq"), blks, lax.axis_size("head") // 2, 2)
    devices = math.prod(lead)
    length = kept.shape[2]
    tail = length - long
    group, _, rows = grad_attn.shape
    main, part = long // rows, long // 2
    anywhere = pl.BlockSpec(memory_space=pl.ANY)
    edges = [(partial.shape[0] // devices, partial.shape[1]) for partial in partials]
    units = len(weight_units(edges))
    pair = [pltpu.SemaphoreType.DMA((group,))] * 2
    return pl.pallas_call(
        functools.partial(attn_bwd_kernel, blks, rows, cols, len(partials)),
        grid=(2 * main,),
        in_specs=[
            pl.BlockSpec((rows, part), lambda step: (lax.rem(step, main), step // main)),
            once((tail, tail)),
            once(kept.shape),
            once((HEAD_DIM, length)),
            once((8, length)),
        ]
        + [anywhere] * (1 + len(partials)),
        out_specs=[once((2, HEAD_DIM, part)), anywhere, anywhere] + [once(edge) for edge in edges],
        out_shape=[
            jax.ShapeDtypeStruct((2, HEAD_DIM, part), jnp.bfloat16),
            jax.ShapeDtypeStruct((group, HEAD_DIM, rows), jnp.bfloat16),
            jax.ShapeDtypeStruct((2, group, HEAD_DIM, rows), jnp.bfloat16),
        ]
        + [jax.ShapeDtypeStruct(edge, jnp.float32) for edge in edges],
        scratch_shapes=[
            pltpu.VMEM((HEAD_DIM, length), jnp.bfloat16),
            pltpu.VMEM((HEAD_DIM, length), jnp.bfloat16),
            pltpu.VMEM((HEAD_DIM, long), jnp.float32),
            pltpu.VMEM((2, HEAD_DIM, part), jnp.bfloat16),
            pltpu.VMEM((2, HEAD_DIM + 16, part), jnp.bfloat16),
            pltpu.VMEM((2, HEAD_DIM, part), jnp.float32),
            pltpu.VMEM((2, HEAD_DIM, part), jnp.float32),
            pltpu.VMEM((2, HEAD_DIM, tail), jnp.bfloat16),
            pltpu.VMEM((2, HEAD_DIM, part), jnp.bfloat16),
            pltpu.VMEM((2, 2, blks, 2, EDGE, UNIT), jnp.bfloat16),
            *reduce_scratch(max(units, 2), blks),
            pltpu.SemaphoreType.DMA((5,)),
            *pair,
            *pair,
            *pair,
        ],
        compiler_params=pltpu.CompilerParams(
            collective_id=collective_id, has_side_effects=True, vmem_limit_bytes=62 * 2**20
        ),
        cost_estimate=pl.CostEstimate(
            flops=8 * long * long * HEAD_DIM, bytes_accessed=2 * long * long, transcendentals=0
        ),
        name="attn_bwd",
    )(
        probs, tail_probs, kept, attn, inv_total, grad_attn,
        *[partial.reshape(lead + edge) for partial, edge in zip(partials, edges)],
    )


def last_kernel(
    blks, devices, dkv_ref, kv_tokens, dq_ref, x_ref, w_ref, base_ref, sums_ref,
    dwq, dwk, dwv, dx_out, sums_out,
    grads, x, xt, weights, base, turned_dx, partial, bias, landed,
    r0, r1a, r1b, r2, r3, send, recv,
    own_sem, kv_send, kv_recv, sums_send, sums_recv,
):
    me = Place(blks)
    group = me.group
    width = x.shape[0]
    depth = x.shape[1]
    index, others = me.others(devices)
    loads = [
        pltpu.make_async_copy(source, target, own_sem.at[number])
        for number, (source, target) in enumerate(
            (
                (x_ref, x),
                (dq_ref, grads.at[0]),
                (w_ref, weights),
                (base_ref, base),
                (sums_ref, bias),
            )
        )
    ]
    for copy in loads:
        copy.start()
    greet(others)
    main = 2 * (dkv_ref.shape[2] // width)
    odd = (me.index < main) & (lax.rem(me.index, 2) == 1)

    def late_sends(which, start):
        for number in range(main // 2):
            block = 2 * lax.rem(number + me.index // 2, main // 2) + 1
            source = lanes(dkv_ref, (which, ALL), block // 2 * width, width)
            remote = wire(
                source,
                grads.at[which + 1, me.index],
                kv_send.at[which * group + number],
                kv_recv.at[which * group + lax.rem(me.index + group - block, group)],
                me.member(block),
            )
            local = pltpu.make_async_copy(
                source, grads.at[which + 1, me.index], own_sem.at[5 + which]
            )

            @pl.when(block != me.index)
            def _():
                if start:
                    remote.start()
                else:
                    remote.wait_send()

            if start:

                @pl.when(block == me.index)
                def _():
                    local.start()

    def await_late(which):
        @pl.when(odd)
        def _():
            pltpu.make_async_copy(
                dkv_ref.at[which, :, pl.ds(0, width)],
                grads.at[which + 1, me.index],
                own_sem.at[5 + which],
            ).wait()
            for ahead_by in range(1, group):
                source, device = me.peer(ahead_by)
                wire(
                    dkv_ref.at[which, :, pl.ds(0, width)],
                    grads.at[which + 1, source],
                    kv_send.at[0],
                    kv_recv.at[which * group + ahead_by],
                    device,
                ).wait_recv()

        @pl.when(jnp.logical_not(odd))
        def _():
            pltpu.make_async_copy(
                kv_tokens.at[pl.ds(which, 1)],
                grads.at[pl.ds(which + 1, 1)],
                own_sem.at[5 + which],
            ).wait()

    for which in range(2):
        late_sends(which, True)

        @pl.when(jnp.logical_not(odd))
        def _():
            pltpu.make_async_copy(
                kv_tokens.at[pl.ds(which, 1)],
                grads.at[pl.ds(which + 1, 1)],
                own_sem.at[5 + which],
            ).start()

    wires = Wires(send, recv)
    plan = []
    for number in range(6):
        tensor, half = number // 2, number % 2
        plan.append(
            Reduce(
                me,
                wires,
                partial.at[tensor],
                ((0, EDGE), (half * UNIT // 2, UNIT // 2)),
                half == 1,
                None,
                None,
                r0.at[number],
                (r1b if half else r1a).at[tensor],
                r2.at[number],
                r3.at[number],
                (dwq, dwk, dwv)[tensor],
                ((0, EDGE), (half * UNIT // 2, UNIT // 2)),
            )
        )

    def work(tensor):
        taken = grads[tensor].reshape(depth, width)
        for first in range(0, depth, 256):
            term = lax.dot_general(
                xt[first : first + 256, :], taken, BY_LAST, preferred_element_type=jnp.float32
            ).astype(jnp.bfloat16)
            for share in range(first // EDGE, (first + 256) // EDGE):
                at = (share // (blks * 4), share // 4 % blks, share // 2 % 2, share % 2)
                partial[(tensor,) + at] = term[share * EDGE - first : (share + 1) * EDGE - first]
        for unit in plan[2 * tensor : 2 * tensor + 2]:
            unit.stage(0)

    def work_input(tensor):
        taken = grads[tensor].reshape(depth, width)
        for first in range(0, depth, 256):
            term = jnp.dot(
                weights[first : first + 256, tensor * depth : (tensor + 1) * depth],
                taken,
                preferred_element_type=jnp.float32,
            )
            if tensor == 0:
                turned_dx[first : first + 256, :] = term
            elif tensor == 1:
                turned_dx[first : first + 256, :] += term
            else:
                total = turned_dx[first : first + 256, :] + term
                dx_out[:, first : first + 256] = base[:, first : first + 256] + total.T

    def stages(tensor, *which):
        for stage in which:
            for unit in plan[2 * tensor : 2 * tensor + 2]:
                unit.stage(stage)

    def note_bias(tensor, row):
        ones = jnp.ones((8, width), jnp.bfloat16)
        found = lax.dot_general(
            ones, grads[tensor].reshape(depth, width), BY_LAST, preferred_element_type=jnp.float32
        )
        per = 128 * devices // depth
        for owner in range(devices):
            first = owner // per * 128
            bias[owner, row : row + 1, :] = found[:1, first : first + 128]

    loads[0].wait()
    xt[...] = x[...].astype(jnp.float32).T.astype(jnp.bfloat16)
    loads[1].wait()
    work(0)
    stages(0, 2)
    loads[4].wait()
    note_bias(0, 3)
    loads[2].wait()
    work_input(0)
    stages(0, 3)
    await_late(0)
    work(1)
    stages(1, 2)
    stages(0, 4)
    work_input(1)
    stages(1, 3)
    await_late(1)
    work(2)
    note_bias(2, 4)
    small = []
    for slot, device in enumerate(others):
        peer = (device["seq"] * blks + device["blk"]) * 4 + device["head"]
        copy = wire(
            bias.at[peer], landed.at[slot], sums_send.at[slot], sums_recv.at[slot], device
        )
        small.append(copy)
    stages(2, 2)
    for copy in small:
        copy.start()
    stages(1, 4)
    loads[3].wait()
    work_input(2)
    stages(2, 3)
    stages(0, 5)
    stages(2, 4)
    for copy in small:
        copy.wait()
    sums_out[...] = jnp.sum(landed[...], axis=0) + bias[index]
    stages(1, 5)
    stages(2, 5)
    for which in range(2):
        late_sends(which, False)


def last_reduce(dkv, kv_tokens, dq, x, w_qkv, base, sums, collective_id):
    seqs, blks, heads = (lax.axis_size(name) for name in EVERY)
    devices = seqs * blks * heads
    group = blks * heads
    width, depth = x.shape
    half = UNIT // 2
    return pl.pallas_call(
        functools.partial(last_kernel, blks, devices),
        out_shape=[
            *[jax.ShapeDtypeStruct((EDGE, depth), jnp.float32)] * 3,
            jax.ShapeDtypeStruct((width, depth), jnp.float32),
            jax.ShapeDtypeStruct(sums.shape[1:], jnp.float32),
        ],
        in_specs=[pl.BlockSpec(memory_space=pl.ANY)] * 7,
        out_specs=[pl.BlockSpec(memory_space=pltpu.VMEM)] * 5,
        scratch_shapes=[
            pltpu.VMEM((3, group, HEAD_DIM, width), jnp.bfloat16),
            pltpu.VMEM((width, depth), jnp.bfloat16),
            pltpu.VMEM((depth, width), jnp.bfloat16),
            pltpu.VMEM((depth, 3 * depth), jnp.bfloat16),
            pltpu.VMEM((width, depth), jnp.float32),
            pltpu.VMEM((depth, width), jnp.float32),
            pltpu.VMEM((3, seqs, blks, heads // 2, 2, EDGE, UNIT), jnp.bfloat16),
            pltpu.VMEM(sums.shape, jnp.float32),
            pltpu.VMEM((devices - 1,) + sums.shape[1:], jnp.float32),
            *reduce_scratch(6, blks, half),
            pltpu.SemaphoreType.DMA((7,)),
            pltpu.SemaphoreType.DMA((2 * group,)),
            pltpu.SemaphoreType.DMA((2 * group,)),
            pltpu.SemaphoreType.DMA((devices,)),
            pltpu.SemaphoreType.DMA((devices,)),
        ],
        compiler_params=pltpu.CompilerParams(
            collective_id=collective_id, has_side_effects=True, vmem_limit_bytes=56 * 2**20
        ),
        name="last_reduce",
    )(dkv, kv_tokens, dq, x, w_qkv, base, sums)


BESIDE = ()


AFTER = ()


def shards_heads(
    layer_input,
    weight_query,
    weight_key,
    weight_value,
    weight_output,
    weight_expand,
    weight_reduce,
    bias_query,
    bias_value,
    bias_output,
    bias_expand,
    bias_reduce,
    first_gain,
    first_shift,
    second_gain,
    second_shift,
    cotangent,
    doc_lengths,
):
    tok_rows, model_width = layer_input.shape[1:]
    head_count = lax.axis_size("head")
    blk_count = lax.axis_size("blk")
    count = head_count * blk_count
    seq_len = tok_rows * count
    long_rows = seq_len - seq_len // blk_count // 2
    flat_rows = layer_input.reshape(tok_rows, model_width)

    vectors = (
        bias_query,
        bias_value,
        bias_output,
        bias_reduce,
        first_gain,
        first_shift,
        second_gain,
        second_shift,
        bias_expand,
    )
    sizes = [vector.shape[0] for vector in vectors]
    lane = 128
    rows = [vector.reshape(1, -1) for vector in vectors[:-1]] + [bias_expand.reshape(-1, sizes[0])]
    vec, at = jnp.zeros((16, lane), layer_input.dtype), 0
    for row in rows:
        count_here = row.shape[0]
        vec = vec + jnp.pad(row, ((at, 16 - at - count_here), (0, lane - sizes[0])))
        at = at + count_here
    rest = (weight_output, weight_expand, weight_reduce)
    beside = {which: lax.all_gather(rest[which], EVERY, axis=0, tiled=True) for which in BESIDE}
    (
        probs, tail_probs, attn, inv_total, kept, attn_flat, w_qkv, vec, *wholes,
    ) = attn_fwd(
        flat_rows,
        vec,
        doc_lengths,
        long_rows,
        (weight_query, weight_key, weight_value),
        tuple(share for which, share in enumerate(rest) if which not in BESIDE),
        5,
    )
    attn_flat = attn_flat.reshape(model_width, tok_rows)
    w_qkv = w_qkv.reshape(model_width, 3 * model_width)
    vec = vec.reshape(-1, sizes[0], lane)[:, :, :16].transpose(2, 0, 1).astype(jnp.float32)
    _, _, b_output, b_reduce, gain_one, shift_one, gain_two, shift_two = [
        vec[number].reshape(-1) for number in range(8)
    ]
    b_expand = vec[8:at].transpose(1, 0, 2).reshape(-1)
    w_output, w_expand, w_reduce = [
        beside[which] if which in BESIDE else wholes.pop(0).reshape(-1, share.shape[1])
        for which, share in enumerate(rest)
    ]

    resid_one = flat_rows.astype(jnp.float32) + left_dot(attn_flat, w_output) + b_output
    normed_one, norm_one_pull = jax.vjp(layer_norm, resid_one, gain_one, shift_one)
    normed_low = normed_one.astype(jnp.bfloat16)
    pre_act = plain_dot(normed_low, w_expand) + b_expand
    hidden_f32, gelu_pull = jax.vjp(gelu_curve, pre_act)
    hidden = hidden_f32.astype(jnp.bfloat16)
    resid_two = normed_one + plain_dot(hidden, w_reduce) + b_reduce
    result, norm_two_pull = jax.vjp(layer_norm, resid_two, gain_two, shift_two)
    layer_output = result.astype(jnp.bfloat16).reshape(layer_input.shape)
    tok_first = (lax.axis_index("blk") * head_count + lax.axis_index("head")) * tok_rows
    tok_seg = segment_ids(doc_lengths, tok_first + lax.iota(jnp.int32, tok_rows))
    live = (tok_seg > 0).astype(jnp.float32)
    grad_out = (cotangent.astype(jnp.float32) * live[..., None]).reshape(-1, model_width)
    grad_resid_two, grad_gain_two, grad_shift_two = norm_two_pull(grad_out)
    grad_ffn = grad_resid_two.astype(jnp.bfloat16)
    grad_w_reduce = left_dot(hidden, grad_ffn)
    grad_b_reduce = jnp.sum(grad_ffn.astype(jnp.float32), axis=0)
    (grad_pre,) = gelu_pull(right_dot(grad_ffn, w_reduce))
    grad_pre = grad_pre.astype(jnp.bfloat16)
    grad_w_expand = left_dot(normed_low, grad_pre)
    grad_b_expand = jnp.sum(grad_pre.astype(jnp.float32), axis=0)
    grad_normed = grad_resid_two + right_dot(grad_pre, w_expand)
    grad_resid_one, grad_gain_one, grad_shift_one = norm_one_pull(grad_normed)
    grad_branch = grad_resid_one.astype(jnp.bfloat16)
    grad_w_output = plain_dot(attn_flat, grad_branch)
    grad_b_output = jnp.sum(grad_branch.astype(jnp.float32), axis=0)
    grad_attn = right_dot(w_output, grad_branch).astype(jnp.bfloat16)
    grad_attn = grad_attn.reshape(HEADS, HEAD_DIM, tok_rows)

    grads = [grad.astype(jnp.bfloat16) for grad in (grad_w_output, grad_w_expand, grad_w_reduce)]
    beside = {
        which: lax.psum_scatter(grads[which], EVERY, scatter_dimension=0, tiled=True).astype(
            jnp.float32
        )
        for which in AFTER
    }
    grad_kv, grad_query, kv_tokens, *totals = attn_bwd(
        probs,
        tail_probs,
        kept,
        attn,
        inv_total,
        grad_attn,
        long_rows,
        [grad for which, grad in enumerate(grads) if which not in AFTER],
        6,
    )
    grad_w_output, grad_w_expand, grad_w_reduce = [
        beside[which] if which in AFTER else totals.pop(0) for which in range(3)
    ]

    sums = (
        jnp.zeros_like(b_output),
        jnp.zeros_like(b_output),
        grad_b_output,
        grad_b_reduce,
        grad_gain_one,
        grad_shift_one,
        grad_gain_two,
        grad_shift_two,
        grad_b_expand,
    )
    sums = jnp.concatenate([term.reshape(-1, size) for term, size in zip(sums, sizes)], axis=1)
    sums = jnp.pad(sums, ((0, 0), (0, 8 * lane - sums.shape[1]))).reshape(-1, 8, lane)
    grad_w_query, grad_w_key, grad_w_value, grad_input, sums = last_reduce(
        grad_kv, kv_tokens, grad_query, flat_rows, w_qkv, grad_resid_one, sums, 7
    )
    owner = (lax.axis_index("seq") * blk_count + lax.axis_index("blk")) * head_count
    owner = owner + lax.axis_index("head")
    within = lax.rem(owner, lane // sizes[0]) * sizes[0]
    g_query = lax.dynamic_slice_in_dim(sums[3], within, sizes[0])
    g_value = lax.dynamic_slice_in_dim(sums[4], within, sizes[1])
    sums = sums.reshape(-1)
    parts, start = [], 0
    for size in sizes:
        parts.append(sums[start : start + size])
        start += size
    g_output, g_reduce, g_gain_one, g_shift_one, g_gain_two, g_shift_two, g_expand = parts[2:]
    return (
        layer_output,
        grad_input.reshape(layer_input.shape),
        grad_w_query,
        grad_w_key,
        grad_w_value,
        grad_w_output,
        grad_w_expand,
        grad_w_reduce,
        g_query,
        g_value,
        g_output,
        g_expand,
        g_reduce,
        g_gain_one,
        g_shift_one,
        g_gain_two,
        g_shift_two,
    )


def solution(mesh):
    placed = (
        P("seq", ("blk", "head"), None),
        P(("seq", "blk", "head"), None),
        P(("seq", "blk", "head"), None),
        P(("seq", "blk", "head"), None),
        P(("seq", "blk", "head"), None),
        P(("seq", "blk", "head"), None),
        P(("seq", "blk", "head"), None),
        P(("seq", "blk", "head")),
        P(("seq", "blk", "head")),
        P(("seq", "blk", "head")),
        P(("seq", "blk", "head")),
        P(("seq", "blk", "head")),
        P(("seq", "blk", "head")),
        P(("seq", "blk", "head")),
        P(("seq", "blk", "head")),
        P(("seq", "blk", "head")),
        P("seq", ("blk", "head"), None),
        P("seq", None),
    )
    group = mesh.shape["blk"] * mesh.shape["head"]
    body = shards_heads if group == HEADS else shards_general
    return jax.shard_map(
        body,
        mesh=mesh,
        in_specs=placed,
        out_specs=(
            P("seq", ("blk", "head"), None),
            P("seq", ("blk", "head"), None),
            P(("seq", "blk", "head"), None),
            P(("seq", "blk", "head"), None),
            P(("seq", "blk", "head"), None),
            P(("seq", "blk", "head"), None),
            P(("seq", "blk", "head"), None),
            P(("seq", "blk", "head"), None),
            P(("seq", "blk", "head")),
            P(("seq", "blk", "head")),
            P(("seq", "blk", "head")),
            P(("seq", "blk", "head")),
            P(("seq", "blk", "head")),
            P(("seq", "blk", "head")),
            P(("seq", "blk", "head")),
            P(("seq", "blk", "head")),
            P(("seq", "blk", "head")),
        ),
        check_vma=False,
    )
```
